32 devices in a mesh: section: 2 (over core), dp: 16 (over z, y, x).
Axes of the slice: x: 2, y: 2, z: 4, core: 2. Of those that a mesh axis runs over, the one named last changes fastest.
Arguments:
- stream_in: bfloat16 [8192, 767], P('dp'), may hold values from -6 to 6
- cotangent: bfloat16 [8192, 767], P('dp'), may hold values from -6 to 6
- qkv_weight: bfloat16 [2, 768, 2304], P('section'), may hold values from -0.21875 to 0.21875
- out_weight: bfloat16 [2, 768, 767], P('section'), may hold values from -1.75 to 1.75
- up_weight: bfloat16 [2, 768, 3072], P('section'), may hold values from -0.21875 to 0.21875
- down_weight: bfloat16 [2, 3072, 767], P('section'), may hold values from -0.109375 to 0.109375
- attn_gain: float32 [2, 768], P('section'), may hold values from 0.1 to 1.9
- mlp_gain: float32 [2, 768], P('section'), may hold values from 0.1 to 1.9
- seq_lengths: int32 [80], replicated, may hold values from 64 to 256, as said below
- seq_slot: int32 [80], replicated, may hold values from 0 to 31, as said below
Outputs:
- stream_out: bfloat16 [2, 8192, 767], P('section', 'dp')
- stream_grad: bfloat16 [2, 8192, 767], P('section', 'dp')
- qkv_grad: float32 [2, 768, 2304], P('section', 'dp')
- out_grad: float32 [2, 768, 767], P('section', 'dp')
- up_grad: float32 [2, 768, 3072], P('section', 'dp')
- down_grad: float32 [2, 3072, 767], P('section', 'dp')
- attn_gain_grad: float32 [2, 768], P('section', 'dp')
- mlp_gain_grad: float32 [2, 768], P('section', 'dp')
- seq_stats: float32 [2, 80, 2], P('section', 'dp')
The draws below stay inside these ranges and needn't reach their ends.
Inputs may be any that keep to these rules, and one draw needn't show every extreme that they name: `seq_slot`: slot k is micro-batch k % 2 of data index k // 2; the sequences of a slot, in increasing index order, fill its 256 tokens end to end. Half of the slots hold one sequence of 256 tokens, the others four of 64. `seq_lengths`: each length is 256 or 64, consistent with seq_slot.
All inputs are finite; a program needn't handle non-finite values.
Results may differ from the reference program's by a relative error of at most 0.019.
Values may be sent and summed in bfloat16 or wider, within the bound.
No kernel may reach another device: no remote copies, remote signals or barrier semaphores. Data moves between devices by JAX's collectives and lax.ppermute only.
A program may use at most 192 MiB of HBM per device.

```python
import jax
import jax.numpy as jnp
from jax import lax

D = 768
H = 12
HD = 64
FF = 3072
MB_TOK = 256
MICRO = 2
TOKENS = 8192
SEQS = 80
N_DP = 16


def sequence_table(key):
    halfway = SEQS // 5
    ordering = jax.random.permutation(jax.random.fold_in(key, 11), 2 * halfway).astype(jnp.int32)
    slot_list = jnp.concatenate([ordering[:halfway], jnp.repeat(ordering[halfway:], 4)])
    lengths = jnp.concatenate([jnp.full((halfway,), MB_TOK, jnp.int32), jnp.full((4 * halfway,), MB_TOK // 4, jnp.int32)])
    shuffle = jax.random.permutation(jax.random.fold_in(key, 12), 5 * halfway)
    return (lengths[shuffle], slot_list[shuffle])


def draw_seq_lengths(key, part):
    return sequence_table(key)[0]


def draw_seq_slot(key, part):
    return sequence_table(key)[1]


def level_of(own_key, shape, cuts, smallest, top_value):
    def one(position, shards_of):
        steps = jax.random.uniform(jax.random.fold_in(jax.random.fold_in(own_key, 6), position), (shards_of,), jnp.float32, smallest / len(cuts), top_value / len(cuts))
        return jnp.repeat(jnp.exp(steps), shape[position] // shards_of).reshape((-1,) + (1,) * (len(shape) - position - 1))

    level = one(*cuts[0])
    for cut in cuts[1:]:
        level = level * one(*cut)
    return level


def bell_draw(rng, shape, width, limit, split=(), kind=jnp.bfloat16):
    level = level_of(rng, shape, split, -0.22, 0.18) if split else 1.0
    drawn = jax.random.normal(rng, shape, jnp.float32) * width * level
    return jnp.minimum(jnp.maximum(drawn, -limit), limit).astype(kind)


def setup_inputs(seed: int = 0) -> dict:
    key_of = jax.random.split(jax.random.key(seed), 11)
    stream_in = bell_draw(key_of[0], (TOKENS, D - 1), 1.0, 6.0, ((0, 16),))
    cotangent = bell_draw(key_of[1], (TOKENS, D - 1), 1.0, 6.0, ((0, 16),))
    qkv_weight = bell_draw(key_of[2], (2, D, 3 * D), D ** -0.5, 0.21875, ((0, 2),))
    out_weight = bell_draw(key_of[3], (2, D, D - 1), (D // 64) ** -0.5, 1.75, ((0, 2),))
    up_weight = bell_draw(key_of[4], (2, D, FF), D ** -0.5, 0.21875, ((0, 2),))
    down_weight = bell_draw(key_of[5], (2, FF, D - 1), FF ** -0.5, 0.109375, ((0, 2),))
    attn_gain = jnp.clip(1.0 + 0.18 * jax.random.normal(key_of[6], (2, D), jnp.float32), 0.1, 1.9)
    mlp_gain = jnp.clip(1.0 + 0.18 * jax.random.normal(key_of[7], (2, D), jnp.float32), 0.1, 1.9)
    seq_lengths = draw_seq_lengths(jax.random.fold_in(key_of[10], 71), 0)
    seq_slot = draw_seq_slot(jax.random.fold_in(key_of[10], 71), 0)
    return {"stream_in": stream_in, "cotangent": cotangent, "qkv_weight": qkv_weight, "out_weight": out_weight, "up_weight": up_weight, "down_weight": down_weight, "attn_gain": attn_gain, "mlp_gain": mlp_gain, "seq_lengths": seq_lengths, "seq_slot": seq_slot}


@jax.custom_vjp
def low(v):
    return lax.optimization_barrier(v.astype(jnp.bfloat16)).astype(jnp.float32)

@jax.custom_vjp
def low_back(v):
    return v

def low_keep(v):
    return (low(v), None)

def low_pass(kept, grad):
    return (grad,)

def back_keep(v):
    return (v, None)

def back_low(kept, grad):
    return (low(grad),)
low.defvjp(low_keep, low_pass)
low_back.defvjp(back_keep, back_low)
epsilon = 1e-05

def exact_dot(former, latter):
    return jnp.dot(former, latter, precision=lax.Precision.HIGHEST)

def centered_norm(stream, gain):
    row_sum = lax.optimization_barrier(jnp.sum(stream, axis=1, keepdims=True))
    decompressed = jnp.concatenate([stream, -row_sum], axis=1)
    mean_sq = lax.optimization_barrier(jnp.mean(decompressed * decompressed, axis=1, keepdims=True))
    return (decompressed * lax.rsqrt(mean_sq + epsilon) * gain, mean_sq[:, 0])

def reference(stream_in, cotangent, qkv_weight, out_weight, up_weight, down_weight, attn_gain, mlp_gain, seq_lengths, seq_slot):
    slot_count = N_DP * MICRO
    slot_ids = jnp.arange(slot_count, dtype=jnp.int32)
    member = seq_slot[None, :] == slot_ids[:, None]
    held_lengths = jnp.where(member, seq_lengths[None, :], 0).astype(jnp.int32)
    starts = (jnp.cumsum(held_lengths, axis=1) - held_lengths).astype(jnp.int32)
    positions = jnp.arange(MB_TOK, dtype=jnp.int32)

    def slot_begins(pieces):
        member_row, start_row = pieces
        inside = member_row[None, :] & (start_row[None, :] <= positions[:, None])
        return lax.optimization_barrier(jnp.max(jnp.where(inside, start_row[None, :], 0), axis=1)).astype(jnp.int32)
    begins = lax.map(slot_begins, (member, starts))

    def attend(pieces):
        packed, begin_row = pieces
        queries = packed[:, 0]
        key_part = packed[:, 1]
        values = packed[:, 2]
        scores = jnp.einsum('qhd,khd->hqk', queries, key_part, precision=lax.Precision.HIGHEST) * HD ** (-0.5)
        scores = low_back(scores)
        allowed = (positions[None, :] <= positions[:, None]) & (positions[None, :] >= begin_row[:, None])
        scores = jnp.where(allowed[None], scores, -1e+30)
        attention = jax.nn.softmax(scores, axis=-1)
        mixed = jnp.einsum('hqk,khd->qhd', low(attention), values, precision=lax.Precision.HIGHEST)
        return mixed.reshape(MB_TOK, H * HD)

    def tally_slot(pieces):
        member_row, start_row, begin_row, squares = pieces
        owner = (member_row[None, :] & (start_row[None, :] == begin_row[:, None])).astype(jnp.float32)
        return jnp.dot(owner.T, squares, precision=lax.Precision.HIGHEST)

    def per_sequence(squares):
        seq_sums = lax.optimization_barrier(jnp.sum(lax.map(tally_slot, (member, starts, begins, squares.reshape(slot_count, MB_TOK, 2))), axis=0))
        return seq_sums / seq_lengths[:, None].astype(jnp.float32)

    def block_layer(stream, qkv_w, out_w, up_w, down_w, gain_attn, gain_mlp):
        normed, attn_square = centered_norm(stream, gain_attn)
        packed = low(low_back(exact_dot(low(normed), qkv_w)))
        blocks = packed.reshape(slot_count, MB_TOK, 3, H, HD)
        heads = lax.map(jax.checkpoint(attend), (blocks, begins))
        heads = low(low_back(heads.reshape(slot_count * MB_TOK, H * HD)))
        middle = stream + low_back(exact_dot(heads, out_w))
        normed_mlp, mlp_square = centered_norm(middle, gain_mlp)
        hidden = low_back(exact_dot(low(normed_mlp), up_w))
        active = low(jax.nn.gelu(hidden, approximate=True))
        result = middle + low_back(exact_dot(active, down_w))
        return (result, jnp.stack([attn_square, mlp_square], axis=1))

    def forward(stream, offset, qkv_w, out_w, up_w, down_w, gain_attn, gain_mlp):
        first_out, first_sq = block_layer(stream, qkv_w[0], out_w[0], up_w[0], down_w[0], gain_attn[0], gain_mlp[0])
        second_in = low(low_back(first_out)) + offset
        second_out, second_sq = block_layer(second_in, qkv_w[1], out_w[1], up_w[1], down_w[1], gain_attn[1], gain_mlp[1])
        statistics = jnp.stack([per_sequence(first_sq), per_sequence(second_sq)])
        return (second_out, (first_out, statistics))
    primal = (stream_in.astype(jnp.float32), jnp.zeros((TOKENS, D - 1), jnp.float32), qkv_weight.astype(jnp.float32), out_weight.astype(jnp.float32), up_weight.astype(jnp.float32), down_weight.astype(jnp.float32), attn_gain.astype(jnp.float32), mlp_gain.astype(jnp.float32))
    second_out, pullback, extras = jax.vjp(forward, *primal, has_aux=True)
    first_out, seq_stats = extras
    gradients = pullback(cotangent.astype(jnp.float32))
    stream_out = jnp.stack([first_out, second_out]).astype(jnp.bfloat16)
    stream_grad = jnp.stack([gradients[0], gradients[1]]).astype(jnp.bfloat16)
    return (stream_out, stream_grad, gradients[2], gradients[3], gradients[4], gradients[5], gradients[6], gradients[7], seq_stats)
```

```python
from functools import partial

import jax
import jax.numpy as jnp
from jax import lax
from jax.sharding import PartitionSpec as P

HD = 64
MICRO = 2


epsilon = 1e-05


def shifted(block, axis, distance):
    devices = range(lax.axis_size(axis))
    route = [(i - distance, i) for i in devices if i - distance in devices]
    return lax.ppermute(block, axis, route)


def exchanged(block, stride, extent):
    size = lax.axis_size("dp")
    place = lambda i: i // stride % extent
    route = [(i, i + (1 - 2 * place(i)) * stride) for i in range(size)]
    return lax.ppermute(block.astype(jnp.bfloat16), "dp", route).astype(jnp.float32)


def along_pair(blocks, stride, dim):
    place = lax.axis_index("dp") // stride % 2
    away = lax.dynamic_index_in_dim(blocks, 1 - place, dim, keepdims=True)
    own = lax.dynamic_index_in_dim(blocks, place, dim, keepdims=True)
    return own + exchanged(away, stride, 2)


def along_line(blocks, stride, dim):
    size = lax.axis_size("dp")
    extent = size // stride
    place = lax.axis_index("dp") // stride
    own = lambda s: lax.dynamic_index_in_dim(blocks, jnp.clip(s, 0, extent - 1), dim, keepdims=True)
    total = own(place)
    for step in (1, -1):
        carry = None
        for turn in range(1, extent):
            out = own(place + step * (extent - turn))
            if carry is not None:
                out = out + carry
            live = [i for i in range(size) if 0 <= i // stride + step * (extent - turn) < extent]
            route = [(i, i + step * stride) for i in live]
            carry = lax.ppermute(out.astype(jnp.bfloat16), "dp", route).astype(jnp.float32)
        total = total + carry
    return total


def scattered(grads, order):
    size = lax.axis_size("dp")
    blocks = grads.reshape(size // 4, 2, 2, grads.shape[0] // size, grads.shape[1])
    for axis in order:
        if axis == "z":
            blocks = along_line(blocks, 4, 0)
        else:
            blocks = along_pair(blocks, *((1, 2) if axis == "x" else (2, 1)))
    return blocks[0, 0, 0]


def rows_product(former, latter):
    return lax.dot_general(
        former, latter, (((0,), (0,)), ((), ())), preferred_element_type=jnp.float32
    )


def against_transposed(former, latter):
    return lax.dot_general(
        former, latter, (((1,), (1,)), ((), ())), preferred_element_type=jnp.float32
    )


def centered_norm(stream):
    row_sum = jnp.sum(stream, axis=1, keepdims=True)
    decompressed = jnp.concatenate([stream, -row_sum], axis=1)
    mean_sq = jnp.mean(decompressed * decompressed, axis=1, keepdims=True)
    factor = lax.rsqrt(mean_sq + epsilon)
    return (decompressed * factor, factor, mean_sq[:, 0])


def centered_norm_back(d_lifted, normed, factor, gain):
    d_normed = d_lifted * gain
    d_gain = jnp.sum(d_lifted * normed, axis=0)
    d_whole = factor * (d_normed - normed * jnp.mean(d_normed * normed, axis=1, keepdims=True))
    return (d_whole[:, :-1] - d_whole[:, -1:], d_gain)


def allowed_keys(begins):
    row_count = begins.shape[0]
    columns = jnp.arange(row_count, dtype=jnp.int32)
    return (columns[None, :] <= columns[:, None]) & (columns[None, :] >= begins[:, None])


def split_heads(packed):
    pieces = packed.reshape(packed.shape[0], 3, -1, HD)
    return (pieces[:, 0], pieces[:, 1], pieces[:, 2])


def masked_scores(queries, key_part, allowed):
    scores = jnp.einsum(
        "qhd,khd->hqk", queries, key_part, preferred_element_type=jnp.float32
    ) * HD ** (-0.5)
    return jnp.where(allowed[None], scores, -1e30)


def attention_forward(packed, begins):
    queries, key_part, values = split_heads(packed)
    scores = masked_scores(queries, key_part, allowed_keys(begins))
    row_peak = jnp.max(scores, axis=2, keepdims=True)
    exponent = jnp.exp(scores - row_peak)
    row_total = jnp.sum(exponent, axis=2, keepdims=True)
    attention = (exponent / row_total).astype(jnp.bfloat16)
    mixed = jnp.einsum("hqk,khd->qhd", attention, values, preferred_element_type=jnp.float32)
    return (mixed.reshape(packed.shape[0], -1).astype(jnp.bfloat16), row_peak + jnp.log(row_total))


def attention_backward(packed, log_total, d_mixed, begins):
    queries, key_part, values = split_heads(packed)
    attention = jnp.exp(masked_scores(queries, key_part, allowed_keys(begins)) - log_total)
    d_heads = d_mixed.reshape(d_mixed.shape[0], -1, HD)
    d_attention = jnp.einsum("qhd,khd->hqk", d_heads, values, preferred_element_type=jnp.float32)
    d_values = jnp.einsum(
        "hqk,qhd->khd", attention.astype(jnp.bfloat16), d_heads, preferred_element_type=jnp.float32
    )
    d_scores = attention * (d_attention - jnp.sum(attention * d_attention, axis=2, keepdims=True))
    d_scores = d_scores.astype(jnp.bfloat16)
    d_queries = jnp.einsum(
        "hqk,khd->qhd", d_scores, key_part, preferred_element_type=jnp.float32
    ) * HD ** (-0.5)
    d_keys = jnp.einsum(
        "hqk,qhd->khd", d_scores, queries, preferred_element_type=jnp.float32
    ) * HD ** (-0.5)
    stacked = jnp.stack([d_queries, d_keys, d_values], axis=1)
    return stacked.reshape(d_mixed.shape[0], -1).astype(jnp.bfloat16)


def layer_forward(stream, begins, weights):
    qkv_w, out_w, up_w, down_w, gain_attn, gain_mlp = weights
    base = stream.astype(jnp.float32)
    normed, factor, attn_square = centered_norm(base)
    lifted = (normed * gain_attn).astype(jnp.bfloat16)
    packed = jnp.dot(lifted, qkv_w, preferred_element_type=jnp.float32).astype(jnp.bfloat16)
    mixed_heads, log_total = attention_forward(packed, begins)
    middle = base + jnp.dot(mixed_heads, out_w, preferred_element_type=jnp.float32)
    normed_mlp, factor_mlp, mlp_square = centered_norm(middle)
    lifted_mlp = (normed_mlp * gain_mlp).astype(jnp.bfloat16)
    hidden = jnp.dot(lifted_mlp, up_w, preferred_element_type=jnp.float32)
    active = jax.nn.gelu(hidden, approximate=True).astype(jnp.bfloat16)
    result = middle + jnp.dot(active, down_w, preferred_element_type=jnp.float32)
    stored = (
        normed,
        factor,
        lifted,
        packed,
        mixed_heads,
        log_total,
        normed_mlp,
        factor_mlp,
        lifted_mlp,
        hidden,
        active,
    )
    return (result, stored, jnp.stack([attn_square, mlp_square], axis=1))


def layer_backward(stored, incoming, begins, weights):
    qkv_w, out_w, up_w, down_w, gain_attn, gain_mlp = weights
    (
        normed,
        factor,
        lifted,
        packed,
        mixed_heads,
        log_total,
        normed_mlp,
        factor_mlp,
        lifted_mlp,
        hidden,
        active,
    ) = stored
    down_part = rows_product(active, incoming)
    d_active = against_transposed(incoming, down_w)
    gelu_value, pullback = jax.vjp(partial(jax.nn.gelu, approximate=True), hidden)
    d_hidden = pullback(d_active)[0].astype(jnp.bfloat16)
    up_part = rows_product(lifted_mlp, d_hidden)
    d_lifted_mlp = against_transposed(d_hidden, up_w)
    d_middle_norm, mlp_gain_part = centered_norm_back(
        d_lifted_mlp, normed_mlp, factor_mlp, gain_mlp
    )
    d_middle = incoming.astype(jnp.float32) + d_middle_norm
    d_branch = d_middle.astype(jnp.bfloat16)
    out_part = rows_product(mixed_heads, d_branch)
    d_heads = against_transposed(d_branch, out_w).astype(jnp.bfloat16)
    d_packed = attention_backward(packed, log_total, d_heads, begins)
    qkv_part = rows_product(lifted, d_packed)
    d_lifted = against_transposed(d_packed, qkv_w)
    d_base_norm, attn_gain_part = centered_norm_back(d_lifted, normed, factor, gain_attn)
    return (
        d_middle + d_base_norm,
        (qkv_part, out_part, up_part, down_part, attn_gain_part, mlp_gain_part),
    )


def shards(
    stream_in,
    cotangent,
    qkv_weight,
    out_weight,
    up_weight,
    down_weight,
    attn_gain,
    mlp_gain,
    seq_lengths,
    seq_slot,
):
    first_section = lax.axis_index("section") == 0
    data_index = lax.axis_index("dp")
    micro_count = MICRO
    row_count = stream_in.shape[0] // micro_count
    compressed = stream_in.shape[1]
    weights = (
        qkv_weight[0],
        out_weight[0],
        up_weight[0],
        down_weight[0],
        attn_gain[0],
        mlp_gain[0],
    )
    inputs = stream_in.reshape(micro_count, row_count, compressed)
    targets = cotangent.reshape(micro_count, row_count, compressed)
    slot_ids = data_index * micro_count + jnp.arange(micro_count, dtype=jnp.int32)
    member = seq_slot[None, :] == slot_ids[:, None]
    held_lengths = jnp.where(member, seq_lengths[None, :], 0)
    order = jnp.arange(seq_lengths.shape[0], dtype=jnp.int32)
    earlier = order[:, None] < order[None, :]
    starts = jnp.sum(jnp.where(earlier[None], held_lengths[:, :, None], 0), axis=1)
    positions = jnp.arange(row_count, dtype=jnp.int32)
    inside = member[:, None, :] & (starts[:, None, :] <= positions[None, :, None])
    begin_table = jnp.max(jnp.where(inside, starts[:, None, :], 0), axis=2)
    owner_table = (member[:, None, :] & (starts[:, None, :] == begin_table[:, :, None])).astype(
        jnp.float32
    )
    received = jnp.zeros((row_count, compressed), jnp.bfloat16)
    kept = []
    results = []
    seq_terms = jnp.zeros((seq_lengths.shape[0], 2), jnp.float32)
    for moment in range(micro_count + 1):
        leading = min(moment, micro_count - 1)
        trailing = max(moment - 1, 0)
        table_index = jnp.where(first_section, leading, trailing)
        begins = begin_table[table_index]
        entering = jnp.where(first_section, inputs[leading], received)
        result, stored, squares = layer_forward(entering, begins, weights)
        leaving = result.astype(jnp.bfloat16)
        usable = jnp.where(first_section, moment < micro_count, moment >= 1)
        tallies = jnp.dot(owner_table[table_index].T, squares, precision=lax.Precision.HIGHEST)
        seq_terms = seq_terms + jnp.where(usable, tallies, 0.0)
        kept.append(stored)
        results.append(leaving)
        if moment < micro_count:
            received = shifted(leaving, "section", 1)
    seq_terms = seq_terms / seq_lengths[:, None].astype(jnp.float32)
    received_grad = jnp.zeros((row_count, compressed), jnp.bfloat16)
    totals = None
    leaving_grads = []
    for moment in range(micro_count + 1):
        source = micro_count - moment
        earliest = max(micro_count - 1 - moment, 0)
        table_index = jnp.where(first_section, min(source, micro_count - 1), earliest)
        begins = begin_table[table_index]
        incoming = jnp.where(first_section, received_grad, targets[earliest])
        d_input, parts = layer_backward(kept[source], incoming, begins, weights)
        usable = jnp.where(first_section, moment >= 1, moment < micro_count)
        parts = tuple((jnp.where(usable, member_part, 0.0) for member_part in parts))
        leaving = d_input.astype(jnp.bfloat16)
        leaving_grads.append(leaving)
        totals = parts if totals is None else jax.tree.map(jnp.add, totals, parts)
        if moment < micro_count:
            received_grad = shifted(leaving, "section", -1)
    totals = (
        scattered(totals[0], "xyz"),
        scattered(totals[1], "yxz"),
        scattered(totals[2], "yzx"),
        scattered(totals[3], "xzy"),
        lax.psum_scatter(totals[4], "dp", scatter_dimension=0, tiled=True),
        lax.psum_scatter(totals[5], "dp", scatter_dimension=0, tiled=True),
        lax.psum_scatter(seq_terms, "dp", scatter_dimension=0, tiled=True),
    )
    stream_out = jnp.concatenate(
        [
            jnp.where(first_section, results[number], results[number + 1])
            for number in range(micro_count)
        ],
        axis=0,
    )
    stream_grad = jnp.concatenate(
        [
            jnp.where(
                first_section,
                leaving_grads[micro_count - number],
                leaving_grads[micro_count - 1 - number],
            )
            for number in range(micro_count)
        ],
        axis=0,
    )
    return (
        stream_out[None],
        stream_grad[None],
        totals[0][None],
        totals[1][None],
        totals[2][None],
        totals[3][None],
        totals[4][None],
        totals[5][None],
        totals[6][None],
    )


def solution(mesh):
    placed = (
        P("dp", None),
        P("dp", None),
        P("section", None, None),
        P("section", None, None),
        P("section", None, None),
        P("section", None, None),
        P("section", None),
        P("section", None),
        P(),
        P(),
    )
    return jax.shard_map(
        shards,
        mesh=mesh,
        in_specs=placed,
        out_specs=(
            P("section", "dp", None),
            P("section", "dp", None),
            P("section", "dp", None),
            P("section", "dp", None),
            P("section", "dp", None),
            P("section", "dp", None),
            P("section", "dp"),
            P("section", "dp"),
            P("section", "dp", None),
        ),
        check_vma=False,
    )
```

```python
import functools

import jax
import jax.numpy as jnp
from jax import lax
from jax.experimental import pallas as pl
from jax.experimental.pallas import tpu as pltpu
from jax.sharding import PartitionSpec as P

HD = 64
MICRO = 2
PAIR = 2 * HD
SCALE = HD ** (-0.5)
LSE_ROWS = 16
GELU_A = 0.7978845608028654
GELU_B = 0.044715
CORE_CHIPS = 16

epsilon = 1e-05

VMEM = pl.BlockSpec(memory_space=pltpu.VMEM)
SMEM = pl.BlockSpec(memory_space=pltpu.SMEM)
ANY = pl.BlockSpec(memory_space=pl.ANY)
MIB = 2**20


def shaped(shape, dtype):
    return jax.ShapeDtypeStruct(shape, dtype)


def shifted(block, axis, distance):
    devices = range(lax.axis_size(axis))
    route = [(i - distance, i) for i in devices if i - distance in devices]
    return lax.ppermute(block, axis, route)


def product(former, latter):
    return jnp.dot(former, latter, preferred_element_type=jnp.float32)


def rows_product(former, latter):
    return lax.dot_general(
        former, latter, (((0,), (0,)), ((), ())), preferred_element_type=jnp.float32
    )


def against_transposed(former, latter):
    return lax.dot_general(
        former, latter, (((1,), (1,)), ((), ())), preferred_element_type=jnp.float32
    )


def centered_norm(stream):
    row_sum = jnp.sum(stream, axis=1, keepdims=True)
    decompressed = jnp.concatenate([stream, -row_sum], axis=1)
    mean_sq = jnp.mean(decompressed * decompressed, axis=1, keepdims=True)
    factor = lax.rsqrt(mean_sq + epsilon)
    return (decompressed * factor, factor, mean_sq)


def centered_norm_back(d_lifted, normed, factor, gain):
    d_normed = d_lifted * gain
    d_gain = jnp.sum(d_lifted * normed, axis=0, keepdims=True)
    d_whole = factor * (d_normed - normed * jnp.mean(d_normed * normed, axis=1, keepdims=True))
    last = d_whole.shape[1] - 1
    return (d_whole[:, :last] - d_whole[:, last:], d_gain)


def row_block(ref, slot, count):
    return ref.at[pl.ds(pl.multiple_of(slot * count, count), count)]


def column_tiles(whole, width):
    return [slice(j * width, (j + 1) * width) for j in range(whole // width)]


class Copies:
    def __init__(self, sems):
        self.sems = sems
        self.used = 0

    def start(self, source, target):
        copy = pltpu.make_async_copy(source, target, self.sems.at[self.used])
        self.used += 1
        copy.start()
        return copy


def forward_kernel(*refs, first_call):
    info, stream_in, received, bias_table, gain_attn, gain_mlp, qkv_h, out_h, up_h, down_h = refs[:10]
    refs = refs[10 if first_call else 21 :]
    leaving = refs[0]
    stacks = refs[1:12]
    qkv_w, out_w, up_w, down_w, bias = refs[12:17]
    entering, result, lifted, packed, mixed, log_total, normed_mlp, lifted_mlp, active, slope, stat = refs[17:28]
    sems = refs[28]
    section, live, slot = info[0], info[1], info[2]
    rows, compressed = entering.shape
    width = compressed + 1

    @pl.when(live == 1)
    def _():
        copies = Copies(sems)

        @pl.when(section == 0)
        def _():
            pltpu.make_async_copy(row_block(stream_in, slot, rows), entering, sems.at[40]).start()

        @pl.when(section != 0)
        def _():
            pltpu.make_async_copy(received, entering, sems.at[40]).start()

        loads_qkv = [copies.start(qkv_h.at[:, t], qkv_w.at[:, t]) for t in column_tiles(3 * width, width)]
        load_bias = copies.start(bias_table.at[slot], bias)
        load_out = copies.start(out_h, out_w)
        tiles = column_tiles(up_h.shape[1], width)
        loads_up = [copies.start(up_h.at[:, t], up_w.at[:, t]) for t in tiles]
        loads_down = [copies.start(down_h.at[t], down_w.at[t]) for t in tiles]
        saves = []

        def save(number, block):
            saves.append(copies.start(block, row_block(stacks[number], slot, block.shape[0])))

        pltpu.make_async_copy(received, entering, sems.at[40]).wait()
        base = entering[...].astype(jnp.float32)
        save(0, entering)
        normed, _, square_attn = centered_norm(base)
        lifted[...] = (normed * gain_attn[...]).astype(jnp.bfloat16)
        save(2, lifted)
        for t, load in zip(column_tiles(3 * width, width), loads_qkv):
            load.wait()
            packed[:, t] = product(lifted[...], qkv_w[:, t]).astype(jnp.bfloat16)
        save(3, packed)
        load_bias.wait()
        lane = lax.broadcasted_iota(jnp.int32, (rows, PAIR), 1)
        zero = jnp.zeros((rows, PAIR), jnp.bfloat16)
        totals = jnp.zeros((rows, PAIR), jnp.float32)
        for pair in range(width // PAIR):
            at = pair * PAIR
            queries = packed[:, at : at + PAIR] * jnp.asarray(SCALE, jnp.bfloat16)
            key_part = packed[:, width + at : width + at + PAIR]
            values = packed[:, 2 * width + at : 2 * width + at + PAIR]
            joined = None
            for half, keep in enumerate((lane < HD, lane >= HD)):
                scores = against_transposed(jnp.where(keep, queries, zero), key_part) + bias[...]
                peak = jnp.max(scores, axis=1, keepdims=True)
                exponent = jnp.exp(scores - peak)
                total = jnp.sum(exponent, axis=1, keepdims=True)
                attention = (exponent / total).astype(jnp.bfloat16)
                part = product(attention, jnp.where(keep, values, zero))
                joined = part if joined is None else joined + part
                totals = jnp.where(lane == 2 * pair + half, peak + jnp.log(total), totals)
            mixed[:, at : at + PAIR] = joined.astype(jnp.bfloat16)
        save(4, mixed)
        log_total[...] = totals.T[: log_total.shape[0]]
        save(5, log_total)
        load_out.wait()
        middle = base + product(mixed[...], out_w[...])
        normed, factor, square_mlp = centered_norm(middle)
        normed_mlp[...] = normed
        save(6, normed_mlp)
        lifted_mlp[...] = (normed * gain_mlp[...]).astype(jnp.bfloat16)
        save(7, lifted_mlp)
        stat[...] = jnp.where(lane == 0, square_attn, jnp.where(lane == 1, square_mlp, factor))
        save(10, stat)
        total = middle
        for t, load_up, load_down in zip(tiles, loads_up, loads_down):
            load_up.wait()
            hidden = product(lifted_mlp[...], up_w[:, t])
            squared = hidden * hidden
            bend = jnp.tanh(hidden * (GELU_A + GELU_A * GELU_B * squared))
            gate = 0.5 + 0.5 * bend
            value = hidden * gate
            slope[:, t] = (gate + value * (1.0 - bend) * (GELU_A + 3 * GELU_A * GELU_B * squared)).astype(jnp.bfloat16)
            active[:, t] = value.astype(jnp.bfloat16)
            load_down.wait()
            total = total + product(active[:, t], down_w[t])
        save(8, active)
        save(9, slope)
        result[...] = total.astype(jnp.bfloat16)
        save(1, result)
        leaving[...] = result[...]
        for copy in saves:
            copy.wait()


def forward_layer(info, stream_in, received, bias, weights, stacks):
    qkv_w, out_w, up_w, down_w, gain_attn, gain_mlp = weights
    rows, compressed = received.shape
    width, inner = up_w.shape
    low, full = jnp.bfloat16, jnp.float32
    blocks = [
        ((rows, compressed), low),
        ((rows, compressed), low),
        ((rows, width), low),
        ((rows, 3 * width), low),
        ((rows, width), low),
        ((LSE_ROWS, rows), full),
        ((rows, width), full),
        ((rows, width), low),
        ((rows, inner), low),
        ((rows, inner), low),
        ((rows, PAIR), full),
    ]
    scratch = [pltpu.VMEM(w.shape, low) for w in (qkv_w, out_w, up_w, down_w)]
    scratch += [pltpu.VMEM((rows, rows), full)]
    scratch += [pltpu.VMEM(shape, kind) for shape, kind in blocks]
    scratch += [pltpu.SemaphoreType.DMA((41,))]
    given = [] if stacks is None else list(stacks)
    outs = pl.pallas_call(
        functools.partial(forward_kernel, first_call=stacks is None),
        out_shape=[shaped((rows, compressed), low)]
        + [shaped((MICRO * shape[0], shape[1]), kind) for shape, kind in blocks],
        in_specs=[SMEM, ANY, ANY, ANY, VMEM, VMEM] + [ANY] * (4 + len(given)),
        out_specs=[VMEM] + [ANY] * len(blocks),
        input_output_aliases={10 + i: 1 + i for i in range(len(given))},
        scratch_shapes=scratch,
        compiler_params=pltpu.CompilerParams(vmem_limit_bytes=40 * MIB),
        cost_estimate=pl.CostEstimate(flops=4 * 10**9, bytes_accessed=22 * 10**6, transcendentals=2 * 10**6),
        name="forward_layer",
    )(info, stream_in, received, bias, gain_attn, gain_mlp, qkv_w, out_w, up_w, down_w, *given)
    return outs[0], outs[1:]


def backward_kernel(*refs, first_call):
    info, cotangent, received, bias_table, gain_attn, gain_mlp, qkv_h, out_h, up_h, down_h = refs[:10]
    stored = refs[10:16]
    refs = refs[16 if first_call else 22 :]
    leaving = refs[0]
    stacks = refs[1:7]
    qkv_w, out_w, up_w, down_w, bias, d_heads = refs[7:13]
    entering, packed, log_total, normed_mlp, stat, slope = refs[13:19]
    incoming, d_input, d_hidden, d_branch, d_packed, gains = refs[19:25]
    sems = refs[25]
    section, live, slot = info[0], info[1], info[2]
    rows, compressed = incoming.shape
    width = compressed + 1

    @pl.when(live == 1)
    def _():
        copies = Copies(sems)

        @pl.when(section == 0)
        def _():
            pltpu.make_async_copy(received, incoming, sems.at[40]).start()

        @pl.when(section != 0)
        def _():
            pltpu.make_async_copy(row_block(cotangent, slot, rows), incoming, sems.at[40]).start()

        def load(number, block):
            return copies.start(row_block(stored[number], slot, block.shape[0]), block)

        tiles = column_tiles(up_h.shape[1], width)
        loads = []
        load_slope = None
        for t in tiles:
            loads.append(copies.start(down_h.at[t], down_w.at[t]))
            if load_slope is None:
                load_slope = load(5, slope)
            loads.append(copies.start(up_h.at[:, t], up_w.at[:, t]))
        load_normed, load_stat = load(3, normed_mlp), load(4, stat)
        load_out = copies.start(out_h, out_w)
        load_packed, load_total = load(1, packed), load(2, log_total)
        load_bias = copies.start(bias_table.at[slot], bias)
        load_entering = load(0, entering)
        loads_qkv = [copies.start(qkv_h.at[:, t], qkv_w.at[:, t]) for t in column_tiles(3 * width, width)]
        saves = []

        def save(number, block):
            saves.append(copies.start(block, row_block(stacks[number], slot, block.shape[0])))

        pltpu.make_async_copy(received, incoming, sems.at[40]).wait()
        save(0, incoming)
        d_lifted = jnp.zeros((rows, width), jnp.float32)
        for number, t in enumerate(tiles):
            loads[2 * number].wait()
            if number == 0:
                load_slope.wait()
            d_active = against_transposed(incoming[...], down_w[t])
            d_hidden[:, t] = (d_active * slope[:, t].astype(jnp.float32)).astype(jnp.bfloat16)
            loads[2 * number + 1].wait()
            d_lifted = d_lifted + against_transposed(d_hidden[:, t], up_w[:, t])
        save(2, d_hidden)
        load_normed.wait()
        load_stat.wait()
        d_norm, mlp_part = centered_norm_back(d_lifted, normed_mlp[...], stat[:, 2:3], gain_mlp[...])
        d_middle = incoming[...].astype(jnp.float32) + d_norm
        d_branch[...] = d_middle.astype(jnp.bfloat16)
        save(3, d_branch)
        load_out.wait()
        d_heads[...] = against_transposed(d_branch[...], out_w[...]).astype(jnp.bfloat16)
        load_packed.wait()
        load_total.wait()
        load_bias.wait()
        lane = lax.broadcasted_iota(jnp.int32, (rows, PAIR), 1)
        zero = jnp.zeros((rows, PAIR), jnp.bfloat16)
        for pair in range(width // PAIR):
            at = pair * PAIR
            queries = packed[:, at : at + PAIR] * jnp.asarray(SCALE, jnp.bfloat16)
            key_part = packed[:, width + at : width + at + PAIR]
            values = packed[:, 2 * width + at : 2 * width + at + PAIR]
            d_part = d_heads[:, at : at + PAIR]
            sums = None
            for half, keep in enumerate((lane < HD, lane >= HD)):
                own_queries = jnp.where(keep, queries, zero)
                own_keys = jnp.where(keep, key_part, zero)
                own_part = jnp.where(keep, d_part, zero)
                head = 2 * pair + half
                attention = jnp.exp(
                    against_transposed(key_part, own_queries) + bias[...] - log_total[head : head + 1, :]
                )
                d_attention = against_transposed(values, own_part)
                d_scores = attention * (d_attention - jnp.sum(attention * d_attention, axis=0, keepdims=True))
                d_scores = d_scores.astype(jnp.bfloat16)
                terms = (
                    rows_product(own_keys, d_scores),
                    product(d_scores, own_queries),
                    product(attention.astype(jnp.bfloat16), own_part),
                )
                sums = terms if sums is None else tuple(a + b for a, b in zip(sums, terms))
            d_packed[:, at : at + PAIR] = (sums[0].T * SCALE).astype(jnp.bfloat16)
            d_packed[:, width + at : width + at + PAIR] = sums[1].astype(jnp.bfloat16)
            d_packed[:, 2 * width + at : 2 * width + at + PAIR] = sums[2].astype(jnp.bfloat16)
        save(4, d_packed)
        d_lifted = jnp.zeros((rows, width), jnp.float32)
        for t, load_qkv in zip(column_tiles(3 * width, width), loads_qkv):
            load_qkv.wait()
            d_lifted = d_lifted + against_transposed(d_packed[:, t], qkv_w[:, t])
        load_entering.wait()
        normed, factor, _ = centered_norm(entering[...].astype(jnp.float32))
        d_norm, attn_part = centered_norm_back(d_lifted, normed, factor, gain_attn[...])
        d_input[...] = (d_middle + d_norm).astype(jnp.bfloat16)
        save(1, d_input)
        leaving[...] = d_input[...]
        number = lax.broadcasted_iota(jnp.int32, gains.shape, 0)
        gains[...] = jnp.where(number == 0, attn_part, jnp.where(number == 1, mlp_part, 0.0))
        save(5, gains)
        for copy in saves:
            copy.wait()


def backward_layer(info, cotangent, received, bias, weights, stored, stacks):
    qkv_w, out_w, up_w, down_w, gain_attn, gain_mlp = weights
    rows, compressed = received.shape
    width, inner = up_w.shape
    low, full = jnp.bfloat16, jnp.float32
    blocks = [
        ((rows, compressed), low),
        ((rows, compressed), low),
        ((rows, inner), low),
        ((rows, compressed), low),
        ((rows, 3 * width), low),
        ((8, width), full),
    ]
    scratch = [pltpu.VMEM(w.shape, low) for w in (qkv_w, out_w, up_w, down_w)]
    scratch += [pltpu.VMEM((rows, rows), full), pltpu.VMEM((rows, width), low)]
    scratch += [pltpu.VMEM((s.shape[0] // MICRO, s.shape[1]), s.dtype) for s in stored]
    scratch += [pltpu.VMEM(shape, kind) for shape, kind in blocks]
    scratch += [pltpu.SemaphoreType.DMA((41,))]
    given = [] if stacks is None else list(stacks)
    outs = pl.pallas_call(
        functools.partial(backward_kernel, first_call=stacks is None),
        out_shape=[shaped((rows, compressed), low)]
        + [shaped((MICRO * shape[0], shape[1]), kind) for shape, kind in blocks],
        in_specs=[SMEM, ANY, ANY, ANY, VMEM, VMEM] + [ANY] * (4 + len(stored) + len(given)),
        out_specs=[VMEM] + [ANY] * len(blocks),
        input_output_aliases={16 + i: 1 + i for i in range(len(given))},
        scratch_shapes=scratch,
        compiler_params=pltpu.CompilerParams(vmem_limit_bytes=40 * MIB),
        cost_estimate=pl.CostEstimate(flops=4 * 10**9, bytes_accessed=25 * 10**6, transcendentals=2 * 10**6),
        name="backward_layer",
    )(info, cotangent, received, bias, gain_attn, gain_mlp, qkv_w, out_w, up_w, down_w, *stored, *given)
    return outs[0], outs[1:]


def divide(side, whole, away, own, dim):
    for target, place in ((away, 1 - side), (own, side)):
        index = (slice(None),) * dim + (pl.ds(place, 1),)
        target[...] = whole[index].astype(target.dtype)


def gradient_by_columns(side, former, latter, away, own, turned, whole, *, dim):
    @pl.when(pl.program_id(0) == 0)
    def _():
        turned[...] = former[...].T

    whole[...] = product(turned[...], latter[...]).reshape(whole.shape)
    divide(side[0], whole, away, own, dim)


def gradient_by_rows(side, former, latter, away, own, whole, *, dim):
    whole[...] = rows_product(former[...], latter[...]).reshape(whole.shape)
    divide(side[0], whole, away, own, dim)


def halved(shape, dim):
    return tuple(1 if i == dim else n for i, n in enumerate(shape))


def weight_gradient(side, former, latter, lead, dim, tile, name):
    tokens, tall = former.shape
    wide = latter.shape[1]
    shape = (lead, 2, 2, tall // (4 * lead), wide)
    if tile:
        block = shape[:4] + (tile,)
        grid = (wide // tile,)
        kernel = gradient_by_columns
        in_specs = [
            pl.BlockSpec((tokens, tall), lambda j, s: (0, 0)),
            pl.BlockSpec((tokens, tile), lambda j, s: (0, j)),
        ]
        out_spec = pl.BlockSpec(halved(block, dim), lambda j, s: (0, 0, 0, 0, j))
        scratch = [pltpu.VMEM((tall, tokens), jnp.bfloat16), pltpu.VMEM(block, jnp.float32)]
    else:
        block = (1,) + shape[1:]
        grid = (lead,)
        kernel = gradient_by_rows
        in_specs = [
            pl.BlockSpec((tokens, tall // lead), lambda j, s: (0, j)),
            pl.BlockSpec((tokens, wide), lambda j, s: (0, 0)),
        ]
        out_spec = pl.BlockSpec(halved(block, dim), lambda j, s: (j, 0, 0, 0, 0))
        scratch = [pltpu.VMEM(block, jnp.float32)]
    return pl.pallas_call(
        functools.partial(kernel, dim=dim),
        grid_spec=pltpu.PrefetchScalarGridSpec(
            num_scalar_prefetch=1,
            grid=grid,
            in_specs=in_specs,
            out_specs=[out_spec, out_spec],
            scratch_shapes=scratch,
        ),
        out_shape=[shaped(halved(shape, dim), jnp.bfloat16), shaped(halved(shape, dim), jnp.float32)],
        compiler_params=pltpu.CompilerParams(vmem_limit_bytes=30 * MIB),
        cost_estimate=pl.CostEstimate(
            flops=2 * tokens * tall * wide,
            bytes_accessed=2 * tokens * (tall + wide) + 3 * tall * wide,
            transcendentals=0,
        ),
        name=name,
    )(side, former, latter)


STRIDES = {"x": 1, "y": 2, "w": 4, "v": 8}


def exchange(block, axis):
    size = lax.axis_size("dp")
    return lax.ppermute(block, "dp", [(i, i ^ STRIDES[axis]) for i in range(size)])


def fold(own, got, axis):
    total = own + got.astype(jnp.float32)
    if axis is None:
        return total
    place = lax.axis_index("dp") // STRIDES[axis] % 2
    dim = "vwyx".index(axis)
    away = lax.dynamic_index_in_dim(total, 1 - place, dim, keepdims=True)
    kept = lax.dynamic_index_in_dim(total, place, dim, keepdims=True)
    return away.astype(jnp.bfloat16), kept


def scattered(parted, order):
    away, own = (part.reshape((2, 2) + part.shape[1:]) for part in parted)
    for axis, following in zip(order, list(order[1:]) + [None]):
        result = fold(own, exchange(away, axis), following)
        if following is None:
            return result.reshape(own.shape[-2:])
        away, own = result


def shards(
    stream_in,
    cotangent,
    qkv_weight,
    out_weight,
    up_weight,
    down_weight,
    attn_gain,
    mlp_gain,
    seq_lengths,
    seq_slot,
):
    section = lax.axis_index("section").astype(jnp.int32)
    data_index = lax.axis_index("dp").astype(jnp.int32)
    chips = lax.axis_size("dp")
    row_count = stream_in.shape[0] // MICRO
    compressed = stream_in.shape[1]
    weights = (qkv_weight[0], out_weight[0], up_weight[0], down_weight[0], attn_gain, mlp_gain)
    slot_ids = data_index * MICRO + jnp.arange(MICRO, dtype=jnp.int32)
    member = seq_slot[None, :] == slot_ids[:, None]
    held_lengths = jnp.where(member, seq_lengths[None, :], 0)
    order = jnp.arange(seq_lengths.shape[0], dtype=jnp.int32)
    earlier = order[:, None] < order[None, :]
    starts = jnp.sum(jnp.where(earlier[None], held_lengths[:, :, None], 0), axis=1)
    positions = jnp.arange(row_count, dtype=jnp.int32)
    inside = member[:, None, :] & (starts[:, None, :] <= positions[None, :, None])
    begin_table = jnp.max(jnp.where(inside, starts[:, None, :], 0), axis=2)
    owner_table = (member[:, None, :] & (starts[:, None, :] == begin_table[:, :, None])).astype(jnp.float32)
    allowed = (positions[None, None, :] <= positions[None, :, None]) & (
        positions[None, None, :] >= begin_table[:, :, None]
    )
    bias = jnp.where(allowed, 0.0, -1e30)
    allowed_turned = (positions[None, :, None] <= positions[None, None, :]) & (
        positions[None, :, None] >= begin_table[:, None, :]
    )
    bias_turned = jnp.where(allowed_turned, 0.0, -1e30)

    received = jnp.zeros((row_count, compressed), jnp.bfloat16)
    stored = None
    for moment in range(MICRO + 1):
        slot = moment - section
        live = ((slot >= 0) & (slot < MICRO)).astype(jnp.int32)
        info = jnp.stack([section, live, jnp.clip(slot, 0, MICRO - 1)])
        leaving, stored = forward_layer(info, stream_in, received, bias, weights, stored)
        if moment < MICRO:
            received = shifted(leaving, "section", 1)
    entering, stream_out, lifted, packed, mixed, log_total, normed_mlp, lifted_mlp, active, slope, stat = stored
    squares = stat[:, :2].reshape(MICRO, row_count, 2)
    seq_terms = jnp.einsum("kpt,kpm->tm", owner_table, squares, precision=lax.Precision.HIGHEST)
    seq_terms = seq_terms / seq_lengths[:, None].astype(jnp.float32)

    kept = (entering, packed, log_total, normed_mlp, stat, slope)
    received = jnp.zeros((row_count, compressed), jnp.bfloat16)
    grads = None
    for moment in range(MICRO + 1):
        slot = MICRO - moment - section
        live = ((slot >= 0) & (slot < MICRO)).astype(jnp.int32)
        info = jnp.stack([section, live, jnp.clip(slot, 0, MICRO - 1)])
        leaving, grads = backward_layer(info, cotangent, received, bias_turned, weights, kept, grads)
        if moment < MICRO:
            received = shifted(leaving, "section", -1)
    incoming, stream_grad, d_hidden, d_branch, d_packed, gains = grads
    gains = jnp.sum(gains.reshape(MICRO, 8, -1)[:, :2], axis=0)

    small = jnp.concatenate(
        [gains[0].reshape(chips, -1), gains[1].reshape(chips, -1), seq_terms.reshape(chips, -1)], axis=1
    )
    small = lax.all_gather(small, "dp", axis=0)
    small = jnp.sum(lax.dynamic_index_in_dim(small, data_index, 1, keepdims=False), axis=0)
    count = gains.shape[1] // chips
    attn_part, mlp_part, seq_part = small[:count], small[count : 2 * count], small[2 * count :].reshape(-1, 2)

    if chips == CORE_CHIPS:
        side_x = (data_index % 2)[None]
        side_y = (data_index // 2 % 2)[None]
        down_part = scattered(weight_gradient(side_x, active, incoming, 4, 2, None, "down_gradient"), "xwvy")
        up_part = scattered(weight_gradient(side_y, lifted_mlp, d_hidden, 4, 1, 512, "up_gradient"), "ywvx")
        out_part = scattered(
            weight_gradient(side_y, mixed, d_branch, 4, 1, compressed, "out_gradient"), "yxwv"
        )
        qkv_part = scattered(weight_gradient(side_x, lifted, d_packed, 4, 2, 768, "qkv_gradient"), "xywv")
    else:
        pairs = ((active, incoming), (lifted_mlp, d_hidden), (mixed, d_branch), (lifted, d_packed))
        down_part, up_part, out_part, qkv_part = (
            lax.psum_scatter(rows_product(a, b), "dp", scatter_dimension=0, tiled=True) for a, b in pairs
        )
    return (
        stream_out[None],
        stream_grad[None],
        qkv_part[None],
        out_part[None],
        up_part[None],
        down_part[None],
        attn_part[None],
        mlp_part[None],
        seq_part[None],
    )


def solution(mesh):
    placed = (
        P("dp", None),
        P("dp", None),
        P("section", None, None),
        P("section", None, None),
        P("section", None, None),
        P("section", None, None),
        P("section", None),
        P("section", None),
        P(),
        P(),
    )
    return jax.shard_map(
        shards,
        mesh=mesh,
        in_specs=placed,
        out_specs=(
            P("section", "dp", None),
            P("section", "dp", None),
            P("section", "dp", None),
            P("section", "dp", None),
            P("section", "dp", None),
            P("section", "dp", None),
            P("section", "dp"),
            P("section", "dp"),
            P("section", "dp", None),
        ),
        check_vma=False,
    )
```

```python
import functools

import jax
import jax.numpy as jnp
from jax import lax
from jax.experimental import pallas as pl
from jax.experimental.pallas import tpu as pltpu
from jax.sharding import PartitionSpec as P

HD = 64
MICRO = 2
PAIR = 2 * HD
SCALE = HD ** (-0.5)
LSE_ROWS = 16
GELU_A = 0.7978845608028654
GELU_B = 0.044715
CORE_CHIPS = 16

epsilon = 1e-05

VMEM = pl.BlockSpec(memory_space=pltpu.VMEM)
SMEM = pl.BlockSpec(memory_space=pltpu.SMEM)
HBM = pl.BlockSpec(memory_space=pltpu.HBM)
MIB = 2**20
KERNEL_VMEM = 12 * MIB


def shaped(shape, dtype):
    return jax.ShapeDtypeStruct(shape, dtype)


def shifted(block, axis, distance):
    devices = range(lax.axis_size(axis))
    route = [(i - distance, i) for i in devices if i - distance in devices]
    return lax.ppermute(block, axis, route)


def product(former, latter):
    return jnp.dot(former, latter, preferred_element_type=jnp.float32)


def rows_product(former, latter):
    return lax.dot_general(
        former, latter, (((0,), (0,)), ((), ())), preferred_element_type=jnp.float32
    )


def against_transposed(former, latter):
    return lax.dot_general(
        former, latter, (((1,), (1,)), ((), ())), preferred_element_type=jnp.float32
    )


def centered_norm(stream):
    row_sum = jnp.sum(stream, axis=1, keepdims=True)
    decompressed = jnp.concatenate([stream, -row_sum], axis=1)
    mean_sq = jnp.mean(decompressed * decompressed, axis=1, keepdims=True)
    factor = lax.rsqrt(mean_sq + epsilon)
    return (decompressed * factor, factor, mean_sq)


def centered_norm_back(d_lifted, normed, factor, gain):
    d_normed = d_lifted * gain
    d_gain = jnp.sum(d_lifted * normed, axis=0, keepdims=True)
    d_whole = factor * (d_normed - normed * jnp.mean(d_normed * normed, axis=1, keepdims=True))
    last = d_whole.shape[1] - 1
    return (d_whole[:, :last] - d_whole[:, last:], d_gain)


def column_tiles(whole, width):
    return [slice(j * width, (j + 1) * width) for j in range(whole // width)]


def in_vmem(array):
    return pltpu.with_memory_space_constraint(array, pltpu.VMEM)


def in_hbm(array):
    return pltpu.with_memory_space_constraint(array, pltpu.HBM)


def slot_rows(slot, count):
    return pl.ds(pl.multiple_of(slot * count, count), count)


def seq_sums_shape(lengths):
    return (-(-lengths.shape[0] // 8) * 8, PAIR)


def add_sequences(table, stat, seq_sums, space):
    lengths, slots, sems = space
    copies = [pltpu.make_async_copy(a, b, sems.at[i]) for i, (a, b) in enumerate(zip(table, (lengths, slots)))]
    for copy in copies:
        copy.start()
    for copy in copies:
        copy.wait()
    first_slot = lax.axis_index("dp") * MICRO
    rows = stat.shape[0] // MICRO
    place = lax.broadcasted_iota(jnp.int32, (rows, PAIR), 0)

    def step(number, starts):
        nexts = []
        for index, start in enumerate(starts):
            member = slots[number] == first_slot + index
            stop = start + lengths[number]

            @pl.when(member)
            def _():
                held = stat[index * rows : (index + 1) * rows]
                total = jnp.sum(jnp.where((place >= start) & (place < stop), held, 0.0), axis=0, keepdims=True)
                seq_sums[pl.ds(number, 1)] = total / lengths[number].astype(jnp.float32)

            nexts.append(jnp.where(member, stop, start))
        return tuple(nexts)

    lax.fori_loop(0, lengths.shape[0], step, (jnp.int32(0),) * MICRO)


def table_space(lengths):
    return [pltpu.SMEM(lengths.shape, jnp.int32)] * 2 + [pltpu.SemaphoreType.DMA((2,))]


def write_masks(lengths, slots, first_slot, bias, bias_turned):
    rows = bias.shape[1]
    place = lax.broadcasted_iota(jnp.int32, (8, rows), 1)

    def step(number, carry):
        nexts, begins = [], []
        for index, (start, begin) in enumerate(zip(*carry)):
            member = slots[number] == first_slot + index
            begins.append(jnp.where(place >= jnp.where(member, start, rows), start, begin))
            nexts.append(start + jnp.where(member, lengths[number], 0))
        return tuple(nexts), tuple(begins)

    none = jnp.zeros((8, rows), jnp.int32)
    _, begins = lax.fori_loop(0, lengths.shape[0], step, ((jnp.int32(0),) * MICRO, (none,) * MICRO))
    key = lax.broadcasted_iota(jnp.int32, (rows, rows), 0)
    row = lax.broadcasted_iota(jnp.int32, (rows, rows), 1)
    for index, begin in enumerate(begins):
        turned = jnp.where((key <= row) & (key >= begin[:1]), 0.0, -1e30)
        bias_turned[index * rows : (index + 1) * rows] = turned
        bias[index * rows : (index + 1) * rows] = turned.T


def forward_kernel(*refs, moment):
    if moment == 0:
        lengths_h, slots_h, attn_h, mlp_h, stream_in, qkv_h, out_h, up_h, down_h = refs[:9]
        refs = refs[9:]
    else:
        received, qkv_w, out_w, up_w, down_w, norm_gains, bias = refs[:7]
        refs = refs[7 + 11 :]
        if moment == MICRO:
            table = refs[:2]
            refs = refs[3:]
    leaving, entering, result, lifted, packed, mixed, log_total, normed_mlp, lifted_mlp, active, slope, stat = refs[:12]
    refs = refs[12:]
    section = lax.axis_index("section")
    slot = moment - section
    rows, compressed = leaving.shape
    width = compressed + 1
    tiles = column_tiles(slope.shape[1], width)
    thirds = column_tiles(3 * width, width)
    waits = {}
    if moment == 0:
        qkv_w, out_w, up_w, down_w, norm_gains, bias, bias_turned, seq_sums, lengths, slots, sems = refs

        def load(name, source, target):
            copy = pltpu.make_async_copy(source, target, sems.at[len(waits)])
            waits[name] = copy
            copy.start()

        load("lengths", lengths_h, lengths)
        load("slots", slots_h, slots)
        load("attn", attn_h, norm_gains.at[pl.ds(0, 1)])
        load("mlp", mlp_h, norm_gains.at[pl.ds(8, 1)])
        load("entering", stream_in, entering)
        for t in thirds:
            load(("qkv", t.start), qkv_h.at[:, t], qkv_w.at[:, t])
        load("out", out_h, out_w)
        for t in tiles:
            load(("up", t.start), up_h.at[:, t], up_w.at[:, t])
            load(("down", t.start), down_h.at[t], down_w.at[t])
        seq_sums[...] = jnp.zeros_like(seq_sums)
        waits.pop("lengths").wait()
        waits.pop("slots").wait()
        write_masks(lengths, slots, lax.axis_index("dp") * MICRO, bias, bias_turned)
    elif moment == MICRO:
        seq_sums, *space = refs

    def arrive(*name):
        if moment == 0:
            waits[name if len(name) > 1 else name[0]].wait()

    def work():
        here = slot_rows(slot, rows)
        if moment == 0:
            arrive("entering")
            arrive("attn")
            arrive("mlp")
        else:

            @pl.when(section != 0)
            def _():
                entering[here] = received[...]

        base = entering[here].astype(jnp.float32)
        normed, _, square_attn = centered_norm(base)
        lifted[here] = (normed * norm_gains[0:1]).astype(jnp.bfloat16)
        for t in thirds:
            arrive("qkv", t.start)
            packed[here, t] = product(lifted[here], qkv_w[:, t]).astype(jnp.bfloat16)
        lane = lax.broadcasted_iota(jnp.int32, (rows, PAIR), 1)
        zero = jnp.zeros((rows, PAIR), jnp.bfloat16)
        totals = jnp.zeros((rows, PAIR), jnp.float32)
        for pair in range(width // PAIR):
            at = pair * PAIR
            queries = packed[here, at : at + PAIR] * jnp.asarray(SCALE, jnp.bfloat16)
            key_part = packed[here, width + at : width + at + PAIR]
            values = packed[here, 2 * width + at : 2 * width + at + PAIR]
            joined = None
            for half, keep in enumerate((lane < HD, lane >= HD)):
                scores = against_transposed(jnp.where(keep, queries, zero), key_part) + bias[here]
                peak = jnp.max(scores, axis=1, keepdims=True)
                exponent = jnp.exp(scores - peak)
                total = jnp.sum(exponent, axis=1, keepdims=True)
                attention = (exponent / total).astype(jnp.bfloat16)
                part = product(attention, jnp.where(keep, values, zero))
                joined = part if joined is None else joined + part
                totals = jnp.where(lane == 2 * pair + half, peak + jnp.log(total), totals)
            mixed[here, at : at + PAIR] = joined.astype(jnp.bfloat16)
        log_total[slot_rows(slot, LSE_ROWS)] = totals.T[:LSE_ROWS]
        arrive("out")
        middle = base + product(mixed[here], out_w[...])
        normed, factor, square_mlp = centered_norm(middle)
        normed_mlp[here] = normed
        lifted_mlp[here] = (normed * norm_gains[8:9]).astype(jnp.bfloat16)
        stat[here] = jnp.where(lane == 0, square_attn, jnp.where(lane == 1, square_mlp, factor))
        total = middle
        for t in tiles:
            arrive("up", t.start)
            hidden = product(lifted_mlp[here], up_w[:, t])
            squared = hidden * hidden
            bend = jnp.tanh(hidden * (GELU_A + GELU_A * GELU_B * squared))
            gate = 0.5 + 0.5 * bend
            value = hidden * gate
            slope[here, t] = (
                gate + value * (1.0 - bend) * (GELU_A + 3 * GELU_A * GELU_B * squared)
            ).astype(jnp.bfloat16)
            active[here, t] = value.astype(jnp.bfloat16)
            arrive("down", t.start)
            total = total + product(active[here, t], down_w[t])
        leaving[...] = total.astype(jnp.bfloat16)
        result[here] = leaving[...]

    pl.when((slot >= 0) & (slot < MICRO))(work)
    if moment == 0:

        @pl.when(slot != 0)
        def _():
            for copy in waits.values():
                copy.wait()

    if moment == MICRO:

        @pl.when(section == 0)
        def _():
            add_sequences(table, stat, seq_sums, space)


def forward_layer(moment, inputs, received, weights, bias, stacks, seq_sums=None):
    if moment == 0:
        lengths, slots, attn_gain, mlp_gain, stream_in = inputs
        rows = stream_in.shape[0] // MICRO
        compressed = stream_in.shape[1]
    else:
        rows, compressed = received.shape
    width, inner = weights[2].shape
    low, full = jnp.bfloat16, jnp.float32
    blocks = [
        ((rows, compressed), low),
        ((rows, compressed), low),
        ((rows, width), low),
        ((rows, 3 * width), low),
        ((rows, width), low),
        ((LSE_ROWS, rows), full),
        ((rows, width), full),
        ((rows, width), low),
        ((rows, inner), low),
        ((rows, inner), low),
        ((rows, PAIR), full),
    ]
    out_shape = [pltpu.VMEM((rows, compressed), low)]
    out_shape += [pltpu.VMEM((MICRO * shape[0], shape[1]), kind) for shape, kind in blocks]
    if moment == 0:
        out_shape += [pltpu.VMEM(w.shape, low) for w in weights]
        out_shape += [pltpu.VMEM((16, width), full)]
        out_shape += [pltpu.VMEM((MICRO * rows, rows), full)] * 2
        out_shape += [pltpu.VMEM(seq_sums_shape(lengths), full)]
        args = [in_hbm(a) for a in (*inputs, *weights)]
        in_specs = [HBM] * len(args)
        aliases = {}
        scratch = [pltpu.SMEM(lengths.shape, jnp.int32)] * 2 + [pltpu.SemaphoreType.DMA((17,))]
    else:
        args = [in_vmem(a) for a in (received, *weights, bias)]
        args += [in_vmem(s) for s in stacks]
        in_specs = [VMEM] * len(args)
        aliases = {7 + i: 1 + i for i in range(len(blocks))}
        scratch = []
        if moment == MICRO:
            aliases[len(args) + 2] = len(out_shape)
            args += [in_hbm(inputs[0]), in_hbm(inputs[1]), in_vmem(seq_sums)]
            in_specs += [HBM, HBM, VMEM]
            out_shape += [pltpu.VMEM(seq_sums.shape, full)]
            scratch = table_space(inputs[0])
    outs = pl.pallas_call(
        functools.partial(forward_kernel, moment=moment),
        out_shape=out_shape,
        in_specs=in_specs,
        out_specs=[VMEM] * len(out_shape),
        input_output_aliases=aliases,
        scratch_shapes=scratch,
        compiler_params=pltpu.CompilerParams(vmem_limit_bytes=KERNEL_VMEM),
        cost_estimate=pl.CostEstimate(flops=4 * 10**9, bytes_accessed=10 * 10**6, transcendentals=2 * 10**6),
        name="forward_layer",
    )(*args)
    return outs[0], outs[1:12], outs[12:]


def backward_kernel(*refs, moment):
    first = moment == 0
    if first:
        cotangent, refs = refs[0], refs[1:]
    else:
        received, refs = refs[0], refs[1:]
    qkv_w, out_w, up_w, down_w, norm_gains, bias = refs[:6]
    entering, packed, log_total, normed_mlp, stat, slope = refs[6:12]
    refs = refs[12 if first else 18 :]
    last = moment == MICRO
    if last:
        table = refs[:2]
        refs = refs[3:]
    leaving, incoming, d_input, d_hidden, d_branch, d_packed, gains = refs[:7]
    refs = refs[7:]
    if last:
        seq_sums, refs = refs[0], refs[1:]
    d_heads = refs[0]
    section = lax.axis_index("section")
    slot = MICRO - moment - section
    rows, compressed = leaving.shape
    width = compressed + 1
    tiles = column_tiles(slope.shape[1], width)
    if first:
        sems = refs[1]

        @pl.when(section != 0)
        def _():
            copy = pltpu.make_async_copy(cotangent, incoming, sems.at[0])
            copy.start()
            copy.wait()

    def work():
        here = slot_rows(slot, rows)
        if not first:

            @pl.when(section == 0)
            def _():
                incoming[here] = received[...]

        d_lifted = jnp.zeros((rows, width), jnp.float32)
        for t in tiles:
            d_active = against_transposed(incoming[here], down_w[t])
            d_hidden[here, t] = (d_active * slope[here, t].astype(jnp.float32)).astype(jnp.bfloat16)
            d_lifted = d_lifted + against_transposed(d_hidden[here, t], up_w[:, t])
        d_norm, mlp_part = centered_norm_back(d_lifted, normed_mlp[here], stat[here, 2:3], norm_gains[8:9])
        d_middle = incoming[here].astype(jnp.float32) + d_norm
        d_branch[here] = d_middle.astype(jnp.bfloat16)
        d_heads[...] = against_transposed(d_branch[here], out_w[...]).astype(jnp.bfloat16)
        lane = lax.broadcasted_iota(jnp.int32, (rows, PAIR), 1)
        zero = jnp.zeros((rows, PAIR), jnp.bfloat16)
        heads_total = log_total[slot_rows(slot, LSE_ROWS)]
        for pair in range(width // PAIR):
            at = pair * PAIR
            queries = packed[here, at : at + PAIR] * jnp.asarray(SCALE, jnp.bfloat16)
            key_part = packed[here, width + at : width + at + PAIR]
            values = packed[here, 2 * width + at : 2 * width + at + PAIR]
            d_part = d_heads[:, at : at + PAIR]
            sums = None
            for half, keep in enumerate((lane < HD, lane >= HD)):
                own_queries = jnp.where(keep, queries, zero)
                own_keys = jnp.where(keep, key_part, zero)
                own_part = jnp.where(keep, d_part, zero)
                head = 2 * pair + half
                attention = jnp.exp(
                    against_transposed(key_part, own_queries) + bias[here] - heads_total[head : head + 1, :]
                )
                d_attention = against_transposed(values, own_part)
                d_scores = attention * (d_attention - jnp.sum(attention * d_attention, axis=0, keepdims=True))
                d_scores = d_scores.astype(jnp.bfloat16)
                terms = (
                    rows_product(own_keys, d_scores),
                    product(d_scores, own_queries),
                    product(attention.astype(jnp.bfloat16), own_part),
                )
                sums = terms if sums is None else tuple(a + b for a, b in zip(sums, terms))
            d_packed[here, at : at + PAIR] = (sums[0].T * SCALE).astype(jnp.bfloat16)
            d_packed[here, width + at : width + at + PAIR] = sums[1].astype(jnp.bfloat16)
            d_packed[here, 2 * width + at : 2 * width + at + PAIR] = sums[2].astype(jnp.bfloat16)
        d_lifted = jnp.zeros((rows, width), jnp.float32)
        for t in column_tiles(3 * width, width):
            d_lifted = d_lifted + against_transposed(d_packed[here, t], qkv_w[:, t])
        normed, factor, _ = centered_norm(entering[here].astype(jnp.float32))
        d_norm, attn_part = centered_norm_back(d_lifted, normed, factor, norm_gains[0:1])
        leaving[...] = (d_middle + d_norm).astype(jnp.bfloat16)
        d_input[here] = leaving[...]
        number = lax.broadcasted_iota(jnp.int32, (8, width), 0)
        gains[slot_rows(slot, 8)] = jnp.where(number == 0, attn_part, jnp.where(number == 1, mlp_part, 0.0))

    pl.when((slot >= 0) & (slot < MICRO))(work)
    if last:

        @pl.when(section != 0)
        def _():
            add_sequences(table, stat, seq_sums, refs[1:])


def backward_layer(moment, cotangent, received, weights, bias, stored, stacks, sequences):
    width, inner = weights[2].shape
    rows = bias.shape[1]
    compressed = width - 1
    low, full = jnp.bfloat16, jnp.float32
    blocks = [
        ((rows, compressed), low),
        ((rows, compressed), low),
        ((rows, inner), low),
        ((rows, compressed), low),
        ((rows, 3 * width), low),
        ((8, width), full),
    ]
    out_shape = [pltpu.VMEM((rows, compressed), low)]
    out_shape += [pltpu.VMEM((MICRO * shape[0], shape[1]), kind) for shape, kind in blocks]
    args = [in_hbm(cotangent) if moment == 0 else in_vmem(received)]
    args += [in_vmem(a) for a in (*weights, bias, *stored)]
    in_specs = [HBM if moment == 0 else VMEM] + [VMEM] * (len(args) - 1)
    aliases = {}
    scratch = [pltpu.VMEM((rows, width), low)]
    if moment == 0:
        scratch += [pltpu.SemaphoreType.DMA((1,))]
    else:
        aliases = {len(args) + i: 1 + i for i in range(len(blocks))}
        in_specs += [VMEM] * len(blocks)
        args += [in_vmem(s) for s in stacks]
    if moment == MICRO:
        lengths, slots, seq_sums = sequences
        aliases[len(args) + 2] = len(out_shape)
        args += [in_hbm(lengths), in_hbm(slots), in_vmem(seq_sums)]
        in_specs += [HBM, HBM, VMEM]
        out_shape += [pltpu.VMEM(seq_sums.shape, full)]
        scratch += table_space(lengths)
    outs = pl.pallas_call(
        functools.partial(backward_kernel, moment=moment),
        out_shape=out_shape,
        in_specs=in_specs,
        out_specs=[VMEM] * len(out_shape),
        input_output_aliases=aliases,
        scratch_shapes=scratch,
        compiler_params=pltpu.CompilerParams(vmem_limit_bytes=KERNEL_VMEM),
        cost_estimate=pl.CostEstimate(flops=4 * 10**9, bytes_accessed=10 * 10**6, transcendentals=2 * 10**6),
        name="backward_layer",
    )(*args)
    return outs[0], outs[1:]


STRIDES = {"v": 8, "w": 4, "y": 2, "x": 1}


def place_along(axis):
    return lax.rem(lax.div(lax.axis_index("dp"), jnp.int32(STRIDES[axis])), jnp.int32(2))


def gradient_kernel(former, latter, *refs, axis, by_columns, chained, last):
    if chained:
        refs = refs[1:]
    away, own = refs[:2]
    refs = refs[2:]
    step = pl.program_id(0)
    if last:
        for number, name in enumerate(STRIDES):
            refs[0][number] = place_along(name)
        refs = refs[1:]
    if by_columns:
        turned, whole = refs[:2]
        tile = whole.shape[-1]
        columns = pl.ds(pl.multiple_of(step * tile, PAIR), tile) if tile % PAIR == 0 else slice(None)

        @pl.when(step == 0)
        def _():
            turned[...] = former[...].T

        whole[...] = product(turned[...], latter[:, columns]).reshape(whole.shape)
    else:
        whole = refs[0]
        tile = former.shape[1] // pl.num_programs(0)
        columns = pl.ds(pl.multiple_of(step * tile, PAIR), tile)
        whole[...] = rows_product(former[:, columns], latter[...]).reshape(whole.shape)
    side = place_along(axis)
    for target, place in ((away, 1 - side), (own, side)):
        index = (slice(None),) * list(STRIDES).index(axis) + (pl.ds(place, 1),)
        target[...] = whole[index].astype(target.dtype)


def halved(shape, axis):
    dim = list(STRIDES).index(axis)
    return shape[:dim] + (1,) + shape[dim + 1 :]


def weight_gradient(former, latter, axis, tile, name, after=None, last=False):
    tokens, tall = former.shape
    wide = latter.shape[1]
    shape = (2, 2, 2, 2, tall // 16, wide)
    if tile:
        block = shape[:5] + (tile,)
        grid = (wide // tile,)
        out_spec = pl.BlockSpec(halved(block, axis), lambda j: (0, 0, 0, 0, 0, j))
        scratch = [pltpu.VMEM((tall, tokens), jnp.bfloat16), pltpu.VMEM(block, jnp.float32)]
    else:
        block = (1, 1) + shape[2:]
        grid = (4,)
        out_spec = pl.BlockSpec(halved(block, axis), lambda j: (j // 2, j % 2, 0, 0, 0, 0))
        scratch = [pltpu.VMEM(block, jnp.float32)]
    args = [in_vmem(former), in_vmem(latter)]
    in_specs = [VMEM, VMEM]
    out_shape = [pltpu.HBM(halved(shape, axis), jnp.bfloat16), pltpu.HBM(halved(shape, axis), jnp.float32)]
    out_specs = [out_spec, out_spec]
    if after is not None:
        args.append(in_hbm(after))
        in_specs.append(HBM)
    if last:
        out_shape.append(shaped((4,), jnp.int32))
        out_specs.append(SMEM)
    return pl.pallas_call(
        functools.partial(
            gradient_kernel, axis=axis, by_columns=bool(tile), chained=after is not None, last=last
        ),
        grid=grid,
        in_specs=in_specs,
        out_specs=out_specs,
        scratch_shapes=scratch,
        out_shape=out_shape,
        compiler_params=pltpu.CompilerParams(vmem_limit_bytes=KERNEL_VMEM),
        cost_estimate=pl.CostEstimate(
            flops=2 * tokens * tall * wide,
            bytes_accessed=2 * tokens * (tall + wide) + 3 * tall * wide,
            transcendentals=0,
        ),
        name=name,
    )(*args)


def exchange(block, axis):
    size = lax.axis_size("dp")
    return lax.ppermute(block, "dp", [(i, i ^ STRIDES[axis]) for i in range(size)])


def parted(total, axis, places):
    dim = list(STRIDES).index(axis)
    away = lax.dynamic_index_in_dim(total, 1 - places[dim], dim, keepdims=True)
    return away, lax.dynamic_index_in_dim(total, places[dim], dim, keepdims=True)


def scattered(halves, orders, places):
    halves = [tuple(h[:2]) for h in halves]
    for turn in range(4):
        got = [exchange(away, order[turn]) for (away, _), order in zip(halves, orders)]
        got = [g.astype(jnp.float32) for g in got]
        totals = [own + g for (_, own), g in zip(halves, got)]
        if turn == 3:
            return [t.reshape(t.shape[-2:]) for t in totals]
        halves = []
        for total, order in zip(totals, orders):
            away, own = parted(total, order[turn + 1], places)
            halves.append((away.astype(jnp.bfloat16), own))


def shards(
    stream_in,
    cotangent,
    qkv_weight,
    out_weight,
    up_weight,
    down_weight,
    attn_gain,
    mlp_gain,
    seq_lengths,
    seq_slot,
):
    chips = lax.axis_size("dp")
    compressed = stream_in.shape[1]
    weights = (qkv_weight[0], out_weight[0], up_weight[0], down_weight[0])
    inputs = (seq_lengths, seq_slot, attn_gain, mlp_gain, stream_in)

    received = stored = bias = seq_sums = None
    for moment in range(MICRO + 1):
        leaving, stored, more = forward_layer(moment, inputs, received, weights, bias, stored, seq_sums)
        if moment == 0:
            weights, bias, bias_turned, seq_sums = more[:5], more[5], more[6], more[7]
        if moment < MICRO:
            received = shifted(leaving, "section", 1)
        else:
            (seq_sums,) = more
    entering, stream_out, lifted, packed, mixed, log_total, normed_mlp, lifted_mlp, active, slope, stat = stored

    kept = (entering, packed, log_total, normed_mlp, stat, slope)
    received = grads = None
    for moment in range(MICRO + 1):
        sequences = (seq_lengths, seq_slot, seq_sums)
        leaving, grads = backward_layer(
            moment, cotangent, received, weights, bias_turned, kept, grads, sequences
        )
        if moment < MICRO:
            received = shifted(leaving, "section", -1)
    incoming, stream_grad, d_hidden, d_branch, d_packed, gain_parts, seq_sums = grads

    if chips == CORE_CHIPS:
        down = weight_gradient(active, incoming, "x", None, "down_gradient")
        up = weight_gradient(lifted_mlp, d_hidden, "y", 512, "up_gradient", down[1])
        out = weight_gradient(mixed, d_branch, "w", compressed, "out_gradient", up[1])
        *qkv, places = weight_gradient(lifted, d_packed, "w", 768, "qkv_gradient", out[1], last=True)
    gains = jnp.sum(gain_parts.reshape(MICRO, 8, -1)[:, :2], axis=0)
    seq_terms = seq_sums[: seq_lengths.shape[0], :2]
    small = jnp.concatenate(
        [gains[0].reshape(chips, -1), gains[1].reshape(chips, -1), seq_terms.reshape(chips, -1)], axis=1
    )
    count = gains.shape[1] // chips
    if chips == CORE_CHIPS:
        small = small.reshape(2, 2, 2, 2, 1, -1)
        for axis in "xywv":
            away, own = parted(small, axis, places)
            small = own + exchange(away, axis)
        small = small.reshape(-1)
        orders = ("xywv", "ywxv", "wxyv", "wxyv")
        down_part, up_part, out_part, qkv_part = scattered((down, up, out, qkv), orders, places)
    else:
        small = lax.psum_scatter(small, "dp", scatter_dimension=0, tiled=True).reshape(-1)
        pairs = ((active, incoming), (lifted_mlp, d_hidden), (mixed, d_branch), (lifted, d_packed))
        down_part, up_part, out_part, qkv_part = (
            lax.psum_scatter(rows_product(a, b), "dp", scatter_dimension=0, tiled=True) for a, b in pairs
        )
    attn_part, mlp_part, seq_part = small[:count], small[count : 2 * count], small[2 * count :].reshape(-1, 2)
    return (
        stream_out[None],
        stream_grad[None],
        qkv_part[None],
        out_part[None],
        up_part[None],
        down_part[None],
        attn_part[None],
        mlp_part[None],
        seq_part[None],
    )


def solution(mesh):
    placed = (
        P("dp", None),
        P("dp", None),
        P("section", None, None),
        P("section", None, None),
        P("section", None, None),
        P("section", None, None),
        P("section", None),
        P("section", None),
        P(),
        P(),
    )
    return jax.shard_map(
        shards,
        mesh=mesh,
        in_specs=placed,
        out_specs=(
            P("section", "dp", None),
            P("section", "dp", None),
            P("section", "dp", None),
            P("section", "dp", None),
            P("section", "dp", None),
            P("section", "dp", None),
            P("section", "dp"),
            P("section", "dp"),
            P("section", "dp", None),
        ),
        check_vma=False,
    )
```

```python
import functools

import jax
import jax.numpy as jnp
from jax import lax
from jax.experimental import pallas as pl
from jax.experimental.pallas import tpu as pltpu
from jax.sharding import PartitionSpec as P

HD = 64
MICRO = 2
PAIR = 2 * HD
SCALE = HD ** (-0.5)
LSE_ROWS = 16
GELU_A = 0.7978845608028654
GELU_B = 0.044715
CORE_CHIPS = 16

epsilon = 1e-05
SPARE = 16

VMEM = pl.BlockSpec(memory_space=pltpu.VMEM)
ANY = pl.BlockSpec(memory_space=pl.ANY)
SMEM = pl.BlockSpec(memory_space=pltpu.SMEM)
HBM = pl.BlockSpec(memory_space=pltpu.HBM)
MIB = 2**20
BRIEF = pl.CostEstimate(flops=10**6, bytes_accessed=10**4, transcendentals=0)
LONG = pl.CostEstimate(flops=8 * 10**9, bytes_accessed=10**4, transcendentals=0)
SHORT = pl.CostEstimate(flops=10**9, bytes_accessed=10**4, transcendentals=0)
KERNEL_VMEM = 30 * MIB


def shaped(shape, dtype):
    return jax.ShapeDtypeStruct(shape, dtype)


def shifted(block, axis, distance):
    devices = range(lax.axis_size(axis))
    route = [(i - distance, i) for i in devices if i - distance in devices]
    return lax.ppermute(block, axis, route)


def product(former, latter):
    return jnp.dot(former, latter, preferred_element_type=jnp.float32)


def rows_product(former, latter):
    return lax.dot_general(
        former, latter, (((0,), (0,)), ((), ())), preferred_element_type=jnp.float32
    )


def against_transposed(former, latter):
    return lax.dot_general(
        former, latter, (((1,), (1,)), ((), ())), preferred_element_type=jnp.float32
    )


def centered_norm(stream):
    row_sum = jnp.sum(stream, axis=1, keepdims=True)
    decompressed = jnp.concatenate([stream, -row_sum], axis=1)
    mean_sq = jnp.mean(decompressed * decompressed, axis=1, keepdims=True)
    factor = lax.rsqrt(mean_sq + epsilon)
    return (decompressed * factor, factor, mean_sq)


def centered_norm_back(d_lifted, normed, factor, gain):
    d_normed = d_lifted * gain
    d_gain = jnp.sum(d_lifted * normed, axis=0, keepdims=True)
    d_whole = factor * (d_normed - normed * jnp.mean(d_normed * normed, axis=1, keepdims=True))
    last = d_whole.shape[1] - 1
    return (d_whole[:, :last] - d_whole[:, last:], d_gain)


def column_tiles(whole, width):
    return [slice(j * width, (j + 1) * width) for j in range(whole // width)]


def in_vmem(array):
    return pltpu.with_memory_space_constraint(array, pltpu.VMEM)


def in_hbm(array):
    return pltpu.with_memory_space_constraint(array, pltpu.HBM)


STRIDES = {"v": 8, "w": 4, "y": 2, "x": 1}


def side(axis):
    if lax.axis_size("dp") != CORE_CHIPS:
        return jnp.int32(0)
    return lax.rem(lax.div(lax.axis_index("dp"), jnp.int32(STRIDES[axis])), jnp.int32(2))


def span(start, size):
    return pl.ds(pl.multiple_of(start * size, size), size)


def slot_rows(slot, count):
    return pl.ds(pl.multiple_of(slot * count, count), count)


def seq_sums_shape(lengths):
    return (-(-lengths.shape[0] // 8) * 8, PAIR)


def add_sequences(table, stat, seq_sums, space):
    lengths, slots, sems = space
    copies = [pltpu.make_async_copy(a, b, sems.at[i]) for i, (a, b) in enumerate(zip(table, (lengths, slots)))]
    for copy in copies:
        copy.start()
    for copy in copies:
        copy.wait()
    first_slot = lax.axis_index("dp") * MICRO
    rows = stat.shape[0] // MICRO
    place = lax.broadcasted_iota(jnp.int32, (rows, PAIR), 0)

    def step(number, starts):
        nexts = []
        for index, start in enumerate(starts):
            member = slots[number] == first_slot + index
            stop = start + lengths[number]

            @pl.when(member)
            def _():
                held = stat[index * rows : (index + 1) * rows]
                total = jnp.sum(jnp.where((place >= start) & (place < stop), held, 0.0), axis=0, keepdims=True)
                seq_sums[pl.ds(number, 1)] = total / lengths[number].astype(jnp.float32)

            nexts.append(jnp.where(member, stop, start))
        return tuple(nexts)

    lax.fori_loop(0, lengths.shape[0], step, (jnp.int32(0),) * MICRO)


def table_space(lengths):
    return [pltpu.SMEM(lengths.shape, jnp.int32)] * 2 + [pltpu.SemaphoreType.DMA((2,))]


def write_masks(lengths, slots, first_slot, bias, bias_turned):
    rows = bias.shape[1]
    place = lax.broadcasted_iota(jnp.int32, (8, rows), 1)

    def step(number, carry):
        nexts, begins = [], []
        for index, (start, begin) in enumerate(zip(*carry)):
            member = slots[number] == first_slot + index
            begins.append(jnp.where(place >= jnp.where(member, start, rows), start, begin))
            nexts.append(start + jnp.where(member, lengths[number], 0))
        return tuple(nexts), tuple(begins)

    none = jnp.zeros((8, rows), jnp.int32)
    _, begins = lax.fori_loop(0, lengths.shape[0], step, ((jnp.int32(0),) * MICRO, (none,) * MICRO))
    key = lax.broadcasted_iota(jnp.int32, (rows, rows), 0)
    row = lax.broadcasted_iota(jnp.int32, (rows, rows), 1)
    for index, begin in enumerate(begins):
        turned = jnp.where((key <= row) & (key >= begin[:1]), 0.0, -1e30)
        bias_turned[index * rows : (index + 1) * rows] = turned.astype(bias_turned.dtype)
        bias[index * rows : (index + 1) * rows] = turned.T.astype(bias.dtype)


def forward_kernel(*refs, moment):
    if moment == 0:
        lengths_h, slots_h, attn_h, mlp_h, stream_in, qkv_h, out_h, up_h, down_h = refs[:9]
        refs = refs[9:]
    else:
        received, qkv_w, out_w, up_w, down_w, norm_gains, bias = refs[:7]
        refs = refs[7 + 11 :]
    leaving, entering, result, packed, log_total, normed_mlp, slope, stat = refs[:8]
    sends, refs = refs[8:12], refs[12:]
    lifted_mixed, lifted_mlp, active_own, active_away, send_sems = refs[-5:]
    refs = refs[:-5]
    section = lax.axis_index("section")
    slot = moment - section
    rows, compressed = leaving.shape
    width = compressed + 1
    thirds = column_tiles(3 * width, width)
    first_half, second_half = column_tiles(2 * width, width)
    tiles = []
    for away in (1, 0):
        for number in range(slope.shape[1] // (2 * width)):
            half = side("w") if away == 0 else 1 - side("w")
            tiles.append((number, away, span(2 * number + half, width)))
    waits = {}
    if moment == 0:
        qkv_w, out_w, up_w, down_w, norm_gains, bias, bias_turned, seq_sums, lengths, slots, sems = refs

        def load(name, source, target):
            copy = pltpu.make_async_copy(source, target, sems.at[len(waits)])
            waits[name] = copy
            copy.start()

        load("lengths", lengths_h, lengths)
        load("slots", slots_h, slots)
        load("attn", attn_h, norm_gains.at[pl.ds(0, 1)])
        load("mlp", mlp_h, norm_gains.at[pl.ds(8, 1)])
        load("entering", stream_in, entering)
        for t in thirds:
            load(("qkv", t.start), qkv_h.at[:, t], qkv_w.at[:, t])
        load("out", out_h, out_w)
        for number, away, t in tiles:
            load(("up", number, away), up_h.at[:, t], up_w.at[:, t])
            load(("down", number, away), down_h.at[t], down_w.at[t])
        seq_sums[...] = jnp.zeros_like(seq_sums)
        waits.pop("lengths").wait()
        waits.pop("slots").wait()
        write_masks(lengths, slots, lax.axis_index("dp") * MICRO, bias, bias_turned)

    def arrive(*name):
        if moment == 0:
            waits[name if len(name) > 1 else name[0]].wait()

    def work():
        here = slot_rows(slot, rows)
        if moment == 0:
            arrive("entering")
            arrive("attn")
            arrive("mlp")
        else:

            @pl.when(section != 0)
            def _():
                entering[here] = received[...]

        copies = []

        def send(number, block):
            copy = pltpu.make_async_copy(block, sends[number].at[here], send_sems.at[number])
            copy.start()
            copies.append(copy)

        base = entering[here].astype(jnp.float32)
        normed, _, square_attn = centered_norm(base)
        lifted_mixed[:, first_half] = (normed * norm_gains[0:1]).astype(jnp.bfloat16)
        for t in thirds:
            arrive("qkv", t.start)
            packed[here, t] = product(lifted_mixed[:, first_half], qkv_w[:, t]).astype(jnp.bfloat16)
        lane = lax.broadcasted_iota(jnp.int32, (rows, PAIR), 1)
        zero = jnp.zeros((rows, PAIR), jnp.bfloat16)
        totals = jnp.zeros((rows, PAIR), jnp.float32)
        for pair in range(width // PAIR):
            at = pair * PAIR
            queries = packed[here, at : at + PAIR] * jnp.asarray(SCALE, jnp.bfloat16)
            key_part = packed[here, width + at : width + at + PAIR]
            values = packed[here, 2 * width + at : 2 * width + at + PAIR]
            joined = None
            for half, keep in enumerate((lane < HD, lane >= HD)):
                scores = against_transposed(jnp.where(keep, queries, zero), key_part) + bias[here].astype(jnp.float32)
                peak = jnp.max(scores, axis=1, keepdims=True)
                exponent = jnp.exp(scores - peak)
                total = jnp.sum(exponent, axis=1, keepdims=True)
                attention = (exponent / total).astype(jnp.bfloat16)
                part = product(attention, jnp.where(keep, values, zero))
                joined = part if joined is None else joined + part
                totals = jnp.where(lane == 2 * pair + half, peak + jnp.log(total), totals)
            lifted_mixed[:, width + at : width + at + PAIR] = joined.astype(jnp.bfloat16)
        send(0, lifted_mixed)
        log_total[slot_rows(slot, LSE_ROWS)] = totals.T[:LSE_ROWS]
        arrive("out")
        middle = base + product(lifted_mixed[:, second_half], out_w[...])
        normed, factor, square_mlp = centered_norm(middle)
        normed_mlp[here] = normed
        lifted_mlp[...] = (normed * norm_gains[8:9]).astype(jnp.bfloat16)
        send(1, lifted_mlp)
        stat[here] = jnp.where(lane == 0, square_attn, jnp.where(lane == 1, square_mlp, factor))
        total = middle
        for number, away, t in tiles:
            arrive("up", number, away)
            hidden = product(lifted_mlp[...], up_w[:, t])
            squared = hidden * hidden
            bend = jnp.tanh(hidden * (GELU_A + GELU_A * GELU_B * squared))
            gate = 0.5 + 0.5 * bend
            value = hidden * gate
            slope[here, t] = (
                gate + value * (1.0 - bend) * (GELU_A + 3 * GELU_A * GELU_B * squared)
            ).astype(jnp.bfloat16)
            active = value.astype(jnp.bfloat16)
            place = slice(number * width, (number + 1) * width)
            if away:
                active_away[:, place] = active
            else:
                active_own[:, place] = active
            arrive("down", number, away)
            total = total + product(active, down_w[t])
            if number + 1 == slope.shape[1] // (2 * width):
                send(2 + away, active_away if away else active_own)
        leaving[...] = total.astype(jnp.bfloat16)
        result[here] = leaving[...]
        for copy in copies:
            copy.wait()

    pl.when((slot >= 0) & (slot < MICRO))(work)
    if moment == 0:

        @pl.when(slot != 0)
        def _():
            for copy in waits.values():
                copy.wait()


def forward_layer(moment, inputs, received, weights, bias, stacks):
    if moment == 0:
        lengths, slots, attn_gain, mlp_gain, stream_in = inputs
        rows = stream_in.shape[0] // MICRO
        compressed = stream_in.shape[1]
    else:
        rows, compressed = received.shape
    width, inner = weights[2].shape
    low, full = jnp.bfloat16, jnp.float32
    blocks = [
        ((rows, compressed), low),
        ((rows, compressed), low),
        ((rows, 3 * width), low),
        ((LSE_ROWS, rows), full),
        ((rows, width), full),
        ((rows, inner), low),
        ((rows, PAIR), full),
    ]
    sent = (2 * width, width, inner // 2, inner // 2)
    out_shape = [pltpu.VMEM((rows, compressed), low)]
    out_shape += [pltpu.VMEM((MICRO * shape[0], shape[1]), kind) for shape, kind in blocks]
    out_shape += [pltpu.HBM((MICRO * rows, wide), low) for wide in sent]
    out_specs = [VMEM] * (1 + len(blocks)) + [HBM] * 4
    if moment == 0:
        out_shape += [pltpu.VMEM(w.shape, low) for w in weights]
        out_shape += [pltpu.VMEM((16, width), full)]
        out_shape += [pltpu.VMEM((MICRO * rows, rows), low)] * 2
        out_shape += [pltpu.VMEM(seq_sums_shape(lengths), full)]
        out_specs += [VMEM] * (len(out_shape) - len(out_specs))
        args = [in_hbm(a) for a in (*inputs, *weights)]
        in_specs = [HBM] * len(args)
        aliases = {}
        scratch = [pltpu.SMEM(lengths.shape, jnp.int32)] * 2 + [pltpu.SemaphoreType.DMA((17,))]
    else:
        args = [in_vmem(a) for a in (received, *weights, bias)]
        in_specs = [VMEM] * len(args) + out_specs[1:]
        aliases = {7 + i: 1 + i for i in range(len(stacks))}
        args += [in_vmem(s) for s in stacks[:-4]] + [in_hbm(s) for s in stacks[-4:]]
        scratch = []
    outs = pl.pallas_call(
        functools.partial(forward_kernel, moment=moment),
        out_shape=out_shape,
        in_specs=in_specs,
        out_specs=out_specs,
        input_output_aliases=aliases,
        scratch_shapes=scratch
        + [pltpu.VMEM((rows, wide), low) for wide in sent]
        + [pltpu.SemaphoreType.DMA((4,))],
        compiler_params=pltpu.CompilerParams(vmem_limit_bytes=KERNEL_VMEM),
        cost_estimate=LONG,
        name="forward_layer",
    )(*args)
    return outs[0], outs[1:12], outs[12:]


def backward_kernel(*refs, moment, ordered):
    first = moment == 0
    if first:
        cotangent, refs = refs[0], refs[1:]
    else:
        received, refs = refs[0], refs[1:]
    if moment == 1:
        cotangent, refs = refs[0], refs[1:]
    qkv_w, out_w, up_w, down_w, norm_gains, bias = refs[:6]
    entering, packed, log_total, normed_mlp, stat, slope = refs[6:12]
    refs = refs[12 + (0, 5, 7)[moment] + ordered :]
    summing = moment != 1
    if summing:
        table = refs[:2]
        refs = refs[3:]
    leaving, incoming, d_input, gains, hidden_h, packed_h, *sends = refs[:8]
    refs = refs[8:]
    if moment == 1:
        crossing, refs = refs[0], refs[1:]
    if summing:
        seq_sums, refs = refs[0], refs[1:]
    d_heads, d_branch, d_packed, hidden_own, hidden_away, packed_own, packed_away, send_sems = refs[:8]
    refs = refs[8:]
    if moment == 1:
        passing = refs[0]
    section = lax.axis_index("section")
    slot = MICRO - moment - section
    rows, compressed = leaving.shape
    width = compressed + 1
    tiles = []
    for away in (1, 0):
        half = side("y") if away == 0 else 1 - side("y")
        for number in range(slope.shape[1] // (2 * width)):
            tiles.append((number, away, span(half * (slope.shape[1] // (2 * width)) + number, width)))
    if first:
        sems = refs[0]

        @pl.when(section != 0)
        def _():
            copy = pltpu.make_async_copy(cotangent, incoming, sems.at[0])
            copy.start()
            copy.wait()

    def work():
        here = slot_rows(slot, rows)
        if not first:

            @pl.when(section == 0)
            def _():
                incoming[here] = received[...]

        copies = []

        def send(block, target):
            copy = pltpu.make_async_copy(block, target, send_sems.at[len(copies)])
            copy.start()
            copies.append(copy)

        d_lifted = jnp.zeros((rows, width), jnp.float32)
        for number, away, t in tiles:
            d_active = against_transposed(incoming[here], down_w[t])
            d_hidden = (d_active * slope[here, t].astype(jnp.float32)).astype(jnp.bfloat16)
            place = slice(number * width, (number + 1) * width)
            if away:
                hidden_away[:, place] = d_hidden
            else:
                hidden_own[:, place] = d_hidden
            d_lifted = d_lifted + against_transposed(d_hidden, up_w[:, t])
            if number + 1 == slope.shape[1] // (2 * width):
                if away:
                    send(hidden_away, sends[0])
                else:
                    send(hidden_own, hidden_h.at[here])
        d_norm, mlp_part = centered_norm_back(d_lifted, normed_mlp[here], stat[here, 2:3], norm_gains[8:9])
        d_middle = incoming[here].astype(jnp.float32) + d_norm
        branch = d_middle.astype(jnp.bfloat16)
        d_branch[...] = jnp.concatenate([branch, jnp.zeros((rows, 1), jnp.bfloat16)], axis=1)
        d_heads[...] = against_transposed(branch, out_w[...]).astype(jnp.bfloat16)
        lane = lax.broadcasted_iota(jnp.int32, (rows, PAIR), 1)
        zero = jnp.zeros((rows, PAIR), jnp.bfloat16)
        heads_total = log_total[slot_rows(slot, LSE_ROWS)]
        for pair in range(width // PAIR):
            at = pair * PAIR
            queries = packed[here, at : at + PAIR] * jnp.asarray(SCALE, jnp.bfloat16)
            key_part = packed[here, width + at : width + at + PAIR]
            values = packed[here, 2 * width + at : 2 * width + at + PAIR]
            d_part = d_heads[:, at : at + PAIR]
            sums = None
            for half, keep in enumerate((lane < HD, lane >= HD)):
                own_queries = jnp.where(keep, queries, zero)
                own_keys = jnp.where(keep, key_part, zero)
                own_part = jnp.where(keep, d_part, zero)
                head = 2 * pair + half
                attention = jnp.exp(
                    against_transposed(key_part, own_queries) + bias[here].astype(jnp.float32) - heads_total[head : head + 1, :]
                )
                d_attention = against_transposed(values, own_part)
                d_scores = attention * (d_attention - jnp.sum(attention * d_attention, axis=0, keepdims=True))
                d_scores = d_scores.astype(jnp.bfloat16)
                terms = (
                    rows_product(own_keys, d_scores),
                    product(d_scores, own_queries),
                    product(attention.astype(jnp.bfloat16), own_part),
                )
                sums = terms if sums is None else tuple(a + b for a, b in zip(sums, terms))
            d_packed[:, at : at + PAIR] = (sums[0].T * SCALE).astype(jnp.bfloat16)
            d_packed[:, width + at : width + at + PAIR] = sums[1].astype(jnp.bfloat16)
            d_packed[:, 2 * width + at : 2 * width + at + PAIR] = sums[2].astype(jnp.bfloat16)
        middle, half = 3 * width // 2, width // 2
        mine = side("x")
        packed_own[:, :middle] = d_packed[:, span(mine, middle)]
        packed_own[:, middle:] = d_branch[:, span(mine, half)]
        packed_away[:, :middle] = d_packed[:, span(1 - mine, middle)]
        packed_away[:, middle:] = d_branch[:, span(1 - mine, half)]
        send(packed_away, sends[1])
        send(packed_own, packed_h.at[here])
        d_lifted = jnp.zeros((rows, width), jnp.float32)
        for t in column_tiles(3 * width, width):
            d_lifted = d_lifted + against_transposed(d_packed[:, t], qkv_w[:, t])
        normed, factor, _ = centered_norm(entering[here].astype(jnp.float32))
        d_norm, attn_part = centered_norm_back(d_lifted, normed, factor, norm_gains[0:1])
        leaving[...] = (d_middle + d_norm).astype(jnp.bfloat16)
        d_input[here] = leaving[...]
        if moment == 1:

            @pl.when(section != 0)
            def _():
                pltpu.make_async_copy(d_input, crossing, send_sems.at[4]).start()

        number = lax.broadcasted_iota(jnp.int32, (8, width), 0)
        gains[slot_rows(slot, 8)] = jnp.where(number == 0, attn_part, jnp.where(number == 1, mlp_part, 0.0))
        for copy in copies:
            copy.wait()

    if moment == 1:

        @pl.when(section == 0)
        def _():
            pltpu.make_async_copy(cotangent, passing, send_sems.at[4]).start()
            pltpu.make_async_copy(cotangent, passing, send_sems.at[4]).wait()
            pltpu.make_async_copy(passing, crossing, send_sems.at[4]).start()

    pl.when((slot >= 0) & (slot < MICRO))(work)
    if moment == 1:
        pltpu.make_async_copy(d_input, crossing, send_sems.at[4]).wait()
    if summing:

        @pl.when(section != 0 if moment else section == 0)
        def _():
            add_sequences(table, stat, seq_sums, refs[-3:])


def backward_layer(moment, cotangent, received, weights, bias, stored, stacks, sequences, after=()):
    width, inner = weights[2].shape
    rows = bias.shape[1]
    compressed = width - 1
    low, full = jnp.bfloat16, jnp.float32
    blocks = [
        ((rows, compressed), low),
        ((rows, compressed), low),
        ((8, width), full),
    ]
    out_shape = [pltpu.VMEM((rows, compressed), low)]
    out_shape += [pltpu.VMEM((MICRO * shape[0], shape[1]), kind) for shape, kind in blocks]
    sent = (inner // 2, 2 * width)
    out_shape += [pltpu.HBM((MICRO * rows, wide), low) for wide in sent]
    out_shape += [pltpu.HBM((rows, wide), low) for wide in sent]
    out_specs = [VMEM] * (1 + len(blocks)) + [HBM] * 4
    args = [in_hbm(cotangent) if moment == 0 else in_vmem(received)]
    if moment == 1:
        args.append(in_hbm(cotangent))
    args += [in_vmem(a) for a in (*weights, bias, *stored)]
    in_specs = ([HBM], [VMEM, HBM], [VMEM])[moment]
    in_specs = in_specs + [VMEM] * (len(args) - len(in_specs))
    scratch = [pltpu.VMEM((rows, n * width), low) for n in (1, 1, 3)]
    scratch += [pltpu.VMEM((rows, wide), low) for wide in sent for _ in range(2)]
    scratch += [pltpu.SemaphoreType.DMA((5,))]
    if moment == 0:
        scratch += [pltpu.SemaphoreType.DMA((1,))]
    given = list(stacks or [])
    aliases = {len(args) + i: 1 + i for i in range(len(given))}
    in_specs += out_specs[1 : 1 + len(given)]
    args += [in_vmem(s) for s in given[:3]] + [in_hbm(s) for s in given[3:]]
    if moment == 1:
        scratch += [pltpu.VMEM((MICRO * rows, compressed), low)]
        out_shape += [pltpu.HBM((MICRO * rows, compressed), low)]
        out_specs += [HBM]
    args += after
    in_specs += [ANY] * len(after)
    if moment != 1:
        lengths, slots, seq_sums = sequences
        aliases[len(args) + 2] = len(out_shape)
        args += [in_hbm(lengths), in_hbm(slots), in_vmem(seq_sums)]
        in_specs += [HBM, HBM, VMEM]
        out_shape += [pltpu.VMEM(seq_sums.shape, full)]
        out_specs += [VMEM]
        scratch += table_space(lengths)
    outs = pl.pallas_call(
        functools.partial(backward_kernel, moment=moment, ordered=len(after)),
        out_shape=out_shape,
        in_specs=in_specs,
        out_specs=out_specs,
        input_output_aliases=aliases,
        scratch_shapes=scratch,
        compiler_params=pltpu.CompilerParams(vmem_limit_bytes=KERNEL_VMEM),
        cost_estimate=LONG,
        name="backward_layer",
    )(*args)
    return outs


def exchange(block, axis):
    size = lax.axis_size("dp")
    return lax.ppermute(block, "dp", [(i, i ^ STRIDES[axis]) for i in range(size)])


def turned_over(block, axis):
    size = lax.axis_size("dp")
    route = [(k * size + i, (1 - k) * size + (i ^ STRIDES[axis])) for k in (0, 1) for i in range(size)]
    return lax.ppermute(block, ("section", "dp"), route)


def turn(target, column, block):
    rows = block.shape[0]
    for t in column_tiles(block.shape[1], 3 * PAIR):
        target[t, column : column + rows] = block[:, t].T


def parting(names, axis, rows):
    outer = 2 ** names.index(axis)
    inner = rows // (2 * outer)
    mine = side(axis)
    return [
        [pl.ds(pl.multiple_of((2 * number + half) * inner, 16), inner) for number in range(outer)]
        for half in (1 - mine, mine)
    ]


def gather_small(gain_parts, seq_sums, small, away, own):
    chips = small.shape[0]
    small[...] = jnp.zeros_like(small)
    count = gain_parts.shape[1] // chips
    each = -(-seq_sums.shape[0] // chips)
    for kind in (0, 1):
        gain = gain_parts[kind : kind + 1] + gain_parts[8 + kind : 9 + kind]
        for chip in range(chips):
            small[chip : chip + 1, kind * PAIR : kind * PAIR + count] = gain[:, chip * count : (chip + 1) * count]
    for chip in range(chips):
        for number in range(each):
            at = (2 + number) * PAIR
            small[chip : chip + 1, at : at + PAIR] = seq_sums[chip * each + number : chip * each + number + 1]
    mine = side("x")
    for number in range(chips // 2):
        away[number : number + 1] = small[pl.ds(2 * number + 1 - mine, 1)]
        own[number : number + 1] = small[pl.ds(2 * number + mine, 1)]


def gradient_kernel(*refs, kind, names, axis, chained):
    *formers, latter, crossing = refs[:4]
    refs = refs[4:]
    if kind != "down":
        crossing, refs = (crossing, refs[0]), refs[1:]
    refs = refs[chained:]
    if kind != "up":
        beside, refs = refs[:2], refs[2:]
    away_stage, own_stage = refs[:2]
    refs = refs[2:]
    if kind == "down":
        smalls, refs = (refs[-1], *refs[:2]), refs[2:-1]
    former_own, former_got, latter_own, latter_got, turned, parts, sems = refs
    tokens, tall = former_own.shape
    rows = tokens // MICRO
    section = lax.axis_index("section")
    copies = []

    def load(source, target):
        copies.append(pltpu.make_async_copy(source, target, sems.at[len(copies)]))
        copies[-1].start()

    load(formers[0], former_own)
    load(formers[1], former_got)
    load(latter, latter_own)
    if kind == "down":
        load(crossing, latter_got)
    else:
        load(crossing[0], latter_got.at[slot_rows(1 - section, rows)])
        load(crossing[1], latter_got.at[slot_rows(section, rows)])
    if kind == "down":
        gather_small(*beside, *smalls)
    copies[0].wait()
    turn(turned, 0, former_own)
    copies[1].wait()
    turn(turned, tokens, former_got)
    for copy in copies[2:]:
        copy.wait()
    height = parts.shape[1]
    for group in range(turned.shape[0] // height // 2):
        for which, spans in enumerate(parting(names, axis, 2 * height)):
            inner = height // len(spans)
            block = turned.at[pl.ds(group * 2 * height, 2 * height)]
            for number, rows_here in enumerate(spans):
                parts[which, number * inner : (number + 1) * inner] = block[rows_here]
        if kind == "mixed":
            edge = 3 * latter_own.shape[1] // 4
            sections = column_tiles(edge, 3 * PAIR) if group == 0 else [slice(edge, latter_own.shape[1])]
        elif kind == "up":
            sections = column_tiles(latter_own.shape[1], 4 * PAIR)
        else:
            sections = [slice(None)]
        for t in sections:
            for which, stage in ((0, away_stage), (1, own_stage)):
                total = product(parts[which, :, :tokens], latter_own[:, t])
                total = total + product(parts[which, :, tokens:], latter_got[:, t])
                stage[:height, t] = total.astype(stage.dtype)
    if kind == "mixed":
        small = beside[0][...] + beside[1][...]
        mine = side(axis)
        for number in range(small.shape[0] // 2):
            for stage, half in ((away_stage, 1 - mine), (own_stage, mine)):
                first = 4 * (number // 2) + number % 2
                row = jnp.where(half == 0, small[first : first + 1], small[first + 2 : first + 3])
                at = height + number * SPARE
                stage[at : at + SPARE] = jnp.broadcast_to(row, (SPARE, row.shape[1])).astype(stage.dtype)


def weight_gradient(kind, names, axis, formers, latters, after, beside=()):
    tokens, tall = formers[0].shape
    wide = latters[0].shape[1]
    height = (tall // 2 if kind == "mixed" else tall) // 2
    args = [in_hbm(formers[0]), formers[1], latters[0] if kind == "down" else in_hbm(latters[0]), *latters[1:]]
    args += after
    in_specs = [ANY] * len(args) + [VMEM] * len(beside)
    args += [in_vmem(b) for b in beside]
    low, full = jnp.bfloat16, jnp.float32
    stacked = height + (SPARE * 4 if kind == "mixed" else 0)
    out_shape = [pltpu.VMEM((stacked, wide), low), pltpu.VMEM((stacked, wide), full)]
    scratch = [
        pltpu.VMEM((tokens, tall), low),
        pltpu.VMEM((tokens, tall), low),
        pltpu.VMEM((tokens, wide), low),
        pltpu.VMEM((tokens, wide), low),
        pltpu.VMEM((tall, 2 * tokens), low),
        pltpu.VMEM((2, height, 2 * tokens), low),
        pltpu.SemaphoreType.DMA((5,)),
    ]
    if kind == "down":
        row = 2 * beside[0].shape[1]
        out_shape += [pltpu.VMEM((CORE_CHIPS // 2, row), full)] * 2
        scratch.append(pltpu.VMEM((CORE_CHIPS, row), full))
    return pl.pallas_call(
        functools.partial(gradient_kernel, kind=kind, names=names, axis=axis, chained=len(after)),
        in_specs=in_specs,
        out_specs=[VMEM] * len(out_shape),
        out_shape=out_shape,
        scratch_shapes=scratch,
        compiler_params=pltpu.CompilerParams(vmem_limit_bytes=24 * MIB),
        cost_estimate=LONG,
        name=kind + "_gradient",
    )(*args)


def fold_kernel(own, got, *refs, names, axis, spare):
    away_out, own_out = refs[-2:]
    rows = own.shape[0] - spare
    height = rows // 2
    for spans, target in zip(parting(names, axis, rows), (away_out, own_out)):
        inner = height // len(spans)
        for number, place in enumerate(spans):
            total = own[place] + got[place].astype(jnp.float32)
            target[number * inner : (number + 1) * inner] = total.astype(target.dtype)
    if not spare:
        return
    kept = away_out.shape[0] - height
    if not kept:
        place = pl.ds(rows, own_out.shape[0] - height)
        own_out[height:] = own[place] + got[place].astype(jnp.float32)
        return
    mine = side(axis)
    for half, target in ((1 - mine, away_out), (mine, own_out)):
        for number in range(kept // SPARE):
            place = pl.ds(pl.multiple_of(rows + (2 * number + half) * SPARE, SPARE), SPARE)
            total = own[place] + got[place].astype(jnp.float32)
            target[height + number * SPARE : height + (number + 1) * SPARE] = total.astype(target.dtype)


def fold(parted, axis, names, following, after, spare=0, kept=0):
    away, own = parted
    got = exchange(away, axis)
    rows, wide = own.shape
    height = (rows - spare) // 2
    own_height = height + (kept or min(spare, 8))
    return pl.pallas_call(
        functools.partial(fold_kernel, names=names, axis=following, spare=spare),
        in_specs=[VMEM, VMEM, ANY],
        out_specs=[VMEM, VMEM],
        out_shape=[pltpu.VMEM((height + kept, wide), jnp.bfloat16), pltpu.VMEM((own_height, wide), jnp.float32)],
        compiler_params=pltpu.CompilerParams(vmem_limit_bytes=8 * MIB),
        cost_estimate=SHORT,
        name="fold",
    )(in_vmem(own), in_vmem(got), after)


def total_kernel(own, got, total):
    total[...] = own[...] + got[...].astype(jnp.float32)


def sides_kernel(own, got, *outs, axis):
    mine = side(axis)
    rows = got.shape[0]
    for source, half in ((own, mine), (got, 1 - mine)):
        done = 0
        for out in outs[:2]:
            wide = out.shape[1] // 2 if out.shape[1] % 2 == 0 else (out.shape[1] + 1) // 2
            block = source[:rows, done : done + wide].astype(jnp.float32)
            if out.shape[1] % 2 == 0:
                out[:, pl.ds(pl.multiple_of(half * wide, PAIR), wide)] = block
            else:

                @pl.when(half == 0)
                def _():
                    out[:, :wide] = block

                @pl.when(half != 0)
                def _():
                    out[:, wide:] = block[:, : wide - 1]

            done += wide


def last_kernel(own, got, *outs, axis):
    sides_kernel(own, got, *outs[:2], axis=axis)
    if len(outs) > 2:
        attn, mlp, seq = outs[2:]
        count = attn.shape[1]
        row = own[got.shape[0] : got.shape[0] + 1]
        attn[...] = row[:, :count]
        mlp[...] = row[:, PAIR : PAIR + count]
        for number in range(seq.shape[0]):
            at = (2 + number) * PAIR
            seq[number : number + 1] = row[:, at : at + seq.shape[1]]


def finish(parted, axis, shapes):
    away, own = parted
    return pl.pallas_call(
        functools.partial(last_kernel, axis=axis),
        in_specs=[VMEM, VMEM],
        out_specs=[VMEM] * len(shapes),
        out_shape=[shaped(shape, jnp.float32) for shape in shapes],
        compiler_params=pltpu.CompilerParams(vmem_limit_bytes=8 * MIB),
        cost_estimate=SHORT,
        name="finish",
    )(in_vmem(own), in_vmem(exchange(away, axis)))


def scattered(down, up, mixed, seq_count):
    down = fold(down, "y", "vx", "x", mixed[1])
    up = fold(up, "x", "vwy", "w", down[1])
    mixed = fold(mixed, "w", "vyx", "y", up[1], 4 * SPARE, 2 * SPARE)
    down = fold(down, "x", "v", "v", mixed[1])
    up = fold(up, "w", "vy", "v", down[1])
    mixed = fold(mixed, "y", "vx", "v", up[1], 2 * SPARE, SPARE)
    away, own = down
    down_part = pl.pallas_call(
        total_kernel,
        in_specs=[VMEM, VMEM],
        out_specs=VMEM,
        out_shape=shaped(own.shape, jnp.float32),
        compiler_params=pltpu.CompilerParams(vmem_limit_bytes=8 * MIB),
        cost_estimate=SHORT,
        name="total",
    )(in_vmem(own), in_vmem(exchange(away, "v")))
    up = fold(up, "v", "y", "y", mixed[1])
    mixed = fold(mixed, "v", "x", "x", up[1], SPARE)
    rows, wide = up[0].shape
    (up_part,) = finish(up, "y", [(rows, 2 * wide)])
    width = wide // 2
    shapes = [(rows, 3 * width), (rows, width - 1), (1, rows), (1, rows), (seq_count, 2)]
    return (down_part, up_part, *finish(mixed, "x", shapes))


def shards(
    stream_in,
    cotangent,
    qkv_weight,
    out_weight,
    up_weight,
    down_weight,
    attn_gain,
    mlp_gain,
    seq_lengths,
    seq_slot,
):
    section = lax.axis_index("section")
    chips = lax.axis_size("dp")
    compressed = stream_in.shape[1]
    weights = (qkv_weight[0], out_weight[0], up_weight[0], down_weight[0])
    inputs = (seq_lengths, seq_slot, attn_gain, mlp_gain, stream_in)

    received = stored = bias = None
    for moment in range(MICRO + 1):
        leaving, stored, more = forward_layer(moment, inputs, received, weights, bias, stored)
        if moment == 0:
            weights, bias, bias_turned, seq_sums = more[:5], more[5], more[6], more[7]
        if moment < MICRO:
            received = shifted(leaving, "section", 1)
    entering, stream_out, packed, log_total, normed_mlp, slope, stat = stored[:7]
    lifted_mixed, lifted_mlp, active_own, active_away = stored[7:]
    split = chips == CORE_CHIPS
    if split:
        mixed_got = exchange(lifted_mixed, "x")
        lifted_got = exchange(lifted_mlp, "y")
        active_got = exchange(active_away, "w")

    kept = (entering, packed, log_total, normed_mlp, stat, slope)
    received = given = None
    pieces = []
    for moment in range(MICRO + 1):
        leaving, *outs = backward_layer(
            moment,
            cotangent,
            received,
            weights,
            bias_turned,
            kept,
            given,
            (seq_lengths, seq_slot, seq_sums),
            [(), (lifted_got,), (mixed_got,)][moment] if split else (),
        )
        if moment != 1:
            seq_sums = outs[7]
        pieces.append(outs[5:7])
        if moment == 0:
            given = outs[:5]
        elif moment == 1:
            given = outs[:5] + pieces[0]
        if moment < MICRO:
            received = shifted(leaving, "section", -1)
        if split and moment == 1:
            hidden_got = [exchange(pieces[1][0], "y")]
            packed_got = [exchange(pieces[1][1], "x")]
            incoming_got = turned_over(outs[7], "w")
    incoming, stream_grad, gain_parts, hidden_own, packed_own = outs[:5]

    if split:
        hidden_got.append(exchange(pieces[2][0], "y"))
        packed_got.append(exchange(pieces[2][1], "x"))
        early = (hidden_got[0], packed_got[0])
        down = weight_gradient(
            "down", "vyx", "y", (active_own, active_got), (incoming, incoming_got), early, (gain_parts, seq_sums)
        )
        small = (down[3], exchange(down[2], "x"))
        up = weight_gradient("up", "vwyx", "x", (lifted_mlp, lifted_got), (hidden_own, *hidden_got), (down[1],))
        mixed = weight_gradient(
            "mixed", "vwyx", "w", (lifted_mixed, mixed_got), (packed_own, *packed_got), (up[1],), small
        )
        down_part, up_part, qkv_part, out_part, attn_part, mlp_part, seq_part = scattered(
            down[:2], up, mixed, seq_lengths.shape[0] // chips
        )
    else:
        gains = jnp.sum(gain_parts.reshape(MICRO, 8, -1)[:, :2], axis=0)
        seq_terms = seq_sums[: seq_lengths.shape[0], :2]
        small = jnp.concatenate(
            [gains[0].reshape(chips, -1), gains[1].reshape(chips, -1), seq_terms.reshape(chips, -1)], axis=1
        )
        small = lax.psum_scatter(small, "dp", scatter_dimension=0, tiled=True)
        count = gains.shape[1] // chips
        attn_part, mlp_part = small[:, :count], small[:, count : 2 * count]
        seq_part = small[:, 2 * count :].reshape(-1, 2)
        width = compressed + 1
        joined = []
        for number, own in ((0, hidden_own), (1, packed_own)):
            other = [jnp.where(section == 0, pieces[2 - k][number], pieces[1 + k][number]) for k in (0, 1)]
            joined.append((own, jnp.concatenate(other, axis=0)))
        edge = 3 * width // 2
        d_hidden = jnp.concatenate(joined[0], axis=1)
        d_packed = jnp.concatenate([part[:, :edge] for part in joined[1]], axis=1)
        d_branch = jnp.concatenate([part[:, edge:] for part in joined[1]], axis=1)[:, :compressed]
        active = jnp.concatenate(
            [part[:, t] for t in column_tiles(active_own.shape[1], width) for part in (active_own, active_away)],
            axis=1,
        )
        pairs = (
            (active, incoming),
            (lifted_mlp, d_hidden),
            (lifted_mixed[:, width:], d_branch),
            (lifted_mixed[:, :width], d_packed),
        )
        down_part, up_part, out_part, qkv_part = (
            lax.psum_scatter(rows_product(a, b), "dp", scatter_dimension=0, tiled=True) for a, b in pairs
        )
    return (
        stream_out[None],
        stream_grad[None],
        qkv_part[None],
        out_part[None],
        up_part[None],
        down_part[None],
        attn_part,
        mlp_part,
        seq_part[None],
    )


def solution(mesh):
    placed = (
        P("dp", None),
        P("dp", None),
        P("section", None, None),
        P("section", None, None),
        P("section", None, None),
        P("section", None, None),
        P("section", None),
        P("section", None),
        P(),
        P(),
    )
    return jax.shard_map(
        shards,
        mesh=mesh,
        in_specs=placed,
        out_specs=(
            P("section", "dp", None),
            P("section", "dp", None),
            P("section", "dp", None),
            P("section", "dp", None),
            P("section", "dp", None),
            P("section", "dp", None),
            P("section", "dp"),
            P("section", "dp"),
            P("section", "dp", None),
        ),
        check_vma=False,
    )
```

```python
import functools

import jax
import jax.numpy as jnp
from jax import lax
from jax.experimental import pallas as pl
from jax.experimental.pallas import tpu as pltpu
from jax.sharding import PartitionSpec as P

HD = 64
MICRO = 2
PAIR = 2 * HD
SCALE = HD ** (-0.5)
LSE_ROWS = 16
GELU_A = 0.7978845608028654
GELU_B = 0.044715
CORE_CHIPS = 16

epsilon = 1e-05
SPARE = 16

VMEM = pl.BlockSpec(memory_space=pltpu.VMEM)
ANY = pl.BlockSpec(memory_space=pl.ANY)
SMEM = pl.BlockSpec(memory_space=pltpu.SMEM)
HBM = pl.BlockSpec(memory_space=pltpu.HBM)
MIB = 2**20
PLAN = {'F1': 20000, 'F2': 1, 'B0': 8000, 'B1': 1000, 'B2': 300, 'down': 8000, 'up': 8000, 'mixed': 300, 'd1': 1000, 'u1': 300, 'm1': 3000, 'd2': 300, 'u2': 300, 'm2': 1000, 'd3': 20000, 'u3': 1, 'm3': 8000, 'u4': 3000, 'm4': 20000}
ORDERS = {"down": "yxv", "up": "xwv", "mixed": "wyv"}
STEPS = "d1 u1 d2 m1 u2 m2 d3 u3 m3 u4 m4"
CHAINED = False
EARLY = {'B1': 'y x0', 'B2': 'x1 h0', 'down': 'p0 h1', 'up': ''}


def told(name):
    return pl.CostEstimate(flops=PLAN.get(name, 8000) * 10**6, bytes_accessed=10**4, transcendentals=0)


epsilon = 1e-05
SPARE = 16

VMEM = pl.BlockSpec(memory_space=pltpu.VMEM)
ANY = pl.BlockSpec(memory_space=pl.ANY)
SMEM = pl.BlockSpec(memory_space=pltpu.SMEM)
HBM = pl.BlockSpec(memory_space=pltpu.HBM)
MIB = 2**20
BRIEF = pl.CostEstimate(flops=10**6, bytes_accessed=10**4, transcendentals=0)
LONG = pl.CostEstimate(flops=8 * 10**9, bytes_accessed=10**4, transcendentals=0)
SHORT = pl.CostEstimate(flops=10**9, bytes_accessed=10**4, transcendentals=0)
KERNEL_VMEM = 30 * MIB


def shaped(shape, dtype):
    return jax.ShapeDtypeStruct(shape, dtype)


def shifted(block, axis, distance):
    devices = range(lax.axis_size(axis))
    route = [(i - distance, i) for i in devices if i - distance in devices]
    return lax.ppermute(block, axis, route)


def product(former, latter):
    return jnp.dot(former, latter, preferred_element_type=jnp.float32)


def rows_product(former, latter):
    return lax.dot_general(
        former, latter, (((0,), (0,)), ((), ())), preferred_element_type=jnp.float32
    )


def against_transposed(former, latter):
    return lax.dot_general(
        former, latter, (((1,), (1,)), ((), ())), preferred_element_type=jnp.float32
    )


def centered_norm(stream):
    row_sum = jnp.sum(stream, axis=1, keepdims=True)
    decompressed = jnp.concatenate([stream, -row_sum], axis=1)
    mean_sq = jnp.mean(decompressed * decompressed, axis=1, keepdims=True)
    factor = lax.rsqrt(mean_sq + epsilon)
    return (decompressed * factor, factor, mean_sq)


def centered_norm_back(d_lifted, normed, factor, gain):
    d_normed = d_lifted * gain
    d_gain = jnp.sum(d_lifted * normed, axis=0, keepdims=True)
    d_whole = factor * (d_normed - normed * jnp.mean(d_normed * normed, axis=1, keepdims=True))
    last = d_whole.shape[1] - 1
    return (d_whole[:, :last] - d_whole[:, last:], d_gain)


def column_tiles(whole, width):
    return [slice(j * width, (j + 1) * width) for j in range(whole // width)]


def in_vmem(array):
    return pltpu.with_memory_space_constraint(array, pltpu.VMEM)


def in_hbm(array):
    return pltpu.with_memory_space_constraint(array, pltpu.HBM)


STRIDES = {"v": 8, "w": 4, "y": 2, "x": 1}


def side(axis):
    if lax.axis_size("dp") != CORE_CHIPS:
        return jnp.int32(0)
    return lax.rem(lax.div(lax.axis_index("dp"), jnp.int32(STRIDES[axis])), jnp.int32(2))


def span(start, size):
    return pl.ds(pl.multiple_of(start * size, size), size)


def slot_rows(slot, count):
    return pl.ds(pl.multiple_of(slot * count, count), count)


def seq_sums_shape(lengths):
    return (-(-lengths.shape[0] // 8) * 8, PAIR)


def add_sequences(owners, stat, seq_sums):
    rows = owners.shape[1]
    number = lax.broadcasted_iota(jnp.int32, (seq_sums.shape[0], rows), 0)
    for index in range(MICRO):
        owned = jnp.where(owners[8 * index : 8 * index + 1] == number, 1.0, 0.0)
        count = jnp.sum(owned, axis=1, keepdims=True)
        total = jnp.dot(
            owned,
            stat[index * rows : (index + 1) * rows],
            preferred_element_type=jnp.float32,
            precision=lax.Precision.HIGHEST,
        )
        seq_sums[...] += total / jnp.maximum(count, 1.0)


def write_masks(lengths, slots, first_slot, bias, bias_turned, owners):
    rows = bias.shape[1]
    place = lax.broadcasted_iota(jnp.int32, (8, rows), 1)

    def step(number, carry):
        nexts, begins, holders = [], [], []
        for index, (start, begin, holder) in enumerate(zip(*carry)):
            member = slots[number] == first_slot + index
            reached = place >= jnp.where(member, start, rows)
            begins.append(jnp.where(reached, start, begin))
            holders.append(jnp.where(reached, number, holder))
            nexts.append(start + jnp.where(member, lengths[number], 0))
        return tuple(nexts), tuple(begins), tuple(holders)

    none = jnp.zeros((8, rows), jnp.int32)
    carry = ((jnp.int32(0),) * MICRO, (none,) * MICRO, (none,) * MICRO)
    _, begins, holders = lax.fori_loop(0, lengths.shape[0], step, carry)
    for index, holder in enumerate(holders):
        owners[8 * index : 8 * (index + 1)] = holder
    key = lax.broadcasted_iota(jnp.int32, (rows, rows), 0)
    row = lax.broadcasted_iota(jnp.int32, (rows, rows), 1)
    for index, begin in enumerate(begins):
        turned = jnp.where((key <= row) & (key >= begin[:1]), 0.0, -1e30)
        bias_turned[index * rows : (index + 1) * rows] = turned.astype(bias_turned.dtype)
        bias[index * rows : (index + 1) * rows] = turned.T.astype(bias.dtype)


def forward_kernel(*refs, moment):
    if moment == 0:
        lengths_h, slots_h, attn_h, mlp_h, stream_in, cotangent, qkv_h, out_h, up_h, down_h = refs[:10]
        refs = refs[10:]
    else:
        received, qkv_w, out_w, up_w, down_w, norm_gains, bias = refs[:7]
        refs = refs[7 + 11 :]
    leaving, entering, result, packed, log_total, normed_mlp, slope, stat = refs[:8]
    sends, refs = refs[8:11], refs[11:]
    mixed_sends, refs = refs[: 1 + moment % 2], refs[1 + moment % 2 :]
    lifted_mixed, lifted_mlp, active_own, active_away, send_sems = refs[-5:]
    refs = refs[:-5]
    section = lax.axis_index("section")
    slot = moment - section
    rows, compressed = leaving.shape
    width = compressed + 1
    thirds = column_tiles(3 * width, width)
    first_half, second_half = column_tiles(2 * width, width)
    tiles = []
    for away in (1, 0):
        for number in range(slope.shape[1] // (2 * width)):
            half = side("w") if away == 0 else 1 - side("w")
            tiles.append((number, away, span(2 * number + half, width)))
    waits = {}
    if moment == 0:
        qkv_w, out_w, up_w, down_w, norm_gains, bias, bias_turned, seq_sums, owners, incoming, lengths, slots, sems = refs

        def load(name, source, target):
            copy = pltpu.make_async_copy(source, target, sems.at[len(waits)])
            waits[name] = copy
            copy.start()

        load("lengths", lengths_h, lengths)
        load("slots", slots_h, slots)
        load("attn", attn_h, norm_gains.at[pl.ds(0, 1)])
        load("mlp", mlp_h, norm_gains.at[pl.ds(8, 1)])
        load("entering", stream_in, entering)
        for t in thirds:
            load(("qkv", t.start), qkv_h.at[:, t], qkv_w.at[:, t])
        load("out", out_h, out_w)
        for number, away, t in tiles:
            load(("up", number, away), up_h.at[:, t], up_w.at[:, t])
            load(("down", number, away), down_h.at[t], down_w.at[t])
        load("cotangent", cotangent, incoming)
        seq_sums[...] = jnp.zeros_like(seq_sums)
        waits.pop("lengths").wait()
        waits.pop("slots").wait()
        write_masks(lengths, slots, lax.axis_index("dp") * MICRO, bias, bias_turned, owners)

    def arrive(*name):
        if moment == 0:
            waits[name if len(name) > 1 else name[0]].wait()

    def work():
        here = slot_rows(slot, rows)
        if moment == 0:
            arrive("entering")
            arrive("attn")
            arrive("mlp")
        else:

            @pl.when(section != 0)
            def _():
                entering[here] = received[...]

        copies = []

        def send(number, block):
            copy = pltpu.make_async_copy(block, sends[number].at[here], send_sems.at[number])
            copy.start()
            copies.append(copy)

        def send_mixed():
            for number, target in enumerate(mixed_sends):
                copy = pltpu.make_async_copy(lifted_mixed, target, send_sems.at[3])
                if len(mixed_sends) == 1:
                    copy.start()
                else:
                    pl.when(slot == number)(copy.start)
            copies.append(copy)

        base = entering[here].astype(jnp.float32)
        normed, _, square_attn = centered_norm(base)
        lifted_mixed[:, first_half] = (normed * norm_gains[0:1]).astype(jnp.bfloat16)
        for t in thirds:
            arrive("qkv", t.start)
            packed[here, t] = product(lifted_mixed[:, first_half], qkv_w[:, t]).astype(jnp.bfloat16)
        lane = lax.broadcasted_iota(jnp.int32, (rows, PAIR), 1)
        zero = jnp.zeros((rows, PAIR), jnp.bfloat16)
        totals = jnp.zeros((rows, PAIR), jnp.float32)
        for pair in range(width // PAIR):
            at = pair * PAIR
            queries = packed[here, at : at + PAIR] * jnp.asarray(SCALE, jnp.bfloat16)
            key_part = packed[here, width + at : width + at + PAIR]
            values = packed[here, 2 * width + at : 2 * width + at + PAIR]
            joined = None
            for half, keep in enumerate((lane < HD, lane >= HD)):
                scores = against_transposed(jnp.where(keep, queries, zero), key_part) + bias[here].astype(jnp.float32)
                peak = jnp.max(scores, axis=1, keepdims=True)
                exponent = jnp.exp(scores - peak)
                total = jnp.sum(exponent, axis=1, keepdims=True)
                part = product(exponent.astype(jnp.bfloat16), jnp.where(keep, values, zero))
                share = 1.0 / total
                scale = share if half == 0 else jnp.where(keep, share, scale)
                joined = part if joined is None else joined + part
                totals = jnp.where(lane == 2 * pair + half, peak + jnp.log(total), totals)
            lifted_mixed[:, width + at : width + at + PAIR] = (joined * scale).astype(jnp.bfloat16)
        send_mixed()
        log_total[slot_rows(slot, LSE_ROWS)] = totals.T[:LSE_ROWS]
        arrive("out")
        middle = base + product(lifted_mixed[:, second_half], out_w[...])
        normed, factor, square_mlp = centered_norm(middle)
        normed_mlp[here] = normed
        lifted_mlp[...] = (normed * norm_gains[8:9]).astype(jnp.bfloat16)
        send(0, lifted_mlp)
        stat[here] = jnp.where(lane == 0, square_attn, jnp.where(lane == 1, square_mlp, factor))
        total = middle
        for number, away, t in tiles:
            arrive("up", number, away)
            hidden = product(lifted_mlp[...], up_w[:, t])
            squared = hidden * hidden
            bend = jnp.tanh(hidden * (GELU_A + GELU_A * GELU_B * squared))
            gate = 0.5 + 0.5 * bend
            value = hidden * gate
            slope[here, t] = (
                gate + value * (1.0 - bend) * (GELU_A + 3 * GELU_A * GELU_B * squared)
            ).astype(jnp.bfloat16)
            active = value.astype(jnp.bfloat16)
            place = slice(number * width, (number + 1) * width)
            if away:
                active_away[:, place] = active
            else:
                active_own[:, place] = active
            arrive("down", number, away)
            total = total + product(active, down_w[t])
            if number + 1 == slope.shape[1] // (2 * width):
                send(1 + away, active_away if away else active_own)
        leaving[...] = total.astype(jnp.bfloat16)
        result[here] = leaving[...]
        for copy in copies:
            copy.wait()
        arrive("cotangent")

    pl.when((slot >= 0) & (slot < MICRO))(work)
    if moment == 0:

        @pl.when(slot != 0)
        def _():
            for copy in waits.values():
                copy.wait()


def forward_layer(moment, inputs, received, weights, bias, stacks):
    if moment == 0:
        lengths, slots, attn_gain, mlp_gain, stream_in, cotangent = inputs
        rows = stream_in.shape[0] // MICRO
        compressed = stream_in.shape[1]
    else:
        rows, compressed = received.shape
    width, inner = weights[2].shape
    low, full = jnp.bfloat16, jnp.float32
    blocks = [
        ((rows, compressed), low),
        ((rows, compressed), low),
        ((rows, 3 * width), low),
        ((LSE_ROWS, rows), full),
        ((rows, width), full),
        ((rows, inner), low),
        ((rows, PAIR), full),
    ]
    sent = (2 * width, width, inner // 2, inner // 2)
    out_shape = [pltpu.VMEM((rows, compressed), low)]
    out_shape += [pltpu.VMEM((MICRO * shape[0], shape[1]), kind) for shape, kind in blocks]
    out_shape += [pltpu.HBM((MICRO * rows, wide), low) for wide in sent[1:]]
    out_shape += [pltpu.HBM((rows, sent[0]), low)] * (1 + moment % 2)
    out_specs = [VMEM] * (1 + len(blocks)) + [HBM] * (len(out_shape) - 1 - len(blocks))
    if moment == 0:
        out_shape += [pltpu.VMEM(w.shape, low) for w in weights]
        out_shape += [pltpu.VMEM((16, width), full)]
        out_shape += [pltpu.VMEM((MICRO * rows, rows), low)] * 2
        out_shape += [pltpu.VMEM(seq_sums_shape(lengths), full)]
        out_shape += [pltpu.VMEM((8 * MICRO, rows), jnp.int32)]
        out_shape += [pltpu.VMEM(cotangent.shape, low)]
        out_specs += [VMEM] * (len(out_shape) - len(out_specs))
        args = [in_hbm(a) for a in (*inputs, *weights)]
        in_specs = [HBM] * len(args)
        aliases = {}
        scratch = [pltpu.SMEM(lengths.shape, jnp.int32)] * 2 + [pltpu.SemaphoreType.DMA((18,))]
    else:
        args = [in_vmem(a) for a in (received, *weights, bias)]
        in_specs = [VMEM] * len(args) + out_specs[1 : 1 + len(stacks)]
        aliases = {7 + i: 1 + i for i in range(len(stacks))}
        args += [in_vmem(s) for s in stacks[:-4]] + [in_hbm(s) for s in stacks[-4:]]
        scratch = []
    outs = pl.pallas_call(
        functools.partial(forward_kernel, moment=moment),
        out_shape=out_shape,
        in_specs=in_specs,
        out_specs=out_specs,
        input_output_aliases=aliases,
        scratch_shapes=scratch
        + [pltpu.VMEM((rows, wide), low) for wide in sent]
        + [pltpu.SemaphoreType.DMA((4,))],
        compiler_params=pltpu.CompilerParams(vmem_limit_bytes=KERNEL_VMEM),
        cost_estimate=told(("F0", "F1", "F2")[moment]),
        name="forward_layer",
    )(*args)
    return outs[0], outs[1:]


def backward_kernel(*refs, moment, ordered):
    first = moment == 0
    if not first:
        received, refs = refs[0], refs[1:]
    qkv_w, out_w, up_w, down_w, norm_gains, bias = refs[:6]
    entering, packed, log_total, normed_mlp, stat, slope = refs[6:12]
    refs = refs[12 + (1, 6, 5)[moment] + ordered :]
    summing = moment != 1
    if summing:
        owners, refs = refs[0], refs[2:]
    leaving, incoming, d_input, gains, hidden_h, packed_h, *sends = refs[:8]
    refs = refs[8:]
    if moment != MICRO:
        crossing, refs = refs[0], refs[1:]
    if summing:
        seq_sums, refs = refs[0], refs[1:]
    d_heads, d_branch, d_packed, hidden_own, hidden_away, packed_own, packed_away, send_sems = refs[:8]
    refs = refs[8:]
    section = lax.axis_index("section")
    slot = MICRO - moment - section
    rows, compressed = leaving.shape
    width = compressed + 1
    tiles = []
    for away in (1, 0):
        half = side("y") if away == 0 else 1 - side("y")
        for number in range(slope.shape[1] // (2 * width)):
            tiles.append((number, away, span(half * (slope.shape[1] // (2 * width)) + number, width)))
    if first:

        @pl.when(section == 0)
        def _():
            pltpu.make_async_copy(incoming, crossing, send_sems.at[4]).start()

    def work():
        here = slot_rows(slot, rows)
        if not first:

            @pl.when(section == 0)
            def _():
                incoming[here] = received[...]

        copies = []

        def send(block, target):
            copy = pltpu.make_async_copy(block, target, send_sems.at[len(copies)])
            copy.start()
            copies.append(copy)

        d_lifted = jnp.zeros((rows, width), jnp.float32)
        for number, away, t in tiles:
            d_active = against_transposed(incoming[here], down_w[t])
            d_hidden = (d_active * slope[here, t].astype(jnp.float32)).astype(jnp.bfloat16)
            place = slice(number * width, (number + 1) * width)
            if away:
                hidden_away[:, place] = d_hidden
            else:
                hidden_own[:, place] = d_hidden
            d_lifted = d_lifted + against_transposed(d_hidden, up_w[:, t])
            if number + 1 == slope.shape[1] // (2 * width):
                if away:
                    send(hidden_away, sends[0])
                else:
                    send(hidden_own, hidden_h.at[here])
        d_norm, mlp_part = centered_norm_back(d_lifted, normed_mlp[here], stat[here, 2:3], norm_gains[8:9])
        d_middle = incoming[here].astype(jnp.float32) + d_norm
        branch = d_middle.astype(jnp.bfloat16)
        d_branch[...] = jnp.concatenate([branch, jnp.zeros((rows, 1), jnp.bfloat16)], axis=1)
        d_heads[...] = against_transposed(branch, out_w[...]).astype(jnp.bfloat16)
        lane = lax.broadcasted_iota(jnp.int32, (rows, PAIR), 1)
        zero = jnp.zeros((rows, PAIR), jnp.bfloat16)
        heads_total = log_total[slot_rows(slot, LSE_ROWS)]
        for pair in range(width // PAIR):
            at = pair * PAIR
            queries = packed[here, at : at + PAIR] * jnp.asarray(SCALE, jnp.bfloat16)
            key_part = packed[here, width + at : width + at + PAIR]
            values = packed[here, 2 * width + at : 2 * width + at + PAIR]
            d_part = d_heads[:, at : at + PAIR]
            sums = None
            for half, keep in enumerate((lane < HD, lane >= HD)):
                own_queries = jnp.where(keep, queries, zero)
                own_keys = jnp.where(keep, key_part, zero)
                own_part = jnp.where(keep, d_part, zero)
                head = 2 * pair + half
                attention = jnp.exp(
                    against_transposed(key_part, own_queries) + bias[here].astype(jnp.float32) - heads_total[head : head + 1, :]
                )
                d_attention = against_transposed(values, own_part)
                d_scores = attention * (d_attention - jnp.sum(attention * d_attention, axis=0, keepdims=True))
                d_scores = d_scores.astype(jnp.bfloat16)
                terms = (
                    rows_product(own_keys, d_scores),
                    product(d_scores, own_queries),
                    product(attention.astype(jnp.bfloat16), own_part),
                )
                sums = terms if sums is None else tuple(a + b for a, b in zip(sums, terms))
            d_packed[:, at : at + PAIR] = (sums[0].T * SCALE).astype(jnp.bfloat16)
            d_packed[:, width + at : width + at + PAIR] = sums[1].astype(jnp.bfloat16)
            d_packed[:, 2 * width + at : 2 * width + at + PAIR] = sums[2].astype(jnp.bfloat16)
        middle, half = 3 * width // 2, width // 2
        mine = side("x")
        packed_own[:, :middle] = d_packed[:, span(mine, middle)]
        packed_own[:, middle:] = d_branch[:, span(mine, half)]
        packed_away[:, :middle] = d_packed[:, span(1 - mine, middle)]
        packed_away[:, middle:] = d_branch[:, span(1 - mine, half)]
        send(packed_away, sends[1])
        send(packed_own, packed_h.at[here])
        d_lifted = jnp.zeros((rows, width), jnp.float32)
        for t in column_tiles(3 * width, width):
            d_lifted = d_lifted + against_transposed(d_packed[:, t], qkv_w[:, t])
        normed, factor, _ = centered_norm(entering[here].astype(jnp.float32))
        d_norm, attn_part = centered_norm_back(d_lifted, normed, factor, norm_gains[0:1])
        leaving[...] = (d_middle + d_norm).astype(jnp.bfloat16)
        d_input[here] = leaving[...]
        if moment == 1:

            @pl.when(section != 0)
            def _():
                pltpu.make_async_copy(d_input, crossing, send_sems.at[4]).start()

        number = lax.broadcasted_iota(jnp.int32, (8, width), 0)
        gains[slot_rows(slot, 8)] = jnp.where(number == 0, attn_part, jnp.where(number == 1, mlp_part, 0.0))
        for copy in copies:
            copy.wait()

    pl.when((slot >= 0) & (slot < MICRO))(work)
    if moment != MICRO:

        @pl.when(section == moment)
        def _():
            pltpu.make_async_copy(d_input, crossing, send_sems.at[4]).wait()

    if summing:

        @pl.when(section != 0 if moment else section == 0)
        def _():
            add_sequences(owners, stat, seq_sums)


def backward_layer(moment, received, weights, bias, stored, stacks, sequences, after=()):
    width, inner = weights[2].shape
    rows = bias.shape[1]
    compressed = width - 1
    low, full = jnp.bfloat16, jnp.float32
    blocks = [
        ((rows, compressed), low),
        ((rows, compressed), low),
        ((8, width), full),
    ]
    out_shape = [pltpu.VMEM((rows, compressed), low)]
    out_shape += [pltpu.VMEM((MICRO * shape[0], shape[1]), kind) for shape, kind in blocks]
    sent = (inner // 2, 2 * width)
    out_shape += [pltpu.HBM((MICRO * rows, wide), low) for wide in sent]
    out_shape += [pltpu.HBM((rows, wide), low) for wide in sent]
    out_specs = [VMEM] * (1 + len(blocks)) + [HBM] * 4
    args = [] if moment == 0 else [in_vmem(received)]
    args += [in_vmem(a) for a in (*weights, bias, *stored)]
    in_specs = [VMEM] * len(args)
    scratch = [pltpu.VMEM((rows, n * width), low) for n in (1, 1, 3)]
    scratch += [pltpu.VMEM((rows, wide), low) for wide in sent for _ in range(2)]
    scratch += [pltpu.SemaphoreType.DMA((5,))]
    given = list(stacks)
    if moment != MICRO:
        out_shape += [pltpu.HBM((MICRO * rows, compressed), low)]
        out_specs += [HBM]
    aliases = {len(args) + i: 1 + i for i in range(min(len(given), 5))}
    if moment == 1:
        aliases[len(args) + 5] = 8
    in_specs += out_specs[1 : 1 + min(len(given), 5)] + [HBM] * (moment == 1)
    args += [in_vmem(s) for s in given[:3]] + [in_hbm(s) for s in given[3:]]
    args += after
    in_specs += [ANY] * len(after)
    if moment != 1:
        owners, seq_sums = sequences
        args += [in_vmem(owners), in_vmem(seq_sums)]
        aliases[len(args) - 1] = len(out_shape)
        in_specs += [VMEM, VMEM]
        out_shape += [pltpu.VMEM(seq_sums.shape, full)]
        out_specs += [VMEM]
    outs = pl.pallas_call(
        functools.partial(backward_kernel, moment=moment, ordered=len(after)),
        out_shape=out_shape,
        in_specs=in_specs,
        out_specs=out_specs,
        input_output_aliases=aliases,
        scratch_shapes=scratch,
        compiler_params=pltpu.CompilerParams(vmem_limit_bytes=KERNEL_VMEM),
        cost_estimate=told(("B0", "B1", "B2")[moment]),
        name="backward_layer",
    )(*args)
    return outs


def exchange(block, axis, section=None):
    size = lax.axis_size("dp")
    if section is None:
        return lax.ppermute(block, "dp", [(i, i ^ STRIDES[axis]) for i in range(size)])
    first = section * size
    return lax.ppermute(block, ("section", "dp"), [(first + i, first + (i ^ STRIDES[axis])) for i in range(size)])


def turned_over(block, axis):
    size = lax.axis_size("dp")
    route = [(k * size + i, (1 - k) * size + (i ^ STRIDES[axis])) for k in (0, 1) for i in range(size)]
    return lax.ppermute(block, ("section", "dp"), route)


def turn(target, column, block):
    rows = block.shape[0]
    for t in column_tiles(block.shape[1], 3 * PAIR):
        target[t, column : column + rows] = block[:, t].T


def parting(names, axis, rows):
    outer = 2 ** names.index(axis)
    inner = rows // (2 * outer)
    mine = side(axis)
    return [
        [pl.ds(pl.multiple_of((2 * number + half) * inner, 16), inner) for number in range(outer)]
        for half in (1 - mine, mine)
    ]


def gather_small(gain_parts, seq_sums, small, away, own):
    chips = small.shape[0]
    small[...] = jnp.zeros_like(small)
    count = gain_parts.shape[1] // chips
    each = -(-seq_sums.shape[0] // chips)
    for kind in (0, 1):
        gain = gain_parts[kind : kind + 1] + gain_parts[8 + kind : 9 + kind]
        for chip in range(chips):
            small[chip : chip + 1, kind * PAIR : kind * PAIR + count] = gain[:, chip * count : (chip + 1) * count]
    for chip in range(chips):
        for number in range(each):
            at = (2 + number) * PAIR
            small[chip : chip + 1, at : at + PAIR] = seq_sums[chip * each + number : chip * each + number + 1]
    mine = side("x")
    for number in range(chips // 2):
        away[number : number + 1] = small[pl.ds(2 * number + 1 - mine, 1)]
        own[number : number + 1] = small[pl.ds(2 * number + mine, 1)]


def gradient_kernel(*refs, kind, names, axis, chained):
    formers, refs = refs[: 4 if kind == "mixed" else 2], refs[4 if kind == "mixed" else 2 :]
    latter, refs = refs[0], refs[1:]
    crossing, refs = refs[: 1 if kind == "down" else 3], refs[1 if kind == "down" else 3 :]
    refs = refs[chained:]
    if kind != "up":
        beside, refs = refs[:2], refs[2:]
    away_stage, own_stage = refs[:2]
    refs = refs[2:]
    if kind == "down":
        smalls, refs = (refs[-1], *refs[:2]), refs[2:-1]
    former_own, former_got, latter_own, latter_got, turned, parts, sems = refs
    tokens, tall = former_own.shape
    rows = tokens // MICRO
    section = lax.axis_index("section")
    copies = []

    def load(source, target):
        copies.append(pltpu.make_async_copy(source, target, sems.at[len(copies)]))
        copies[-1].start()

    if kind == "mixed":
        for number, (source, target) in enumerate(zip(formers, (former_own,) * 2 + (former_got,) * 2)):
            load(source, target.at[slot_rows(number % 2, rows)])
    else:
        load(formers[0], former_own)
        load(formers[1], former_got)
    firsts = len(copies) // 2
    load(latter, latter_own)
    if kind == "down":
        load(crossing[0], latter_got)
    else:
        load(crossing[1], latter_got.at[slot_rows(1 - section, rows)])
        target = latter_got.at[slot_rows(section, rows)]
        for number, source in ((0, crossing[2]), (1, crossing[0])):
            copy = pltpu.make_async_copy(source, target, sems.at[len(copies)])
            pl.when(section == number)(copy.start)
        copies.append(copy)
    if kind == "down":
        gather_small(*beside, *smalls)
    for copy in copies[:firsts]:
        copy.wait()
    turn(turned, 0, former_own)
    for copy in copies[firsts : 2 * firsts]:
        copy.wait()
    turn(turned, tokens, former_got)
    for copy in copies[2 * firsts :]:
        copy.wait()
    height = parts.shape[1]
    for group in range(turned.shape[0] // height // 2):
        for which, spans in enumerate(parting(names, axis, 2 * height)):
            inner = height // len(spans)
            block = turned.at[pl.ds(group * 2 * height, 2 * height)]
            for number, rows_here in enumerate(spans):
                parts[which, number * inner : (number + 1) * inner] = block[rows_here]
        if kind == "mixed":
            edge = 3 * latter_own.shape[1] // 4
            sections = column_tiles(edge, 3 * PAIR) if group == 0 else [slice(edge, latter_own.shape[1])]
        elif kind == "up":
            sections = column_tiles(latter_own.shape[1], 4 * PAIR)
        else:
            sections = [slice(None)]
        for t in sections:
            for which, stage in ((0, away_stage), (1, own_stage)):
                total = product(parts[which, :, :tokens], latter_own[:, t])
                total = total + product(parts[which, :, tokens:], latter_got[:, t])
                stage[:height, t] = total.astype(stage.dtype)
    if kind == "mixed":
        small = beside[0][...] + beside[1][...]
        mine = side(axis)
        for number in range(small.shape[0] // 2):
            for stage, half in ((away_stage, 1 - mine), (own_stage, mine)):
                stride = STRIDES[axis] // 2
                first = number // stride * 2 * stride + number % stride
                row = jnp.where(half == 0, small[first : first + 1], small[first + stride : first + stride + 1])
                at = height + number * SPARE
                stage[at : at + SPARE] = jnp.broadcast_to(row, (SPARE, row.shape[1])).astype(stage.dtype)


def weight_gradient(kind, names, axis, formers, latters, after, beside=()):
    tokens, wide = latters[0].shape
    tall = formers[0].shape[1]
    height = (tall // 2 if kind == "mixed" else tall) // 2
    owned = len(formers) // 2
    args = [*(in_hbm(f) for f in formers[:owned]), *formers[owned:]]
    args += [latters[0] if kind == "down" else in_hbm(latters[0]), *latters[1:]]
    args += after
    in_specs = [ANY] * len(args) + [VMEM] * len(beside)
    args += [in_vmem(b) for b in beside]
    low, full = jnp.bfloat16, jnp.float32
    stacked = height + (SPARE * 4 if kind == "mixed" else 0)
    out_shape = [pltpu.VMEM((stacked, wide), low), pltpu.VMEM((stacked, wide), full)]
    scratch = [
        pltpu.VMEM((tokens, tall), low),
        pltpu.VMEM((tokens, tall), low),
        pltpu.VMEM((tokens, wide), low),
        pltpu.VMEM((tokens, wide), low),
        pltpu.VMEM((tall, 2 * tokens), low),
        pltpu.VMEM((2, height, 2 * tokens), low),
        pltpu.SemaphoreType.DMA((8,)),
    ]
    if kind == "down":
        row = 2 * beside[0].shape[1]
        out_shape += [pltpu.VMEM((CORE_CHIPS // 2, row), full)] * 2
        scratch.append(pltpu.VMEM((CORE_CHIPS, row), full))
    return pl.pallas_call(
        functools.partial(gradient_kernel, kind=kind, names=names, axis=axis, chained=len(after)),
        in_specs=in_specs,
        out_specs=[VMEM] * len(out_shape),
        out_shape=out_shape,
        scratch_shapes=scratch,
        compiler_params=pltpu.CompilerParams(vmem_limit_bytes=24 * MIB),
        cost_estimate=told(kind),
        name=kind + "_gradient",
    )(*args)


def fold_kernel(own, got, *refs, names, axis, spare):
    away_out, own_out = refs[-2:]
    rows = own.shape[0] - spare
    height = rows // 2
    for spans, target in zip(parting(names, axis, rows), (away_out, own_out)):
        inner = height // len(spans)
        for number, place in enumerate(spans):
            total = own[place] + got[place].astype(jnp.float32)
            target[number * inner : (number + 1) * inner] = total.astype(target.dtype)
    if not spare:
        return
    kept = away_out.shape[0] - height
    if not kept:
        place = pl.ds(rows, own_out.shape[0] - height)
        own_out[height:] = own[place] + got[place].astype(jnp.float32)
        return
    mine = side(axis)
    for half, target in ((1 - mine, away_out), (mine, own_out)):
        for number in range(kept // SPARE):
            place = pl.ds(pl.multiple_of(rows + (2 * number + half) * SPARE, SPARE), SPARE)
            total = own[place] + got[place].astype(jnp.float32)
            target[height + number * SPARE : height + (number + 1) * SPARE] = total.astype(target.dtype)


def fold(name, parted, axis, names, following, after, spare=0, kept=0):
    away, own = parted
    got = exchange(away, axis)
    rows, wide = own.shape
    height = (rows - spare) // 2
    own_height = height + (kept or min(spare, 8))
    return pl.pallas_call(
        functools.partial(fold_kernel, names=names, axis=following, spare=spare),
        in_specs=[VMEM, VMEM] + [ANY] * len(after),
        out_specs=[VMEM, VMEM],
        out_shape=[pltpu.VMEM((height + kept, wide), jnp.bfloat16), pltpu.VMEM((own_height, wide), jnp.float32)],
        compiler_params=pltpu.CompilerParams(vmem_limit_bytes=8 * MIB),
        cost_estimate=told(name),
        name="fold",
    )(in_vmem(own), in_vmem(got), *after)


def total_kernel(own, got, total):
    total[...] = own[...] + got[...].astype(jnp.float32)


def sides_kernel(own, got, *outs, axis):
    mine = side(axis)
    rows = got.shape[0]
    for source, half in ((own, mine), (got, 1 - mine)):
        done = 0
        for out in outs[:2]:
            wide = out.shape[1] // 2 if out.shape[1] % 2 == 0 else (out.shape[1] + 1) // 2
            block = source[:rows, done : done + wide].astype(jnp.float32)
            if out.shape[1] % 2 == 0:
                out[:, pl.ds(pl.multiple_of(half * wide, PAIR), wide)] = block
            else:

                @pl.when(half == 0)
                def _():
                    out[:, :wide] = block

                @pl.when(half != 0)
                def _():
                    out[:, wide:] = block[:, : wide - 1]

            done += wide


def last_kernel(own, got, *outs, axis):
    sides_kernel(own, got, *outs[:2], axis=axis)
    if len(outs) > 2:
        attn, mlp, seq = outs[2:]
        count = attn.shape[1]
        row = own[got.shape[0] : got.shape[0] + 1]
        attn[...] = row[:, :count]
        mlp[...] = row[:, PAIR : PAIR + count]
        for number in range(seq.shape[0]):
            at = (2 + number) * PAIR
            seq[number : number + 1] = row[:, at : at + seq.shape[1]]


def finish(name, parted, axis, shapes):
    away, own = parted
    return pl.pallas_call(
        functools.partial(last_kernel, axis=axis),
        in_specs=[VMEM, VMEM],
        out_specs=[VMEM] * len(shapes),
        out_shape=[shaped(shape, jnp.float32) for shape in shapes],
        compiler_params=pltpu.CompilerParams(vmem_limit_bytes=8 * MIB),
        cost_estimate=told(name),
        name="finish",
    )(in_vmem(own), in_vmem(exchange(away, axis)))


def scattered(down, up, mixed, seq_count):
    parts = {"d": down, "u": up, "m": mixed}
    orders = {"d": ORDERS["down"], "u": ORDERS["up"] + "y", "m": ORDERS["mixed"] + "x"}
    names = {"d": "vyx", "u": "vwyx", "m": "vwyx"}
    spares = {"1": (4 * SPARE, 2 * SPARE), "2": (2 * SPARE, SPARE), "3": (SPARE, 0)}
    results = {}
    before = None
    for step in STEPS.split():
        kind, phase = step
        order = orders[kind]
        axis = order[int(phase) - 1]
        names[kind] = names[kind].replace(axis, "")
        away, own = parts[kind]
        rows, wide = own.shape
        if int(phase) < len(order):
            spare = spares[phase] if kind == "m" else (0, 0)
            after = (before,) if CHAINED and before is not None else ()
            parts[kind] = fold(step, parts[kind], axis, names[kind], order[int(phase)], after, *spare)
            before = parts[kind][1]
        elif kind == "d":
            results[kind] = [
                pl.pallas_call(
                    total_kernel,
                    in_specs=[VMEM, VMEM],
                    out_specs=VMEM,
                    out_shape=shaped(own.shape, jnp.float32),
                    compiler_params=pltpu.CompilerParams(vmem_limit_bytes=8 * MIB),
                    cost_estimate=told(step),
                    name="total",
                )(in_vmem(own), in_vmem(exchange(away, axis)))
            ]
        else:
            rows, width = away.shape[0], wide // 2
            shapes = [(rows, 2 * wide)]
            if kind == "m":
                shapes = [(rows, 3 * width), (rows, width - 1), (1, rows), (1, rows), (seq_count, 2)]
            results[kind] = finish(step, parts[kind], axis, shapes)
    return (*results["d"], *results["u"], *results["m"])


def shards(
    stream_in,
    cotangent,
    qkv_weight,
    out_weight,
    up_weight,
    down_weight,
    attn_gain,
    mlp_gain,
    seq_lengths,
    seq_slot,
):
    section = lax.axis_index("section")
    chips = lax.axis_size("dp")
    compressed = stream_in.shape[1]
    weights = (qkv_weight[0], out_weight[0], up_weight[0], down_weight[0])
    inputs = (seq_lengths, seq_slot, attn_gain, mlp_gain, stream_in, cotangent)

    split = chips == CORE_CHIPS
    swapped = {}

    def swap(name, block, axis, section=None):
        if split:
            swapped[name] = exchange(block, axis, section)

    def early(name):
        return tuple(swapped[n] for n in EARLY.get(name, "").split()) if split else ()

    received = stored = bias = None
    mixed = []
    for moment in range(MICRO + 1):
        leaving, outs = forward_layer(moment, inputs, received, weights, bias, stored)
        if moment == 0:
            weights = outs[11:16]
            bias, bias_turned, seq_sums, owners, incoming = outs[16:]
        stored = outs[:11]
        if moment == 1:
            mixed.append(outs[10])
            swap("x0", mixed[0], "x")
            stored = outs[:10] + outs[11:12]
        if moment < MICRO:
            received = shifted(leaving, "section", 1)
    entering, stream_out, packed, log_total, normed_mlp, slope, stat, lifted_mlp, active_own, active_away = stored[:10]
    mixed.append(stored[10])
    swap("x1", mixed[1], "x")
    swap("y", lifted_mlp, "y")
    swap("w", active_away, "w")

    kept = (entering, packed, log_total, normed_mlp, stat, slope)
    received = None
    given = [incoming]
    pieces = []
    for moment in range(MICRO + 1):
        leaving, *outs = backward_layer(
            moment, received, weights, bias_turned, kept, given, (owners, seq_sums), early("B%d" % moment)
        )
        if moment != 1:
            seq_sums = outs[-1]
        given = outs[:5] + ([outs[7]] if moment == 0 else [])
        pieces.append(outs[5:7])
        if moment < MICRO:
            received = shifted(leaving, "section", -1)
        only = (1, None, 0)[moment]
        swap("h%d" % moment, pieces[moment][0], "y", only)
        swap("p%d" % moment, pieces[moment][1], "x", only)
        if split and moment == 1:
            swapped["e"] = turned_over(outs[7], "w")
    incoming, stream_grad, gain_parts, hidden_own, packed_own = outs[:5]

    if split:
        down = weight_gradient(
            "down",
            "vyx",
            ORDERS["down"][0],
            (active_own, swapped["w"]),
            (incoming, swapped["e"]),
            early("down"),
            (gain_parts, seq_sums),
        )
        small = (down[3], exchange(down[2], "x"))
        up = weight_gradient(
            "up",
            "vwyx",
            ORDERS["up"][0],
            (lifted_mlp, swapped["y"]),
            (hidden_own, *(swapped[n] for n in ("h0", "h1", "h2"))),
            (down[1], *early("up")),
        )
        mixed = weight_gradient(
            "mixed",
            "vwyx",
            ORDERS["mixed"][0],
            (*mixed, swapped["x0"], swapped["x1"]),
            (packed_own, *(swapped[n] for n in ("p0", "p1", "p2"))),
            (up[1],),
            small,
        )
        down_part, up_part, qkv_part, out_part, attn_part, mlp_part, seq_part = scattered(
            down[:2], up, mixed, seq_lengths.shape[0] // chips
        )
    else:
        lifted_mixed = jnp.concatenate(mixed, axis=0)
        gains = jnp.sum(gain_parts.reshape(MICRO, 8, -1)[:, :2], axis=0)
        seq_terms = seq_sums[: seq_lengths.shape[0], :2]
        small = jnp.concatenate(
            [gains[0].reshape(chips, -1), gains[1].reshape(chips, -1), seq_terms.reshape(chips, -1)], axis=1
        )
        small = lax.psum_scatter(small, "dp", scatter_dimension=0, tiled=True)
        count = gains.shape[1] // chips
        attn_part, mlp_part = small[:, :count], small[:, count : 2 * count]
        seq_part = small[:, 2 * count :].reshape(-1, 2)
        width = compressed + 1
        joined = []
        for number, own in ((0, hidden_own), (1, packed_own)):
            other = [jnp.where(section == 0, pieces[2 - k][number], pieces[1 - k][number]) for k in (0, 1)]
            joined.append((own, jnp.concatenate(other, axis=0)))
        edge = 3 * width // 2
        d_hidden = jnp.concatenate(joined[0], axis=1)
        d_packed = jnp.concatenate([part[:, :edge] for part in joined[1]], axis=1)
        d_branch = jnp.concatenate([part[:, edge:] for part in joined[1]], axis=1)[:, :compressed]
        active = jnp.concatenate(
            [part[:, t] for t in column_tiles(active_own.shape[1], width) for part in (active_own, active_away)],
            axis=1,
        )
        pairs = (
            (active, incoming),
            (lifted_mlp, d_hidden),
            (lifted_mixed[:, width:], d_branch),
            (lifted_mixed[:, :width], d_packed),
        )
        down_part, up_part, out_part, qkv_part = (
            lax.psum_scatter(rows_product(a, b), "dp", scatter_dimension=0, tiled=True) for a, b in pairs
        )
    return (
        stream_out[None],
        stream_grad[None],
        qkv_part[None],
        out_part[None],
        up_part[None],
        down_part[None],
        attn_part,
        mlp_part,
        seq_part[None],
    )


def solution(mesh):
    placed = (
        P("dp", None),
        P("dp", None),
        P("section", None, None),
        P("section", None, None),
        P("section", None, None),
        P("section", None, None),
        P("section", None),
        P("section", None),
        P(),
        P(),
    )
    return jax.shard_map(
        shards,
        mesh=mesh,
        in_specs=placed,
        out_specs=(
            P("section", "dp", None),
            P("section", "dp", None),
            P("section", "dp", None),
            P("section", "dp", None),
            P("section", "dp", None),
            P("section", "dp", None),
            P("section", "dp"),
            P("section", "dp"),
            P("section", "dp", None),
        ),
        check_vma=False,
    )
```

```python
import functools

import jax
import jax.numpy as jnp
from jax import lax
from jax.experimental import pallas as pl
from jax.experimental.pallas import tpu as pltpu
from jax.sharding import PartitionSpec as P

HD = 64
MICRO = 2
PAIR = 2 * HD
SCALE = HD ** (-0.5)
LSE_ROWS = 16
GELU_A = 0.7978845608028654
GELU_B = 0.044715
CORE_CHIPS = 16

epsilon = 1e-05
SPARE = 16

VMEM = pl.BlockSpec(memory_space=pltpu.VMEM)
ANY = pl.BlockSpec(memory_space=pl.ANY)
SMEM = pl.BlockSpec(memory_space=pltpu.SMEM)
HBM = pl.BlockSpec(memory_space=pltpu.HBM)
MIB = 2**20
PLAN = {'F1': 20000, 'F2': 1, 'B0': 8000, 'B1': 1000, 'B2': 300, 'down': 30000, 'up': 3000, 'mixed': 30000, 'd1': 1, 'u1': 8000, 'm1': 20000, 'd2': 8000, 'u2': 1, 'm2': 1, 'd3': 60000, 'u3': 1000, 'm3': 60000, 'u4': 8000, 'm4': 8000}
ORDERS = {"down": "yxv", "up": "xvw", "mixed": "wyv"}
STEPS = ('d1', 'u1', 'd2', 'm1', 'u2', 'd3', 'm2', 'u3', 'm3', 'u4', 'm4')
CHAINED = False
MIXED_LAST = False
EARLY = {'B1': ('y', 'x0'), 'B2': ('x1', 'h0'), 'down': ('p0', 'h1'), 'up': ('x1',)}


def told(name):
    return pl.CostEstimate(flops=PLAN.get(name, 8000) * 10**6, bytes_accessed=10**4, transcendentals=0)


epsilon = 1e-05
SPARE = 16

VMEM = pl.BlockSpec(memory_space=pltpu.VMEM)
ANY = pl.BlockSpec(memory_space=pl.ANY)
SMEM = pl.BlockSpec(memory_space=pltpu.SMEM)
HBM = pl.BlockSpec(memory_space=pltpu.HBM)
MIB = 2**20
BRIEF = pl.CostEstimate(flops=10**6, bytes_accessed=10**4, transcendentals=0)
LONG = pl.CostEstimate(flops=8 * 10**9, bytes_accessed=10**4, transcendentals=0)
SHORT = pl.CostEstimate(flops=10**9, bytes_accessed=10**4, transcendentals=0)
KERNEL_VMEM = 30 * MIB


def shaped(shape, dtype):
    return jax.ShapeDtypeStruct(shape, dtype)


def shifted(block, axis, distance):
    devices = range(lax.axis_size(axis))
    route = [(i - distance, i) for i in devices if i - distance in devices]
    return lax.ppermute(block, axis, route)


def product(former, latter):
    return jnp.dot(former, latter, preferred_element_type=jnp.float32)


def rows_product(former, latter):
    return lax.dot_general(
        former, latter, (((0,), (0,)), ((), ())), preferred_element_type=jnp.float32
    )


def against_transposed(former, latter):
    return lax.dot_general(
        former, latter, (((1,), (1,)), ((), ())), preferred_element_type=jnp.float32
    )


def centered_norm(stream):
    row_sum = jnp.sum(stream, axis=1, keepdims=True)
    decompressed = jnp.concatenate([stream, -row_sum], axis=1)
    mean_sq = jnp.mean(decompressed * decompressed, axis=1, keepdims=True)
    factor = lax.rsqrt(mean_sq + epsilon)
    return (decompressed * factor, factor, mean_sq)


def centered_norm_back(d_lifted, normed, factor, gain):
    d_normed = d_lifted * gain
    d_gain = jnp.sum(d_lifted * normed, axis=0, keepdims=True)
    d_whole = factor * (d_normed - normed * jnp.mean(d_normed * normed, axis=1, keepdims=True))
    last = d_whole.shape[1] - 1
    return (d_whole[:, :last] - d_whole[:, last:], d_gain)


def column_tiles(whole, width):
    return [slice(j * width, (j + 1) * width) for j in range(whole // width)]


def in_vmem(array):
    return pltpu.with_memory_space_constraint(array, pltpu.VMEM)


def in_hbm(array):
    return pltpu.with_memory_space_constraint(array, pltpu.HBM)


STRIDES = {"v": 8, "w": 4, "y": 2, "x": 1}


def side(axis):
    if lax.axis_size("dp") != CORE_CHIPS:
        return jnp.int32(0)
    return lax.rem(lax.div(lax.axis_index("dp"), jnp.int32(STRIDES[axis])), jnp.int32(2))


def span(start, size):
    return pl.ds(pl.multiple_of(start * size, size), size)


def slot_rows(slot, count):
    return pl.ds(pl.multiple_of(slot * count, count), count)


def seq_sums_shape(lengths):
    return (-(-lengths.shape[0] // 8) * 8, PAIR)


def add_sequences(owners, stat, seq_sums):
    rows = owners.shape[1]
    number = lax.broadcasted_iota(jnp.int32, (seq_sums.shape[0], rows), 0)
    for index in range(MICRO):
        owned = jnp.where(owners[8 * index : 8 * index + 1] == number, 1.0, 0.0)
        count = jnp.sum(owned, axis=1, keepdims=True)
        total = jnp.dot(
            owned,
            stat[index * rows : (index + 1) * rows],
            preferred_element_type=jnp.float32,
            precision=lax.Precision.HIGHEST,
        )
        seq_sums[...] += total / jnp.maximum(count, 1.0)


def write_masks(lengths, slots, first_slot, bias, bias_turned, owners):
    rows = bias.shape[1]
    place = lax.broadcasted_iota(jnp.int32, (8, rows), 1)

    def step(number, carry):
        nexts, begins, holders = [], [], []
        for index, (start, begin, holder) in enumerate(zip(*carry)):
            member = slots[number] == first_slot + index
            reached = place >= jnp.where(member, start, rows)
            begins.append(jnp.where(reached, start, begin))
            holders.append(jnp.where(reached, number, holder))
            nexts.append(start + jnp.where(member, lengths[number], 0))
        return tuple(nexts), tuple(begins), tuple(holders)

    none = jnp.zeros((8, rows), jnp.int32)
    carry = ((jnp.int32(0),) * MICRO, (none,) * MICRO, (none,) * MICRO)
    _, begins, holders = lax.fori_loop(0, lengths.shape[0], step, carry)
    for index, holder in enumerate(holders):
        owners[8 * index : 8 * (index + 1)] = holder
    key = lax.broadcasted_iota(jnp.int32, (rows, rows), 0)
    row = lax.broadcasted_iota(jnp.int32, (rows, rows), 1)
    for index, begin in enumerate(begins):
        turned = jnp.where((key <= row) & (key >= begin[:1]), 0.0, -1e30)
        bias_turned[index * rows : (index + 1) * rows] = turned.astype(bias_turned.dtype)
        bias[index * rows : (index + 1) * rows] = turned.T.astype(bias.dtype)


def forward_kernel(*refs, moment):
    if moment == 0:
        lengths_h, slots_h, attn_h, mlp_h, stream_in, cotangent, qkv_h, out_h, up_h, down_h = refs[:10]
        refs = refs[10:]
    else:
        received, qkv_w, out_w, up_w, down_w, norm_gains, bias = refs[:7]
        refs = refs[7 + 11 :]
    leaving, entering, result, packed, log_total, normed_mlp, slope, stat = refs[:8]
    sends, refs = refs[8:11], refs[11:]
    mixed_sends, refs = refs[: 1 + moment % 2], refs[1 + moment % 2 :]
    lifted_mixed, lifted_mlp, active_own, active_away, send_sems = refs[-5:]
    refs = refs[:-5]
    section = lax.axis_index("section")
    slot = moment - section
    rows, compressed = leaving.shape
    width = compressed + 1
    thirds = column_tiles(3 * width, width)
    first_half, second_half = column_tiles(2 * width, width)
    tiles = []
    for away in (1, 0):
        for number in range(slope.shape[1] // (2 * width)):
            half = side("w") if away == 0 else 1 - side("w")
            tiles.append((number, away, span(2 * number + half, width)))
    waits = {}
    if moment == 0:
        qkv_w, out_w, up_w, down_w, norm_gains, bias, bias_turned, seq_sums, owners, incoming, lengths, slots, sems = refs

        def load(name, source, target):
            copy = pltpu.make_async_copy(source, target, sems.at[len(waits)])
            waits[name] = copy
            copy.start()

        load("lengths", lengths_h, lengths)
        load("slots", slots_h, slots)
        load("attn", attn_h, norm_gains.at[pl.ds(0, 1)])
        load("mlp", mlp_h, norm_gains.at[pl.ds(8, 1)])
        load("entering", stream_in, entering)
        for t in thirds:
            load(("qkv", t.start), qkv_h.at[:, t], qkv_w.at[:, t])
        load("out", out_h, out_w)
        for number, away, t in tiles:
            load(("up", number, away), up_h.at[:, t], up_w.at[:, t])
            load(("down", number, away), down_h.at[t], down_w.at[t])
        load("cotangent", cotangent, incoming)
        seq_sums[...] = jnp.zeros_like(seq_sums)
        waits.pop("lengths").wait()
        waits.pop("slots").wait()
        write_masks(lengths, slots, lax.axis_index("dp") * MICRO, bias, bias_turned, owners)

    def arrive(*name):
        if moment == 0:
            waits[name if len(name) > 1 else name[0]].wait()

    def work():
        here = slot_rows(slot, rows)
        if moment == 0:
            arrive("entering")
            arrive("attn")
            arrive("mlp")
        else:

            @pl.when(section != 0)
            def _():
                entering[here] = received[...]

        copies = []

        def send(number, block):
            copy = pltpu.make_async_copy(block, sends[number].at[here], send_sems.at[number])
            copy.start()
            copies.append(copy)

        def send_mixed():
            for number, target in enumerate(mixed_sends):
                copy = pltpu.make_async_copy(lifted_mixed, target, send_sems.at[3])
                if len(mixed_sends) == 1:
                    copy.start()
                else:
                    pl.when(slot == number)(copy.start)
            copies.append(copy)

        base = entering[here].astype(jnp.float32)
        normed, _, square_attn = centered_norm(base)
        lifted_mixed[:, first_half] = (normed * norm_gains[0:1]).astype(jnp.bfloat16)
        for t in thirds:
            arrive("qkv", t.start)
            packed[here, t] = product(lifted_mixed[:, first_half], qkv_w[:, t]).astype(jnp.bfloat16)
        lane = lax.broadcasted_iota(jnp.int32, (rows, PAIR), 1)
        zero = jnp.zeros((rows, PAIR), jnp.bfloat16)
        totals = jnp.zeros((rows, PAIR), jnp.float32)
        mask = bias[here].astype(jnp.float32)
        for pair in range(width // PAIR):
            at = pair * PAIR
            queries = packed[here, at : at + PAIR] * jnp.asarray(SCALE, jnp.bfloat16)
            key_part = packed[here, width + at : width + at + PAIR]
            values = packed[here, 2 * width + at : 2 * width + at + PAIR]
            low, high = lane < HD, lane >= HD
            both = jnp.concatenate([jnp.where(low, queries, zero), jnp.where(high, queries, zero)], axis=0)
            scores = against_transposed(both, key_part).reshape(2, rows, rows) + mask[None]
            peak = jnp.max(scores, axis=2, keepdims=True)
            exponent = jnp.exp(scores - peak)
            total = jnp.sum(exponent, axis=2, keepdims=True)
            attention = (exponent / total).astype(jnp.bfloat16)
            joined = product(attention[0], jnp.where(low, values, zero)) + product(
                attention[1], jnp.where(high, values, zero)
            )
            lifted_mixed[:, width + at : width + at + PAIR] = joined.astype(jnp.bfloat16)
            level = peak + jnp.log(total)
            totals = jnp.where(lane == 2 * pair, level[0], jnp.where(lane == 2 * pair + 1, level[1], totals))
        send_mixed()
        log_total[slot_rows(slot, LSE_ROWS)] = totals.T[:LSE_ROWS]
        arrive("out")
        middle = base + product(lifted_mixed[:, second_half], out_w[...])
        normed, factor, square_mlp = centered_norm(middle)
        normed_mlp[here] = normed
        lifted_mlp[...] = (normed * norm_gains[8:9]).astype(jnp.bfloat16)
        send(0, lifted_mlp)
        stat[here] = jnp.where(lane == 0, square_attn, jnp.where(lane == 1, square_mlp, factor))
        total = middle
        for number, away, t in tiles:
            arrive("up", number, away)
            hidden = product(lifted_mlp[...], up_w[:, t])
            squared = hidden * hidden
            bend = jnp.tanh(hidden * (GELU_A + GELU_A * GELU_B * squared))
            gate = 0.5 + 0.5 * bend
            value = hidden * gate
            slope[here, t] = (
                gate + value * (1.0 - bend) * (GELU_A + 3 * GELU_A * GELU_B * squared)
            ).astype(jnp.bfloat16)
            active = value.astype(jnp.bfloat16)
            place = slice(number * width, (number + 1) * width)
            if away:
                active_away[:, place] = active
            else:
                active_own[:, place] = active
            arrive("down", number, away)
            total = total + product(active, down_w[t])
            if number + 1 == slope.shape[1] // (2 * width):
                send(1 + away, active_away if away else active_own)
        leaving[...] = total.astype(jnp.bfloat16)
        result[here] = leaving[...]
        for copy in copies:
            copy.wait()
        arrive("cotangent")

    pl.when((slot >= 0) & (slot < MICRO))(work)
    if moment == 0:

        @pl.when(slot != 0)
        def _():
            for copy in waits.values():
                copy.wait()


def forward_layer(moment, inputs, received, weights, bias, stacks):
    if moment == 0:
        lengths, slots, attn_gain, mlp_gain, stream_in, cotangent = inputs
        rows = stream_in.shape[0] // MICRO
        compressed = stream_in.shape[1]
    else:
        rows, compressed = received.shape
    width, inner = weights[2].shape
    low, full = jnp.bfloat16, jnp.float32
    blocks = [
        ((rows, compressed), low),
        ((rows, compressed), low),
        ((rows, 3 * width), low),
        ((LSE_ROWS, rows), full),
        ((rows, width), full),
        ((rows, inner), low),
        ((rows, PAIR), full),
    ]
    sent = (2 * width, width, inner // 2, inner // 2)
    out_shape = [pltpu.VMEM((rows, compressed), low)]
    out_shape += [pltpu.VMEM((MICRO * shape[0], shape[1]), kind) for shape, kind in blocks]
    out_shape += [pltpu.HBM((MICRO * rows, wide), low) for wide in sent[1:]]
    out_shape += [pltpu.HBM((rows, sent[0]), low)] * (1 + moment % 2)
    out_specs = [VMEM] * (1 + len(blocks)) + [HBM] * (len(out_shape) - 1 - len(blocks))
    if moment == 0:
        out_shape += [pltpu.VMEM(w.shape, low) for w in weights]
        out_shape += [pltpu.VMEM((16, width), full)]
        out_shape += [pltpu.VMEM((MICRO * rows, rows), low)] * 2
        out_shape += [pltpu.VMEM(seq_sums_shape(lengths), full)]
        out_shape += [pltpu.VMEM((8 * MICRO, rows), jnp.int32)]
        out_shape += [pltpu.VMEM(cotangent.shape, low)]
        out_specs += [VMEM] * (len(out_shape) - len(out_specs))
        args = [in_hbm(a) for a in (*inputs, *weights)]
        in_specs = [HBM] * len(args)
        aliases = {}
        scratch = [pltpu.SMEM(lengths.shape, jnp.int32)] * 2 + [pltpu.SemaphoreType.DMA((18,))]
    else:
        args = [in_vmem(a) for a in (received, *weights, bias)]
        in_specs = [VMEM] * len(args) + out_specs[1 : 1 + len(stacks)]
        aliases = {7 + i: 1 + i for i in range(len(stacks))}
        args += [in_vmem(s) for s in stacks[:-4]] + [in_hbm(s) for s in stacks[-4:]]
        scratch = []
    outs = pl.pallas_call(
        functools.partial(forward_kernel, moment=moment),
        out_shape=out_shape,
        in_specs=in_specs,
        out_specs=out_specs,
        input_output_aliases=aliases,
        scratch_shapes=scratch
        + [pltpu.VMEM((rows, wide), low) for wide in sent]
        + [pltpu.SemaphoreType.DMA((4,))],
        compiler_params=pltpu.CompilerParams(vmem_limit_bytes=KERNEL_VMEM),
        cost_estimate=told(("F0", "F1", "F2")[moment]),
        name="forward_layer",
    )(*args)
    return outs[0], outs[1:]


def backward_kernel(*refs, moment, ordered):
    first = moment == 0
    if not first:
        received, refs = refs[0], refs[1:]
    qkv_w, out_w, up_w, down_w, norm_gains, bias = refs[:6]
    entering, packed, log_total, normed_mlp, stat, slope = refs[6:12]
    refs = refs[12 + (1, 6, 5)[moment] + ordered :]
    summing = moment != 1
    if summing:
        owners, refs = refs[0], refs[2:]
    leaving, incoming, d_input, gains, hidden_h, packed_h, *sends = refs[:8]
    refs = refs[8:]
    if moment != MICRO:
        crossing, refs = refs[0], refs[1:]
    if summing:
        seq_sums, refs = refs[0], refs[1:]
    d_heads, d_branch, d_packed, hidden_own, hidden_away, packed_own, packed_away, send_sems = refs[:8]
    refs = refs[8:]
    section = lax.axis_index("section")
    slot = MICRO - moment - section
    rows, compressed = leaving.shape
    width = compressed + 1
    tiles = []
    for away in (1, 0):
        half = side("y") if away == 0 else 1 - side("y")
        for number in range(slope.shape[1] // (2 * width)):
            tiles.append((number, away, span(half * (slope.shape[1] // (2 * width)) + number, width)))
    if first:

        @pl.when(section == 0)
        def _():
            pltpu.make_async_copy(incoming, crossing, send_sems.at[4]).start()

    def work():
        here = slot_rows(slot, rows)
        if not first:

            @pl.when(section == 0)
            def _():
                incoming[here] = received[...]

        copies = []

        def send(block, target):
            copy = pltpu.make_async_copy(block, target, send_sems.at[len(copies)])
            copy.start()
            copies.append(copy)

        d_lifted = jnp.zeros((rows, width), jnp.float32)
        for number, away, t in tiles:
            d_active = against_transposed(incoming[here], down_w[t])
            d_hidden = (d_active * slope[here, t].astype(jnp.float32)).astype(jnp.bfloat16)
            place = slice(number * width, (number + 1) * width)
            if away:
                hidden_away[:, place] = d_hidden
            else:
                hidden_own[:, place] = d_hidden
            d_lifted = d_lifted + against_transposed(d_hidden, up_w[:, t])
            if number + 1 == slope.shape[1] // (2 * width):
                if away:
                    send(hidden_away, sends[0])
                else:
                    send(hidden_own, hidden_h.at[here])
        d_norm, mlp_part = centered_norm_back(d_lifted, normed_mlp[here], stat[here, 2:3], norm_gains[8:9])
        d_middle = incoming[here].astype(jnp.float32) + d_norm
        branch = d_middle.astype(jnp.bfloat16)
        d_branch[...] = jnp.concatenate([branch, jnp.zeros((rows, 1), jnp.bfloat16)], axis=1)
        d_heads[...] = against_transposed(branch, out_w[...]).astype(jnp.bfloat16)
        lane = lax.broadcasted_iota(jnp.int32, (rows, PAIR), 1)
        zero = jnp.zeros((rows, PAIR), jnp.bfloat16)
        heads_total = log_total[slot_rows(slot, LSE_ROWS)]
        for pair in range(width // PAIR):
            at = pair * PAIR
            queries = packed[here, at : at + PAIR] * jnp.asarray(SCALE, jnp.bfloat16)
            key_part = packed[here, width + at : width + at + PAIR]
            values = packed[here, 2 * width + at : 2 * width + at + PAIR]
            d_part = d_heads[:, at : at + PAIR]
            sums = None
            for half, keep in enumerate((lane < HD, lane >= HD)):
                own_queries = jnp.where(keep, queries, zero)
                own_keys = jnp.where(keep, key_part, zero)
                own_part = jnp.where(keep, d_part, zero)
                head = 2 * pair + half
                attention = jnp.exp(
                    against_transposed(key_part, own_queries) + bias[here].astype(jnp.float32) - heads_total[head : head + 1, :]
                )
                d_attention = against_transposed(values, own_part)
                d_scores = attention * (d_attention - jnp.sum(attention * d_attention, axis=0, keepdims=True))
                d_scores = d_scores.astype(jnp.bfloat16)
                terms = (
                    rows_product(own_keys, d_scores),
                    product(d_scores, own_queries),
                    product(attention.astype(jnp.bfloat16), own_part),
                )
                sums = terms if sums is None else tuple(a + b for a, b in zip(sums, terms))
            d_packed[:, at : at + PAIR] = (sums[0].T * SCALE).astype(jnp.bfloat16)
            d_packed[:, width + at : width + at + PAIR] = sums[1].astype(jnp.bfloat16)
            d_packed[:, 2 * width + at : 2 * width + at + PAIR] = sums[2].astype(jnp.bfloat16)
        middle, half = 3 * width // 2, width // 2
        mine = side("x")
        packed_own[:, :middle] = d_packed[:, span(mine, middle)]
        packed_own[:, middle:] = d_branch[:, span(mine, half)]
        packed_away[:, :middle] = d_packed[:, span(1 - mine, middle)]
        packed_away[:, middle:] = d_branch[:, span(1 - mine, half)]
        send(packed_away, sends[1])
        send(packed_own, packed_h.at[here])
        d_lifted = jnp.zeros((rows, width), jnp.float32)
        for t in column_tiles(3 * width, width):
            d_lifted = d_lifted + against_transposed(d_packed[:, t], qkv_w[:, t])
        normed, factor, _ = centered_norm(entering[here].astype(jnp.float32))
        d_norm, attn_part = centered_norm_back(d_lifted, normed, factor, norm_gains[0:1])
        leaving[...] = (d_middle + d_norm).astype(jnp.bfloat16)
        d_input[here] = leaving[...]
        if moment == 1:

            @pl.when(section != 0)
            def _():
                pltpu.make_async_copy(d_input, crossing, send_sems.at[4]).start()

        number = lax.broadcasted_iota(jnp.int32, (8, width), 0)
        gains[slot_rows(slot, 8)] = jnp.where(number == 0, attn_part, jnp.where(number == 1, mlp_part, 0.0))
        for copy in copies:
            copy.wait()

    pl.when((slot >= 0) & (slot < MICRO))(work)
    if moment != MICRO:

        @pl.when(section == moment)
        def _():
            pltpu.make_async_copy(d_input, crossing, send_sems.at[4]).wait()

    if summing:

        @pl.when(section != 0 if moment else section == 0)
        def _():
            add_sequences(owners, stat, seq_sums)


def backward_layer(moment, received, weights, bias, stored, stacks, sequences, after=()):
    width, inner = weights[2].shape
    rows = bias.shape[1]
    compressed = width - 1
    low, full = jnp.bfloat16, jnp.float32
    blocks = [
        ((rows, compressed), low),
        ((rows, compressed), low),
        ((8, width), full),
    ]
    out_shape = [pltpu.VMEM((rows, compressed), low)]
    out_shape += [pltpu.VMEM((MICRO * shape[0], shape[1]), kind) for shape, kind in blocks]
    sent = (inner // 2, 2 * width)
    out_shape += [pltpu.HBM((MICRO * rows, wide), low) for wide in sent]
    out_shape += [pltpu.HBM((rows, wide), low) for wide in sent]
    out_specs = [VMEM] * (1 + len(blocks)) + [HBM] * 4
    args = [] if moment == 0 else [in_vmem(received)]
    args += [in_vmem(a) for a in (*weights, bias, *stored)]
    in_specs = [VMEM] * len(args)
    scratch = [pltpu.VMEM((rows, n * width), low) for n in (1, 1, 3)]
    scratch += [pltpu.VMEM((rows, wide), low) for wide in sent for _ in range(2)]
    scratch += [pltpu.SemaphoreType.DMA((5,))]
    given = list(stacks)
    if moment != MICRO:
        out_shape += [pltpu.HBM((MICRO * rows, compressed), low)]
        out_specs += [HBM]
    aliases = {len(args) + i: 1 + i for i in range(min(len(given), 5))}
    if moment == 1:
        aliases[len(args) + 5] = 8
    in_specs += out_specs[1 : 1 + min(len(given), 5)] + [HBM] * (moment == 1)
    args += [in_vmem(s) for s in given[:3]] + [in_hbm(s) for s in given[3:]]
    args += after
    in_specs += [ANY] * len(after)
    if moment != 1:
        owners, seq_sums = sequences
        args += [in_vmem(owners), in_vmem(seq_sums)]
        aliases[len(args) - 1] = len(out_shape)
        in_specs += [VMEM, VMEM]
        out_shape += [pltpu.VMEM(seq_sums.shape, full)]
        out_specs += [VMEM]
    outs = pl.pallas_call(
        functools.partial(backward_kernel, moment=moment, ordered=len(after)),
        out_shape=out_shape,
        in_specs=in_specs,
        out_specs=out_specs,
        input_output_aliases=aliases,
        scratch_shapes=scratch,
        compiler_params=pltpu.CompilerParams(vmem_limit_bytes=KERNEL_VMEM),
        cost_estimate=told(("B0", "B1", "B2")[moment]),
        name="backward_layer",
    )(*args)
    return outs


def exchange(block, axis, section=None):
    size = lax.axis_size("dp")
    if section is None:
        return lax.ppermute(block, "dp", [(i, i ^ STRIDES[axis]) for i in range(size)])
    first = section * size
    return lax.ppermute(block, ("section", "dp"), [(first + i, first + (i ^ STRIDES[axis])) for i in range(size)])


def turned_over(block, axis):
    size = lax.axis_size("dp")
    route = [(k * size + i, (1 - k) * size + (i ^ STRIDES[axis])) for k in (0, 1) for i in range(size)]
    return lax.ppermute(block, ("section", "dp"), route)


def turn(target, column, block):
    rows = block.shape[0]
    for t in column_tiles(block.shape[1], 3 * PAIR):
        target[t, column : column + rows] = block[:, t].T


def parting(names, axis, rows):
    outer = 2 ** names.index(axis)
    inner = rows // (2 * outer)
    mine = side(axis)
    return [
        [pl.ds(pl.multiple_of((2 * number + half) * inner, 16), inner) for number in range(outer)]
        for half in (1 - mine, mine)
    ]


def gather_small(gain_parts, seq_sums, small, away, own):
    chips = small.shape[0]
    small[...] = jnp.zeros_like(small)
    count = gain_parts.shape[1] // chips
    each = -(-seq_sums.shape[0] // chips)
    for kind in (0, 1):
        gain = gain_parts[kind : kind + 1] + gain_parts[8 + kind : 9 + kind]
        for chip in range(chips):
            small[chip : chip + 1, kind * PAIR : kind * PAIR + count] = gain[:, chip * count : (chip + 1) * count]
    for chip in range(chips):
        for number in range(each):
            at = (2 + number) * PAIR
            small[chip : chip + 1, at : at + PAIR] = seq_sums[chip * each + number : chip * each + number + 1]
    mine = side("x")
    for number in range(chips // 2):
        away[number : number + 1] = small[pl.ds(2 * number + 1 - mine, 1)]
        own[number : number + 1] = small[pl.ds(2 * number + mine, 1)]


def gradient_kernel(*refs, kind, names, axis, chained):
    formers, refs = refs[: 4 if kind == "mixed" else 2], refs[4 if kind == "mixed" else 2 :]
    latter, refs = refs[0], refs[1:]
    crossing, refs = refs[: 1 if kind == "down" else 3], refs[1 if kind == "down" else 3 :]
    refs = refs[chained:]
    if kind != "up":
        beside, refs = refs[:2], refs[2:]
    away_stage, own_stage = refs[:2]
    refs = refs[2:]
    if kind == "down":
        smalls, refs = (refs[-1], *refs[:2]), refs[2:-1]
    former_own, former_got, latter_own, latter_got, turned, parts, sems = refs
    tokens, tall = former_own.shape
    rows = tokens // MICRO
    section = lax.axis_index("section")
    copies = []

    def load(source, target):
        copies.append(pltpu.make_async_copy(source, target, sems.at[len(copies)]))
        copies[-1].start()

    if kind == "mixed":
        for number, (source, target) in enumerate(zip(formers, (former_own,) * 2 + (former_got,) * 2)):
            load(source, target.at[slot_rows(number % 2, rows)])
    else:
        load(formers[0], former_own)
        load(formers[1], former_got)
    firsts = len(copies) // 2
    load(latter, latter_own)
    if kind == "down":
        load(crossing[0], latter_got)
    else:
        load(crossing[1], latter_got.at[slot_rows(1 - section, rows)])
        target = latter_got.at[slot_rows(section, rows)]
        for number, source in ((0, crossing[2]), (1, crossing[0])):
            copy = pltpu.make_async_copy(source, target, sems.at[len(copies)])
            pl.when(section == number)(copy.start)
        copies.append(copy)
    if kind == "down":
        gather_small(*beside, *smalls)
    for copy in copies[:firsts]:
        copy.wait()
    turn(turned, 0, former_own)
    for copy in copies[firsts : 2 * firsts]:
        copy.wait()
    turn(turned, tokens, former_got)
    for copy in copies[2 * firsts :]:
        copy.wait()
    height = parts.shape[1]
    for group in range(turned.shape[0] // height // 2):
        for which, spans in enumerate(parting(names, axis, 2 * height)):
            inner = height // len(spans)
            block = turned.at[pl.ds(group * 2 * height, 2 * height)]
            for number, rows_here in enumerate(spans):
                parts[which, number * inner : (number + 1) * inner] = block[rows_here]
        if kind == "mixed":
            edge = 3 * latter_own.shape[1] // 4
            sections = column_tiles(edge, 3 * PAIR) if group == 0 else [slice(edge, latter_own.shape[1])]
        elif kind == "up":
            sections = column_tiles(latter_own.shape[1], 4 * PAIR)
        else:
            sections = [slice(None)]
        for t in sections:
            for which, stage in ((0, away_stage), (1, own_stage)):
                total = product(parts[which, :, :tokens], latter_own[:, t])
                total = total + product(parts[which, :, tokens:], latter_got[:, t])
                stage[:height, t] = total.astype(stage.dtype)
    if kind == "mixed":
        small = beside[0][...] + beside[1][...]
        mine = side(axis)
        for number in range(small.shape[0] // 2):
            for stage, half in ((away_stage, 1 - mine), (own_stage, mine)):
                stride = STRIDES[axis] // 2
                first = number // stride * 2 * stride + number % stride
                row = jnp.where(half == 0, small[first : first + 1], small[first + stride : first + stride + 1])
                at = height + number * SPARE
                stage[at : at + SPARE] = jnp.broadcast_to(row, (SPARE, row.shape[1])).astype(stage.dtype)


def weight_gradient(kind, names, axis, formers, latters, after, beside=()):
    tokens, wide = latters[0].shape
    tall = formers[0].shape[1]
    height = (tall // 2 if kind == "mixed" else tall) // 2
    owned = len(formers) // 2
    args = [*(in_hbm(f) for f in formers[:owned]), *formers[owned:]]
    args += [latters[0] if kind == "down" else in_hbm(latters[0]), *latters[1:]]
    args += after
    in_specs = [ANY] * len(args) + [VMEM] * len(beside)
    args += [in_vmem(b) for b in beside]
    low, full = jnp.bfloat16, jnp.float32
    stacked = height + (SPARE * 4 if kind == "mixed" else 0)
    out_shape = [pltpu.VMEM((stacked, wide), low), pltpu.VMEM((stacked, wide), full)]
    scratch = [
        pltpu.VMEM((tokens, tall), low),
        pltpu.VMEM((tokens, tall), low),
        pltpu.VMEM((tokens, wide), low),
        pltpu.VMEM((tokens, wide), low),
        pltpu.VMEM((tall, 2 * tokens), low),
        pltpu.VMEM((2, height, 2 * tokens), low),
        pltpu.SemaphoreType.DMA((8,)),
    ]
    if kind == "down":
        row = 2 * beside[0].shape[1]
        out_shape += [pltpu.VMEM((CORE_CHIPS // 2, row), full)] * 2
        scratch.append(pltpu.VMEM((CORE_CHIPS, row), full))
    return pl.pallas_call(
        functools.partial(gradient_kernel, kind=kind, names=names, axis=axis, chained=len(after)),
        in_specs=in_specs,
        out_specs=[VMEM] * len(out_shape),
        out_shape=out_shape,
        scratch_shapes=scratch,
        compiler_params=pltpu.CompilerParams(vmem_limit_bytes=24 * MIB),
        cost_estimate=told(kind),
        name=kind + "_gradient",
    )(*args)


def fold_kernel(own, got, *refs, names, axis, spare):
    away_out, own_out = refs[-2:]
    rows = own.shape[0] - spare
    height = rows // 2
    for spans, target in zip(parting(names, axis, rows), (away_out, own_out)):
        inner = height // len(spans)
        for number, place in enumerate(spans):
            total = own[place] + got[place].astype(jnp.float32)
            target[number * inner : (number + 1) * inner] = total.astype(target.dtype)
    if not spare:
        return
    kept = away_out.shape[0] - height
    if not kept:
        place = pl.ds(rows, own_out.shape[0] - height)
        own_out[height:] = own[place] + got[place].astype(jnp.float32)
        return
    mine = side(axis)
    for half, target in ((1 - mine, away_out), (mine, own_out)):
        for number in range(kept // SPARE):
            place = pl.ds(pl.multiple_of(rows + (2 * number + half) * SPARE, SPARE), SPARE)
            total = own[place] + got[place].astype(jnp.float32)
            target[height + number * SPARE : height + (number + 1) * SPARE] = total.astype(target.dtype)


def fold(name, parted, axis, names, following, after, spare=0, kept=0):
    away, own = parted
    got = exchange(away, axis)
    rows, wide = own.shape
    height = (rows - spare) // 2
    own_height = height + (kept or min(spare, 8))
    return pl.pallas_call(
        functools.partial(fold_kernel, names=names, axis=following, spare=spare),
        in_specs=[VMEM, VMEM] + [ANY] * len(after),
        out_specs=[VMEM, VMEM],
        out_shape=[pltpu.VMEM((height + kept, wide), jnp.bfloat16), pltpu.VMEM((own_height, wide), jnp.float32)],
        compiler_params=pltpu.CompilerParams(vmem_limit_bytes=8 * MIB),
        cost_estimate=told(name),
        name="fold",
    )(in_vmem(own), in_vmem(got), *after)


def total_kernel(own, got, total):
    total[...] = own[...] + got[...].astype(jnp.float32)


def sides_kernel(own, got, *outs, axis):
    mine = side(axis)
    rows = got.shape[0]
    for source, half in ((own, mine), (got, 1 - mine)):
        done = 0
        for out in outs[:2]:
            wide = out.shape[1] // 2 if out.shape[1] % 2 == 0 else (out.shape[1] + 1) // 2
            block = source[:rows, done : done + wide].astype(jnp.float32)
            if out.shape[1] % 2 == 0:
                out[:, pl.ds(pl.multiple_of(half * wide, PAIR), wide)] = block
            else:

                @pl.when(half == 0)
                def _():
                    out[:, :wide] = block

                @pl.when(half != 0)
                def _():
                    out[:, wide:] = block[:, : wide - 1]

            done += wide


def last_kernel(own, got, *outs, axis):
    sides_kernel(own, got, *outs[:2], axis=axis)
    if len(outs) > 2:
        attn, mlp, seq = outs[2:]
        count = attn.shape[1]
        row = own[got.shape[0] : got.shape[0] + 1]
        attn[...] = row[:, :count]
        mlp[...] = row[:, PAIR : PAIR + count]
        for number in range(seq.shape[0]):
            at = (2 + number) * PAIR
            seq[number : number + 1] = row[:, at : at + seq.shape[1]]


def finish(name, parted, axis, shapes):
    away, own = parted
    return pl.pallas_call(
        functools.partial(last_kernel, axis=axis),
        in_specs=[VMEM, VMEM],
        out_specs=[VMEM] * len(shapes),
        out_shape=[shaped(shape, jnp.float32) for shape in shapes],
        compiler_params=pltpu.CompilerParams(vmem_limit_bytes=8 * MIB),
        cost_estimate=told(name),
        name="finish",
    )(in_vmem(own), in_vmem(exchange(away, axis)))


def scattered(down, up, make_mixed, seq_count):
    parts = {"d": down, "u": up}
    orders = {"d": ORDERS["down"], "u": ORDERS["up"] + "y", "m": ORDERS["mixed"] + "x"}
    names = {"d": "vyx", "u": "vwyx", "m": "vwyx"}
    spares = {"1": (4 * SPARE, 2 * SPARE), "2": (2 * SPARE, SPARE), "3": (SPARE, 0)}
    results = {}
    before = None
    for step in STEPS:
        kind, phase = step
        order = orders[kind]
        axis = order[int(phase) - 1]
        names[kind] = names[kind].replace(axis, "")
        if step == "m1":
            parts["m"] = make_mixed((before,) if MIXED_LAST and before is not None else (up[1],))
        away, own = parts[kind]
        rows, wide = own.shape
        if int(phase) < len(order):
            spare = spares[phase] if kind == "m" else (0, 0)
            after = (before,) if CHAINED and before is not None else ()
            parts[kind] = fold(step, parts[kind], axis, names[kind], order[int(phase)], after, *spare)
            before = parts[kind][1]
        elif kind == "d":
            results[kind] = [
                pl.pallas_call(
                    total_kernel,
                    in_specs=[VMEM, VMEM],
                    out_specs=VMEM,
                    out_shape=shaped(own.shape, jnp.float32),
                    compiler_params=pltpu.CompilerParams(vmem_limit_bytes=8 * MIB),
                    cost_estimate=told(step),
                    name="total",
                )(in_vmem(own), in_vmem(exchange(away, axis)))
            ]
        else:
            rows, width = away.shape[0], wide // 2
            shapes = [(rows, 2 * wide)]
            if kind == "m":
                shapes = [(rows, 3 * width), (rows, width - 1), (1, rows), (1, rows), (seq_count, 2)]
            results[kind] = finish(step, parts[kind], axis, shapes)
    return (*results["d"], *results["u"], *results["m"])


def shards(
    stream_in,
    cotangent,
    qkv_weight,
    out_weight,
    up_weight,
    down_weight,
    attn_gain,
    mlp_gain,
    seq_lengths,
    seq_slot,
):
    section = lax.axis_index("section")
    chips = lax.axis_size("dp")
    compressed = stream_in.shape[1]
    weights = (qkv_weight[0], out_weight[0], up_weight[0], down_weight[0])
    inputs = (seq_lengths, seq_slot, attn_gain, mlp_gain, stream_in, cotangent)

    split = chips == CORE_CHIPS
    swapped = {}

    def swap(name, block, axis, section=None):
        if split:
            swapped[name] = exchange(block, axis, section)

    def early(name):
        return tuple(swapped[n] for n in EARLY.get(name, ())) if split else ()

    received = stored = bias = None
    mixed = []
    for moment in range(MICRO + 1):
        leaving, outs = forward_layer(moment, inputs, received, weights, bias, stored)
        if moment == 0:
            weights = outs[11:16]
            bias, bias_turned, seq_sums, owners, incoming = outs[16:]
        stored = outs[:11]
        if moment == 1:
            mixed.append(outs[10])
            swap("x0", mixed[0], "x")
            stored = outs[:10] + outs[11:12]
        if moment < MICRO:
            received = shifted(leaving, "section", 1)
    entering, stream_out, packed, log_total, normed_mlp, slope, stat, lifted_mlp, active_own, active_away = stored[:10]
    mixed.append(stored[10])
    swap("x1", mixed[1], "x")
    swap("y", lifted_mlp, "y")
    swap("w", active_away, "w")

    kept = (entering, packed, log_total, normed_mlp, stat, slope)
    received = None
    given = [incoming]
    pieces = []
    for moment in range(MICRO + 1):
        leaving, *outs = backward_layer(
            moment, received, weights, bias_turned, kept, given, (owners, seq_sums), early("B%d" % moment)
        )
        if moment != 1:
            seq_sums = outs[-1]
        given = outs[:5] + ([outs[7]] if moment == 0 else [])
        pieces.append(outs[5:7])
        if moment < MICRO:
            received = shifted(leaving, "section", -1)
        only = (1, None, 0)[moment]
        swap("h%d" % moment, pieces[moment][0], "y", only)
        swap("p%d" % moment, pieces[moment][1], "x", only)
        if split and moment == 1:
            swapped["e"] = turned_over(outs[7], "w")
    incoming, stream_grad, gain_parts, hidden_own, packed_own = outs[:5]

    if split:
        down = weight_gradient(
            "down",
            "vyx",
            ORDERS["down"][0],
            (active_own, swapped["w"]),
            (incoming, swapped["e"]),
            early("down"),
            (gain_parts, seq_sums),
        )
        small = (down[3], exchange(down[2], "x"))
        up = weight_gradient(
            "up",
            "vwyx",
            ORDERS["up"][0],
            (lifted_mlp, swapped["y"]),
            (hidden_own, *(swapped[n] for n in ("h0", "h1", "h2"))),
            (down[1], *early("up")),
        )

        def make_mixed(after):
            formers = (*mixed, swapped["x0"], swapped["x1"])
            latters = (packed_own, *(swapped[n] for n in ("p0", "p1", "p2")))
            return weight_gradient("mixed", "vwyx", ORDERS["mixed"][0], formers, latters, after, small)

        down_part, up_part, qkv_part, out_part, attn_part, mlp_part, seq_part = scattered(
            down[:2], up, make_mixed, seq_lengths.shape[0] // chips
        )
    else:
        lifted_mixed = jnp.concatenate(mixed, axis=0)
        gains = jnp.sum(gain_parts.reshape(MICRO, 8, -1)[:, :2], axis=0)
        seq_terms = seq_sums[: seq_lengths.shape[0], :2]
        small = jnp.concatenate(
            [gains[0].reshape(chips, -1), gains[1].reshape(chips, -1), seq_terms.reshape(chips, -1)], axis=1
        )
        small = lax.psum_scatter(small, "dp", scatter_dimension=0, tiled=True)
        count = gains.shape[1] // chips
        attn_part, mlp_part = small[:, :count], small[:, count : 2 * count]
        seq_part = small[:, 2 * count :].reshape(-1, 2)
        width = compressed + 1
        joined = []
        for number, own in ((0, hidden_own), (1, packed_own)):
            other = [jnp.where(section == 0, pieces[2 - k][number], pieces[1 - k][number]) for k in (0, 1)]
            joined.append((own, jnp.concatenate(other, axis=0)))
        edge = 3 * width // 2
        d_hidden = jnp.concatenate(joined[0], axis=1)
        d_packed = jnp.concatenate([part[:, :edge] for part in joined[1]], axis=1)
        d_branch = jnp.concatenate([part[:, edge:] for part in joined[1]], axis=1)[:, :compressed]
        active = jnp.concatenate(
            [part[:, t] for t in column_tiles(active_own.shape[1], width) for part in (active_own, active_away)],
            axis=1,
        )
        pairs = (
            (active, incoming),
            (lifted_mlp, d_hidden),
            (lifted_mixed[:, width:], d_branch),
            (lifted_mixed[:, :width], d_packed),
        )
        down_part, up_part, out_part, qkv_part = (
            lax.psum_scatter(rows_product(a, b), "dp", scatter_dimension=0, tiled=True) for a, b in pairs
        )
    return (
        stream_out[None],
        stream_grad[None],
        qkv_part[None],
        out_part[None],
        up_part[None],
        down_part[None],
        attn_part,
        mlp_part,
        seq_part[None],
    )


def solution(mesh):
    placed = (
        P("dp", None),
        P("dp", None),
        P("section", None, None),
        P("section", None, None),
        P("section", None, None),
        P("section", None, None),
        P("section", None),
        P("section", None),
        P(),
        P(),
    )
    return jax.shard_map(
        shards,
        mesh=mesh,
        in_specs=placed,
        out_specs=(
            P("section", "dp", None),
            P("section", "dp", None),
            P("section", "dp", None),
            P("section", "dp", None),
            P("section", "dp", None),
            P("section", "dp", None),
            P("section", "dp"),
            P("section", "dp"),
            P("section", "dp", None),
        ),
        check_vma=False,
    )
```
